32 devices in a mesh: dp: 4 (over y, core), seq: 8 (over z, x).
Axes of the slice: x: 2, y: 2, z: 4, core: 2. Of those that a mesh axis runs over, the one named last changes fastest.
Arguments:
- tok_ids: int32 [4, 2048], P('dp'), may hold values from 0 to 31999, as said below
- targets: int32 [4, 512], P('dp'), may hold values from 0 to 31999
- positions: int32 [4, 512], P('dp'), may hold values from 0 to 2047, as said below
- answer_mask: int32 [4, 512], replicated, may hold values from 0 to 1, as said below
- emb: float32 [32000, 2048], P('dp', 'seq'), may hold values from -6 to 6
- head: float32 [32000, 2048], P('seq', 'dp'), may hold values from -0.5745243 to 0.5745243
- attn_w: float32 [2048, 4608], P(('dp', 'seq')), may hold values from -1.06066017 to 1.06066017
- mlp_w: float32 [2048, 16896], P(('dp', 'seq')), may hold values from -0.13258252 to 0.13258252
- gains: float32 [3, 2048], P(None, ('dp', 'seq')), may hold values from 0.48 to 2.16
- emb_row: float32 [32000], P('dp'), may hold values from 7.45284975e-11 to 9.9868187e-09
- emb_col: float32 [2048], P('seq'), may hold values from 4.47171e-10 to 3.8754819e-09
- head_row: float32 [32000], P('seq'), may hold values from 1.5258789e-09 to 2.0446777e-07
- head_col: float32 [2048], P('dp'), may hold values from 9.15527344e-09 to 7.93457e-08
- attn_row: float32 [2048], P(('dp', 'seq')), may hold values from 6.2421453e-06 to 5.4098593e-05
- attn_col: float32 [4608], replicated, may hold values from 6.2421453e-06 to 5.4098593e-05
- mlp_row: float32 [2048], P(('dp', 'seq')), may hold values from 5.78706915e-08 to 5.0154599e-07
- mlp_col: float32 [16896], replicated, may hold values from 5.78706915e-08 to 5.0154599e-07
- gains_moment: float32 [3, 2048], P(None, ('dp', 'seq')), may hold values from 1.31607056e-07 to 7.8037691e-05
Outputs:
- loss_sum: float32 [], replicated
- valid_count: float32 [], replicated
- emb_grad: float32 [32000, 2048], P('dp', 'seq')
- emb_new: float32 [32000, 2048], P('dp', 'seq')
- emb_row_new: float32 [32000], P('dp')
- emb_col_new: float32 [2048], P('seq')
- head_grad: float32 [32000, 2048], P('seq', 'dp')
- head_new: float32 [32000, 2048], P('seq', 'dp')
- head_row_new: float32 [32000], P('seq')
- head_col_new: float32 [2048], P('dp')
- attn_grad: float32 [2048, 4608], P(('dp', 'seq'))
- attn_new: float32 [2048, 4608], P(('dp', 'seq'))
- attn_row_new: float32 [2048], P(('dp', 'seq'))
- attn_col_new: float32 [4608], replicated
- mlp_grad: float32 [2048, 16896], P(('dp', 'seq'))
- mlp_new: float32 [2048, 16896], P(('dp', 'seq'))
- mlp_row_new: float32 [2048], P(('dp', 'seq'))
- mlp_col_new: float32 [16896], replicated
- gains_grad: float32 [3, 2048], P(None, ('dp', 'seq'))
- gains_moment_new: float32 [3, 2048], P(None, ('dp', 'seq'))
- gains_new: float32 [3, 2048], P(None, ('dp', 'seq'))
The draws below stay inside these ranges and needn't reach their ends.
Inputs may be any that keep to these rules, and one draw needn't show every extreme that they name: `positions`: distinct and increasing within a row; the first is 0 and the last 2047. `answer_mask`: every row has a 1 in its first place. `tok_ids`: at each answer position the token equals the target there.
All inputs are finite; a program needn't handle non-finite values.
Results may differ from the reference program's by a relative error of at most 0.025.
The reference program's roundings to bfloat16 on the way count: a program that leaves them out, or rounds other values in their place, can miss the bound.
Values may be sent and summed in bfloat16 or wider, within the bound.
A program may use at most 640 MiB of HBM per device.

```python
import math
import jax
import jax.numpy as jnp
from jax import lax

D = 2048
HEADS = 32
KVH = 4
HD = 64
FF = 5632
VOCAB = 32000
PICKS = 512
SEQLEN = 2048
NSEQS = 4
QKV = 2560


def answer_draws(key):
    key = jax.random.fold_in(key, 101)
    place_key, target_key = jax.random.split(key)
    keys = jax.random.split(place_key, NSEQS)

    def one_row(row_key):
        inner = jax.random.permutation(row_key, SEQLEN - 2)[:PICKS - 2] + 1
        return jnp.concatenate([jnp.zeros((1,), jnp.int32), jnp.sort(inner).astype(jnp.int32), jnp.full((1,), SEQLEN - 1, jnp.int32)])
    places = jax.vmap(one_row)(keys).astype(jnp.int32)
    wanted = jax.random.randint(target_key, (NSEQS, PICKS), 0, VOCAB).astype(jnp.int32)
    return (places, wanted)


def shared_table(key):
    key = jax.random.fold_in(key, 103)
    return jax.random.truncated_normal(key, -6.0, 6.0, (VOCAB, D), jnp.float32)


def spread_factor():
    return min(584.0, 19300.0 * SEQLEN ** (-0.74))


def level_stat(key, shape, mean, top):
    count = shape[-1]
    jitter = jax.random.uniform(key, shape, jnp.float32, math.log(0.5), math.log(2.0))
    rise = jnp.power(top, jnp.arange(count, dtype=jnp.float32) / count)
    profile = (top - 1.0) / math.log(top) if top > 1.0 else 1.0
    return jnp.exp(jitter) * rise * (mean / (1.082 * profile))


def emb_level():
    return (2.87 * spread_factor() + 3.7) / (NSEQS * PICKS * VOCAB * D)


def head_level():
    return 2.0 / (NSEQS * PICKS * VOCAB)


def attn_level():
    return 2.87 * spread_factor() / (NSEQS * PICKS * (QKV + D))


def mlp_level():
    return (0.96 / FF + 0.46 / D) / (NSEQS * PICKS)


def draw_positions(key, part):
    places, wanted = answer_draws(key)
    return places


def draw_targets(key, part):
    places, wanted = answer_draws(key)
    return wanted


def draw_tok_ids(key, part):
    places, wanted = answer_draws(key)
    key = jax.random.fold_in(key, 17)
    filler = jax.random.randint(key, (NSEQS, SEQLEN), 0, VOCAB).astype(jnp.int32)
    rows = jnp.arange(NSEQS, dtype=jnp.int32)[:, None]
    return filler.at[rows, places].set(wanted).astype(jnp.int32)


def draw_answer_mask(key, part):
    key = jax.random.fold_in(key, 12)
    rolls = jax.random.randint(key, (NSEQS, PICKS), 0, 100)
    levels = 25 + 50 * jnp.arange(NSEQS, dtype=jnp.int32) // max(NSEQS - 1, 1)
    marked = (rolls < levels[:, None]).astype(jnp.int32)
    return marked.at[:, 0].set(1)


def draw_emb(key, part):
    return shared_table(key)


def draw_head(key, part):
    common = shared_table(key)
    key = jax.random.fold_in(key, 13)
    own = jax.random.truncated_normal(key, -6.0, 6.0, (VOCAB, D), jnp.float32)
    rising = 1.0 + 2.0 * jnp.arange(VOCAB, dtype=jnp.float32) / VOCAB
    return (own + 3.0 * D ** (-0.5) * common) * rising[:, None] * D ** (-0.5)


def draw_attn_w(key, part):
    key = jax.random.fold_in(key, 14)
    base = jax.random.truncated_normal(key, -6.0, 6.0, (D, QKV + D), jnp.float32)
    columns = jnp.arange(QKV + D)
    scale = jnp.where(columns < QKV, 1.0, 8.0) * D ** (-0.5)
    return base * scale[None, :]


def draw_mlp_w(key, part):
    key = jax.random.fold_in(key, 15)
    base = jax.random.truncated_normal(key, -6.0, 6.0, (D, 3 * FF), jnp.float32)
    columns = jnp.arange(3 * FF)
    scale = jnp.where(columns < 2 * FF, D ** (-0.5), FF ** (-0.5))
    return base * scale[None, :]


def draw_gains(key, part):
    key = jax.random.fold_in(key, 16)
    jitter = jax.random.uniform(key, (3, D), jnp.float32, 0.8, 1.2)
    rising = 0.6 + 1.2 * jnp.arange(D, dtype=jnp.float32) / D
    return jitter * rising[None, :]


def draw_emb_row(key, part):
    key = jax.random.fold_in(key, 21)
    return level_stat(key, (VOCAB,), emb_level(), 16.0)


def draw_emb_col(key, part):
    key = jax.random.fold_in(key, 22)
    return level_stat(key, (D,), emb_level(), 1.0)


def draw_head_row(key, part):
    key = jax.random.fold_in(key, 23)
    return level_stat(key, (VOCAB,), head_level(), 16.0)


def draw_head_col(key, part):
    key = jax.random.fold_in(key, 24)
    return level_stat(key, (D,), head_level(), 1.0)


def draw_attn_row(key, part):
    key = jax.random.fold_in(key, 25)
    return level_stat(key, (D,), attn_level(), 1.0)


def draw_attn_col(key, part):
    key = jax.random.fold_in(key, 28)
    return level_stat(key, (QKV + D,), attn_level(), 1.0)


def draw_mlp_row(key, part):
    key = jax.random.fold_in(key, 26)
    return level_stat(key, (D,), mlp_level(), 1.0)


def draw_mlp_col(key, part):
    key = jax.random.fold_in(key, 29)
    return level_stat(key, (3 * FF,), mlp_level(), 1.0)


def draw_gains_moment(key, part):
    key = jax.random.fold_in(key, 27)
    levels = jnp.array([[1.84 * spread_factor()], [1.84], [5.9]], jnp.float32) / (NSEQS * PICKS * D)
    return level_stat(key, (3, D), levels, 1.0)


def setup_inputs(seed: int = 0) -> dict:
    arg_keys = jax.random.split(jax.random.key(seed), 19)
    tok_ids = draw_tok_ids(jax.random.fold_in(arg_keys[18], 71), 0)
    targets = draw_targets(jax.random.fold_in(arg_keys[18], 71), 0)
    positions = draw_positions(jax.random.fold_in(arg_keys[18], 71), 0)
    answer_mask = draw_answer_mask(jax.random.fold_in(arg_keys[18], 71), 0)
    emb = draw_emb(jax.random.fold_in(arg_keys[18], 71), 0)
    head = draw_head(jax.random.fold_in(arg_keys[18], 71), 0)
    attn_w = draw_attn_w(jax.random.fold_in(arg_keys[18], 71), 0)
    mlp_w = draw_mlp_w(jax.random.fold_in(arg_keys[18], 71), 0)
    gains = draw_gains(jax.random.fold_in(arg_keys[18], 71), 0)
    emb_row = draw_emb_row(jax.random.fold_in(arg_keys[18], 71), 0)
    emb_col = draw_emb_col(jax.random.fold_in(arg_keys[18], 71), 0)
    head_row = draw_head_row(jax.random.fold_in(arg_keys[18], 71), 0)
    head_col = draw_head_col(jax.random.fold_in(arg_keys[18], 71), 0)
    attn_row = draw_attn_row(jax.random.fold_in(arg_keys[18], 71), 0)
    attn_col = draw_attn_col(jax.random.fold_in(arg_keys[18], 71), 0)
    mlp_row = draw_mlp_row(jax.random.fold_in(arg_keys[18], 71), 0)
    mlp_col = draw_mlp_col(jax.random.fold_in(arg_keys[18], 71), 0)
    gains_moment = draw_gains_moment(jax.random.fold_in(arg_keys[18], 71), 0)
    return dict(tok_ids=tok_ids, targets=targets, positions=positions, answer_mask=answer_mask, emb=emb, head=head, attn_w=attn_w, mlp_w=mlp_w, gains=gains, emb_row=emb_row, emb_col=emb_col, head_row=head_row, head_col=head_col, attn_row=attn_row, attn_col=attn_col, mlp_row=mlp_row, mlp_col=mlp_col, gains_moment=gains_moment)


eps_norm = 1e-05
eps_square = 1e-30
decay_rate = 0.5
learn_rate = 1.0
zloss_weight = 0.0001
orig_context = 2048.0
yarn_factor = 4.0
highest = lax.Precision.HIGHEST

@jax.custom_vjp
def low(v):
    return lax.optimization_barrier(v.astype(jnp.bfloat16)).astype(jnp.float32)

@jax.custom_vjp
def low_back(v):
    return v

def low_keep(v):
    return (low(v), None)

def low_pass(kept, grad):
    return (grad,)

def back_keep(v):
    return (v, None)

def back_low(kept, grad):
    return (low(grad),)
low.defvjp(low_keep, low_pass)
low_back.defvjp(back_keep, back_low)

def yarn_tables(places):
    halves = jnp.arange(HD // 2, dtype=jnp.float32)
    inverse = jnp.power(10000.0, -2.0 * halves / HD)
    ratio = orig_context * inverse / (2.0 * math.pi)
    ramp_part = jnp.clip((ratio - 1.0) / 31.0, 0.0, 1.0)
    frequency = inverse / yarn_factor * (1.0 - ramp_part) + inverse * ramp_part
    angles = places[:, None] * frequency[None, :]
    magnitude = 0.1 * math.log(yarn_factor) + 1.0
    return (jnp.cos(angles) * magnitude, jnp.sin(angles) * magnitude)

def rotate(values, cosine, sine):
    first = values[..., :HD // 2]
    second = values[..., HD // 2:]
    cosine_row = cosine[:, None, :]
    sine_row = sine[:, None, :]
    return jnp.concatenate([first * cosine_row - second * sine_row, second * cosine_row + first * sine_row], -1)

def rms_norm(values, gain_row):
    return values * lax.rsqrt(lax.optimization_barrier(jnp.mean(values * values, -1, keepdims=True)) + eps_norm) * gain_row

def matmul(left, right):
    return jnp.dot(left, right, precision=highest)

def attend_sequence(queries, keys, values):
    length = queries.shape[0]
    block = math.gcd(length, 512)
    group = HEADS // KVH
    grouped = queries.reshape(length // block, block, KVH, group, HD)
    starts = jnp.arange(length // block, dtype=jnp.int32) * block

    def one_block(pair):
        query_block, start = pair
        scores = jnp.einsum('qgho,kgo->ghqk', query_block, keys, precision=highest) * HD ** (-0.5)
        scores = low_back(scores)
        query_pos = start + jnp.arange(block, dtype=jnp.int32)
        key_pos = jnp.arange(length, dtype=jnp.int32)
        allowed = key_pos[None, :] <= query_pos[:, None]
        scores = jnp.where(allowed, scores, -1e+30)
        weights = low(jax.nn.softmax(scores, -1))
        output = jnp.einsum('ghqk,kgo->qgho', weights, values, precision=highest)
        return output.reshape(block, HEADS * HD)
    return lax.map(jax.checkpoint(one_block), (grouped, starts)).reshape(length, HEADS * HD)

def sequence_total(tables, token_row, target_row, place_row, mask_row):
    emb_low, head_low, attn_low, mlp_low, gain_low = tables
    length = token_row.shape[0]
    kv_width = KVH * HD
    start_x = jnp.take(emb_low, token_row, axis=0)
    normed = low(rms_norm(start_x, gain_low[0]))
    projected = low_back(matmul(normed, attn_low[:, :QKV]))
    cosine, sine = yarn_tables(jnp.arange(length, dtype=jnp.float32))
    queries = low(rotate(projected[:, :D].reshape(length, HEADS, HD), cosine, sine))
    keys = low(rotate(projected[:, D:D + kv_width].reshape(length, KVH, HD), cosine, sine))
    values = low(projected[:, D + kv_width:].reshape(length, KVH, HD))
    attended = low_back(low(attend_sequence(queries, keys, values)))
    middle = start_x + low_back(matmul(attended, attn_low[:, QKV:].T))
    normed_two = low(rms_norm(middle, gain_low[1]))
    gate_up = low_back(matmul(normed_two, mlp_low[:, :2 * FF]))
    mixed = low(jax.nn.silu(gate_up[:, :FF]) * gate_up[:, FF:])
    ending = middle + low_back(matmul(mixed, mlp_low[:, 2 * FF:].T))
    chosen = low(rms_norm(jnp.take(ending, place_row, axis=0), gain_low[2]))
    logits = low_back(matmul(chosen, head_low.T))
    log_total = jax.nn.logsumexp(logits, -1)
    target_logit = jnp.take_along_axis(logits, target_row[:, None], 1)[:, 0]
    return jnp.sum(mask_row * (log_total - target_logit + zloss_weight * log_total * log_total))

def factored(weight, grad, row_stat, col_stat):
    square = grad * grad + eps_square
    row_new = decay_rate * row_stat + (1.0 - decay_rate) * lax.optimization_barrier(jnp.mean(square, 1))
    col_new = decay_rate * col_stat + (1.0 - decay_rate) * lax.optimization_barrier(jnp.mean(square, 0))
    second = row_new[:, None] * col_new[None, :] / jnp.mean(row_new)
    update = grad * lax.rsqrt(second)
    scale = jnp.maximum(0.001, jnp.sqrt(jnp.mean(weight * weight)))
    return (weight - learn_rate * scale * update, row_new, col_new)

def reference(tok_ids, targets, positions, answer_mask, emb, head, attn_w, mlp_w, gains, emb_row, emb_col, head_row, head_col, attn_row, attn_col, mlp_row, mlp_col, gains_moment):
    mask_float = answer_mask.astype(jnp.float32)
    count = jnp.sum(mask_float)

    def objective(emb_in, head_in, attn_in, mlp_in, gains_in):
        tables = (low(emb_in), low(head_in), low(attn_in), low(mlp_in), low(gains_in))
        total = jnp.zeros((), jnp.float32)
        for seq_index in range(NSEQS):
            total = total + sequence_total(tables, tok_ids[seq_index], targets[seq_index], positions[seq_index], mask_float[seq_index])
        return total
    total, pull = jax.vjp(objective, emb, head, attn_w, mlp_w, gains)
    emb_grad, head_grad, attn_grad, mlp_grad, gains_grad = pull(jnp.ones((), jnp.float32) / count)
    emb_new, emb_row_new, emb_col_new = factored(emb, emb_grad, emb_row, emb_col)
    head_new, head_row_new, head_col_new = factored(head, head_grad, head_row, head_col)
    attn_new, attn_row_new, attn_col_new = factored(attn_w, attn_grad, attn_row, attn_col)
    mlp_new, mlp_row_new, mlp_col_new = factored(mlp_w, mlp_grad, mlp_row, mlp_col)
    moment_new = decay_rate * gains_moment + (1.0 - decay_rate) * (gains_grad * gains_grad + eps_square)
    update = gains_grad * lax.rsqrt(moment_new)
    gains_new = gains - learn_rate * jnp.maximum(0.001, jnp.sqrt(jnp.mean(gains * gains))) * update
    return (total, count, emb_grad, emb_new, emb_row_new, emb_col_new, head_grad, head_new, head_row_new, head_col_new, attn_grad, attn_new, attn_row_new, attn_col_new, mlp_grad, mlp_new, mlp_row_new, mlp_col_new, gains_grad, moment_new, gains_new)
```

```python
import math

import jax
import jax.numpy as jnp
from jax import lax
from jax.sharding import PartitionSpec as P

D = 2048
HEADS = 32
KVH = 4
HD = 64
FF = 5632
VOCAB = 32000
QKV = 2560


eps_norm = 1e-05
eps_square = 1e-30
decay_rate = 0.5
learn_rate = 1.0
zloss_weight = 0.0001
orig_context = 2048.0
yarn_factor = 4.0
highest = lax.Precision.HIGHEST


def yarn_tables(places):
    halves = jnp.arange(HD // 2, dtype=jnp.float32)
    inverse = jnp.power(10000.0, -2.0 * halves / HD)
    ratio = orig_context * inverse / (2.0 * math.pi)
    ramp_part = jnp.clip((ratio - 1.0) / 31.0, 0.0, 1.0)
    frequency = inverse / yarn_factor * (1.0 - ramp_part) + inverse * ramp_part
    angles = places[:, None] * frequency[None, :]
    magnitude = 0.1 * math.log(yarn_factor) + 1.0
    return (jnp.cos(angles) * magnitude, jnp.sin(angles) * magnitude)


def rotate(values, cosine, sine):
    first = values[..., : HD // 2]
    second = values[..., HD // 2 :]
    cosine_row = cosine[:, None, :]
    sine_row = sine[:, None, :]
    return jnp.concatenate(
        [first * cosine_row - second * sine_row, second * cosine_row + first * sine_row], -1
    )


def unrotate(values, cosine, sine):
    first = values[..., : HD // 2]
    second = values[..., HD // 2 :]
    cosine_row = cosine[:, None, :]
    sine_row = sine[:, None, :]
    return jnp.concatenate(
        [first * cosine_row + second * sine_row, second * cosine_row - first * sine_row], -1
    )


def rms_norm(values, gain_row):
    return values * lax.rsqrt(jnp.mean(values * values, -1, keepdims=True) + eps_norm) * gain_row


def norm_back(values, gain_row, upstream):
    factor = lax.rsqrt(jnp.mean(values * values, -1, keepdims=True) + eps_norm)
    normed = values * factor
    gain_grad = jnp.sum(upstream * normed, 0)
    inner = upstream * gain_row
    return (factor * (inner - normed * jnp.mean(inner * normed, -1, keepdims=True)), gain_grad)


def matmul(left, right):
    return jnp.dot(left, right, preferred_element_type=jnp.float32)


def matmul_nt(left, right):
    return lax.dot_general(
        left, right, (((1,), (1,)), ((), ())), preferred_element_type=jnp.float32
    )


def matmul_tn(left, right):
    return lax.dot_general(
        left, right, (((0,), (0,)), ((), ())), preferred_element_type=jnp.float32
    )


def finish(weight, update, weight_square, entries):
    return weight - learn_rate * jnp.maximum(0.001, jnp.sqrt(weight_square / entries)) * update


low = jnp.bfloat16
full = jnp.float32


class Place:
    def __init__(self):
        self.seqs = lax.axis_size("seq")
        self.dps = lax.axis_size("dp")
        self.dp = lax.axis_index("dp")
        self.s = lax.axis_index("seq")
        self.his = self.seqs // 2
        self.y, self.c = self.dp // 2, self.dp % 2
        self.hi, self.lo = self.s // 2, self.s % 2
        self.t = self.dp * 2 + self.lo

    def send(self, value, dy=0, dc=0, dlo=0, up=0):
        pairs = []
        for d in range(self.dps):
            for s in range(self.seqs):
                to_d = d ^ (2 * dy + dc)
                to_s = ((s // 2 + up) % self.his) * 2 + ((s % 2) ^ dlo)
                pairs.append((d * self.seqs + s, to_d * self.seqs + to_s))
        return lax.ppermute(value, ("dp", "seq"), pairs)


def pick(array, index, axis):
    return lax.dynamic_index_in_dim(array, index, axis, keepdims=False)


def put(array, block, index, axis):
    return lax.dynamic_update_slice_in_dim(array, jnp.expand_dims(block, axis), index, axis)


def plane_parts(k):
    return dict(dy=(k >> 2) & 1, dc=(k >> 1) & 1, dlo=k & 1)


def plane_swap(pl, blocks):
    out = put(jnp.zeros_like(blocks), pick(blocks, pl.t, 0), pl.t, 0)
    for k in range(1, 8):
        out = put(out, pl.send(pick(blocks, pl.t ^ k, 0), **plane_parts(k)), pl.t ^ k, 0)
    return out


def plane_gather(pl, rows):
    first = [rows] + [pl.send(rows, dy=j >> 1, dlo=j & 1) for j in (1, 2, 3)]
    first = jnp.stack(first)
    return jnp.stack([first, pl.send(first, dc=1)]).reshape(8 * rows.shape[0], rows.shape[1])


def plane_scatter(pl, part):
    part = part.reshape(2, 4, part.shape[0] // 8, part.shape[1])
    both = part[0] + pl.send(part[1].astype(low), dc=1).astype(full)
    total = both[0]
    for j in (1, 2, 3):
        total = total + pl.send(both[j].astype(low), dy=j >> 1, dlo=j & 1).astype(full)
    return total


def ring_sum(pl, part, axis):
    n = pl.his
    acc = pick(part, (pl.hi + n - 1) % n, axis).astype(low)
    for j in range(1, n):
        got = pl.send(acc, up=1).astype(full)
        acc = got + pick(part, (pl.hi + 2 * n - 1 - j) % n, axis).astype(full)
        if j < n - 1:
            acc = acc.astype(low)
    return acc


def halve(pl, part, mine, axis, **way):
    got = pl.send(pick(part, 1 - mine, axis).astype(low), **way)
    return pick(part, mine, axis).astype(full) + got.astype(full)


def layer_scatter(pl, part):
    part = part.astype(low)
    columns = part.shape[-1]
    cut = columns // 256 * 128
    first, second = part[..., :cut], part[..., cut:]
    first = halve(pl, halve(pl, first, pl.y, 0, dy=1), pl.lo, 1, dlo=1)
    second = halve(pl, halve(pl, second, pl.lo, 2, dlo=1), pl.y, 0, dy=1)
    return jnp.concatenate([ring_sum(pl, first, 0), ring_sum(pl, second, 0)], -1)


def seq_sum(value):
    n = lax.axis_size("seq")
    got = lax.all_to_all(value.astype(low), "seq", split_axis=0, concat_axis=0, tiled=True)
    return jnp.sum(got.reshape(n, value.shape[0] // n, value.shape[1]).astype(full), 0)


def attend(queries, keys, values, places):
    allowed = jnp.arange(keys.shape[0], dtype=jnp.int32)[None, :] <= places[:, None]
    scores = jnp.einsum(
        "qgho,kgo->ghqk", queries, keys, preferred_element_type=full
    ) * HD ** (-0.5)
    scores = jnp.where(allowed, scores, -1e30)
    high = jnp.max(scores, -1)
    weights = jnp.exp(scores - high[..., None])
    denominator = jnp.sum(weights, -1)
    out = jnp.einsum(
        "ghqk,kgo->ghqo", weights.astype(low), values, preferred_element_type=full
    )
    out = jnp.transpose(out / denominator[..., None], (2, 0, 1, 3))
    return out, high + jnp.log(denominator)


def attend_back(queries, grad_out, log_total, delta, keys, values, places):
    allowed = jnp.arange(keys.shape[0], dtype=jnp.int32)[None, :] <= places[:, None]
    scale = HD ** (-0.5)
    scores = jnp.einsum("qgho,kgo->ghqk", queries, keys, preferred_element_type=full) * scale
    weights = jnp.where(allowed, jnp.exp(scores - log_total[..., None]), 0.0)
    weight_grad = jnp.einsum("qgho,kgo->ghqk", grad_out, values, preferred_element_type=full)
    score_grad = (weights * (weight_grad - delta[..., None])).astype(low)
    query_grad = (
        jnp.einsum("ghqk,kgo->qgho", score_grad, keys, preferred_element_type=full) * scale
    )
    key_grad = (
        jnp.einsum("ghqk,qgho->kgo", score_grad, queries, preferred_element_type=full) * scale
    )
    value_grad = jnp.einsum(
        "ghqk,qgho->kgo", weights.astype(low), grad_out, preferred_element_type=full
    )
    return query_grad, key_grad, value_grad


def on_device(
    tok_ids,
    targets,
    positions,
    answer_mask,
    emb,
    head,
    attn_w,
    mlp_w,
    gains,
    emb_row,
    emb_col,
    head_row,
    head_col,
    attn_row,
    attn_col,
    mlp_row,
    mlp_col,
    gains_moment,
):
    pl = Place()
    seqs, his = pl.seqs, pl.his
    tokens = tok_ids.shape[1] // seqs
    picks = targets.shape[1] // seqs
    group = HEADS // KVH
    kv_width = KVH * HD
    block = D // (pl.dps * seqs)
    emb_n, emb_m = emb.shape
    part = FF // 8

    attn_block = jnp.concatenate(
        [attn_w, jnp.pad(gains.T, ((0, 0), (0, 125)))], 1
    ).astype(low)
    attn_full = lax.all_gather(attn_block, ("dp", "seq"), axis=0, tiled=True)
    gain_float = attn_full[:, QKV + D : QKV + D + 3].astype(full).T
    head_rows = lax.all_gather(head.astype(low), "dp", axis=1, tiled=True)
    mlp_blocks = jnp.transpose(mlp_w.astype(low).reshape(block, 3, 8, part), (2, 0, 1, 3))
    mlp_plane = plane_swap(pl, mlp_blocks.reshape(8, block, 3 * part))
    mlp_full = jnp.zeros((pl.dps, his, 2, block, 3 * part), low)
    moving = mlp_plane.reshape(pl.dps, 2, block, 3 * part)
    mlp_full = put(mlp_full, moving, pl.hi, 1)
    for j in range(1, his):
        moving = pl.send(moving, up=1)
        mlp_full = put(mlp_full, moving, (pl.hi + his - j) % his, 1)
    mlp_full = mlp_full.reshape(D, 3 * part)

    ids = jnp.concatenate([tok_ids.reshape(seqs, tokens), targets.reshape(seqs, picks)], 1)
    ids = ids.reshape(seqs * (tokens + picks))
    ids_two = jnp.stack([ids, pl.send(ids, dy=1)])
    emb_low = emb.astype(low)
    chip_low = jnp.concatenate([emb_low, pl.send(emb_low, dc=1), jnp.zeros((8, emb_m), low)])
    local = ids_two - pl.dp * emb_n
    other = ids_two - (pl.dp ^ 1) * emb_n
    places_in = jnp.where(
        (local >= 0) & (local < emb_n),
        local,
        jnp.where((other >= 0) & (other < emb_n), other + emb_n, 2 * emb_n),
    )
    looked = jnp.take(chip_low, places_in[1], axis=0)
    looked = jnp.take(chip_low, places_in[0], axis=0) + pl.send(looked, dy=1)
    start = lax.all_to_all(looked, "seq", split_axis=0, concat_axis=1, tiled=True).astype(full)
    start_tok, start_pick = start[:tokens], start[tokens:]

    token_pos = pl.s * tokens + jnp.arange(tokens, dtype=jnp.int32)
    pick_pos = lax.dynamic_slice_in_dim(positions[0], pl.s * picks, picks)
    cosine, sine = yarn_tables(token_pos.astype(full))
    pick_cosine, pick_sine = yarn_tables(pick_pos.astype(full))
    normed = rms_norm(start, gain_float[0]).astype(low)
    normed_tok, normed_pick = normed[:tokens], normed[tokens:]
    projected = matmul(normed_tok, attn_full[:, D:QKV])
    keys = rotate(projected[:, :kv_width].reshape(tokens, KVH, HD), cosine, sine).astype(low)
    both = jnp.concatenate(
        [keys.reshape(tokens, kv_width), projected[:, kv_width:].astype(low)], 1
    )
    both = lax.all_gather(both, "seq", axis=0, tiled=True)
    key_all = both[:, :kv_width].reshape(-1, KVH, HD)
    value_all = both[:, kv_width:].reshape(-1, KVH, HD)
    queries = (
        rotate(
            matmul(normed_pick, attn_full[:, :D]).reshape(picks, HEADS, HD),
            pick_cosine,
            pick_sine,
        )
        .astype(low)
        .reshape(picks, KVH, group, HD)
    )
    attended, log_total = attend(queries, key_all, value_all, pick_pos)
    attended_low = attended.reshape(picks, D).astype(low)
    middle = start_pick + matmul_nt(attended_low, attn_full[:, QKV : QKV + D])
    normed_two = plane_gather(pl, rms_norm(middle, gain_float[1]).astype(low))
    gate_up = matmul(normed_two, mlp_full[:, : 2 * part])
    gate = gate_up[:, :part]
    upward = gate_up[:, part:]
    mixed = (jax.nn.silu(gate) * upward).astype(low)
    ending = middle + plane_scatter(pl, matmul_nt(mixed, mlp_full[:, 2 * part :]))
    final = rms_norm(ending, gain_float[2]).astype(low)
    chosen = lax.all_gather(final, "seq", axis=0, tiled=True)
    logits = matmul_nt(chosen, head_rows)
    vocab_part = head_rows.shape[0]
    target_hit = (
        targets[0][:, None]
        == pl.s * vocab_part + jnp.arange(vocab_part, dtype=jnp.int32)[None, :]
    )
    part_high = jnp.max(logits, 1)
    part_sum = jnp.sum(jnp.exp(logits - part_high[:, None]), 1)
    part_target = jnp.sum(jnp.where(target_hit, logits, 0.0), 1)
    stats = lax.all_gather(jnp.stack([part_high, part_sum, part_target]), "seq")
    all_high = jnp.max(stats[:, 0], 0)
    all_sum_exp = jnp.sum(stats[:, 1] * jnp.exp(stats[:, 0] - all_high), 0)
    target_logit = jnp.sum(stats[:, 2], 0)
    row_total = all_high + jnp.log(all_sum_exp)
    mask_float = answer_mask.astype(full)
    count = jnp.sum(mask_float)
    own_mask = lax.dynamic_slice_in_dim(mask_float, pl.dp, 1, 0)[0]
    loss_part = jnp.where(
        pl.s == 0,
        jnp.sum(own_mask * (row_total - target_logit + zloss_weight * row_total * row_total)),
        0.0,
    )
    probs = jnp.exp(logits - row_total[:, None])
    logit_grad = (
        (own_mask / count)[:, None]
        * (probs * (1.0 + 2.0 * zloss_weight * row_total)[:, None] - target_hit.astype(full))
    ).astype(low)
    head_rows_grad = matmul_tn(logit_grad, chosen)
    head_grad = lax.psum_scatter(
        head_rows_grad.astype(low), "dp", scatter_dimension=1, tiled=True
    ).astype(full)
    final_grad = seq_sum(matmul(logit_grad, head_rows))
    ending_grad, final_gain_grad = norm_back(ending, gain_float[2], final_grad)
    branch_grad = plane_gather(pl, ending_grad.astype(low))
    down_grad = matmul_tn(branch_grad, mixed)
    mixed_grad = matmul(branch_grad, mlp_full[:, 2 * part :])
    sigmoid_gate = jax.nn.sigmoid(gate)
    gate_grad = mixed_grad * upward * sigmoid_gate * (1.0 + gate * (1.0 - sigmoid_gate))
    upward_grad = mixed_grad * gate * sigmoid_gate
    gate_up_grad = jnp.concatenate([gate_grad, upward_grad], 1).astype(low)
    mlp_term = jnp.concatenate([matmul_tn(normed_two, gate_up_grad), down_grad], 1)
    mlp_term = ring_sum(
        pl, mlp_term.astype(low).reshape(pl.dps, his, 2, block, 3 * part), 1
    )
    mlp_term = plane_swap(pl, mlp_term.astype(low).reshape(8, block, 3 * part))
    mlp_grad = (
        jnp.transpose(mlp_term.reshape(8, block, 3, part), (1, 2, 0, 3))
        .reshape(block, 3 * FF)
        .astype(full)
    )
    middle_part, middle_gain_grad = norm_back(
        middle, gain_float[1], plane_scatter(pl, matmul_nt(gate_up_grad, mlp_full[:, : 2 * part]))
    )
    middle_grad = ending_grad + middle_part
    attn_branch_grad = middle_grad.astype(low)
    attended_grad = matmul(attn_branch_grad, attn_full[:, QKV : QKV + D]).astype(low)
    grad_out = attended_grad.reshape(picks, KVH, group, HD)
    delta = jnp.einsum("qgho,qgho->ghq", grad_out.astype(full), attended)
    query_grad, key_term, value_term = attend_back(
        queries, grad_out, log_total, delta, key_all, value_all, pick_pos
    )
    kv_grad = seq_sum(
        jnp.concatenate([key_term.reshape(-1, kv_width), value_term.reshape(-1, kv_width)], 1)
    )
    query_raw = (
        unrotate(query_grad.reshape(picks, HEADS, HD), pick_cosine, pick_sine)
        .reshape(picks, D)
        .astype(low)
    )
    key_raw = unrotate(kv_grad[:, :kv_width].reshape(tokens, KVH, HD), cosine, sine)
    kv_raw = jnp.concatenate(
        [key_raw.reshape(tokens, kv_width), kv_grad[:, kv_width:]], 1
    ).astype(low)
    tok_up = matmul_nt(kv_raw, attn_full[:, D:QKV])
    pick_up = matmul_nt(query_raw, attn_full[:, :D])
    start_part, start_gain_grad = norm_back(
        start, gain_float[0], jnp.concatenate([tok_up, pick_up], 0)
    )
    start_grad = jnp.concatenate(
        [start_part[:tokens], start_part[tokens:] + middle_grad], 0
    ).astype(low)

    gains_term = jnp.stack([start_gain_grad, middle_gain_grad, final_gain_grad], 1)

    def by_core(rows, core):
        rows = rows.reshape(rows.shape[0], 2, 2, seqs * block)
        return pick(rows, core, 2).reshape(rows.shape[0], D // 2)

    def attn_term(core):
        return jnp.concatenate(
            [
                matmul_tn(by_core(normed_pick, core), query_raw),
                matmul_tn(by_core(normed_tok, core), kv_raw),
                matmul_tn(by_core(attn_branch_grad, core), attended_low),
                jnp.pad(by_core(gains_term.T, core).T, ((0, 0), (0, 125))),
            ],
            1,
        )

    attn_sum = attn_term(pl.c) + pl.send(attn_term(1 - pl.c).astype(low), dc=1).astype(full)
    attn_sum = layer_scatter(pl, attn_sum.reshape(2, his, 2, block, attn_sum.shape[-1]))
    attn_grad = attn_sum[:, : QKV + D]
    gains_grad = attn_sum[:, QKV + D : QKV + D + 3].T

    back_rows = lax.all_to_all(start_grad, "seq", split_axis=1, concat_axis=0, tiled=True)
    back_two = jnp.concatenate([back_rows, pl.send(back_rows, dy=1)], 0)
    chip_grad = (
        jnp.zeros((2 * emb_n + 8, emb_m), full).at[places_in.reshape(-1)].add(back_two.astype(full))
    )
    emb_grad = chip_grad[:emb_n] + pl.send(chip_grad[emb_n : 2 * emb_n], dc=1)

    attn_square = attn_grad * attn_grad + eps_square
    mlp_square = mlp_grad * mlp_grad + eps_square
    emb_square = emb_grad * emb_grad + eps_square
    head_square = head_grad * head_grad + eps_square
    attn_row_new = decay_rate * attn_row + (1.0 - decay_rate) * jnp.mean(attn_square, 1)
    mlp_row_new = decay_rate * mlp_row + (1.0 - decay_rate) * jnp.mean(mlp_square, 1)
    emb_rows = jnp.sum(emb_square, 1)
    head_rows_sum = jnp.sum(head_square, 1)
    scalars = jnp.stack(
        [
            loss_part,
            jnp.sum(attn_row_new),
            jnp.sum(attn_w * attn_w),
            jnp.sum(mlp_row_new),
            jnp.sum(mlp_w * mlp_w),
            jnp.where(pl.s == 0, jnp.sum(emb_row), 0.0),
            jnp.sum(emb * emb),
            jnp.where(pl.dp == 0, jnp.sum(head_row), 0.0),
            jnp.sum(head * head),
            jnp.sum(gains * gains),
            jnp.sum(emb_rows),
            jnp.sum(head_rows_sum),
        ]
    )
    attn_cols_sum, mlp_cols_sum, totals = lax.psum(
        (jnp.sum(attn_square, 0), jnp.sum(mlp_square, 0), scalars), ("dp", "seq")
    )
    emb_row_sum, head_col_sum = lax.psum((emb_rows, jnp.sum(head_square, 0)), "seq")
    head_row_sum, emb_col_sum = lax.psum((head_rows_sum, jnp.sum(emb_square, 0)), "dp")
    attn_col_new = decay_rate * attn_col + (1.0 - decay_rate) * attn_cols_sum / D
    mlp_col_new = decay_rate * mlp_col + (1.0 - decay_rate) * mlp_cols_sum / D
    attn_update = attn_grad * lax.rsqrt(
        attn_row_new[:, None] * attn_col_new[None, :] / (totals[1] / D)
    )
    mlp_update = mlp_grad * lax.rsqrt(mlp_row_new[:, None] * mlp_col_new[None, :] / (totals[3] / D))
    emb_row_new = decay_rate * emb_row + (1.0 - decay_rate) * emb_row_sum / D
    emb_col_new = decay_rate * emb_col + (1.0 - decay_rate) * emb_col_sum / VOCAB
    emb_mean = (decay_rate * totals[5] + (1.0 - decay_rate) * totals[10] / D) / VOCAB
    emb_update = emb_grad * lax.rsqrt(emb_row_new[:, None] * emb_col_new[None, :] / emb_mean)
    head_row_new = decay_rate * head_row + (1.0 - decay_rate) * head_row_sum / D
    head_col_new = decay_rate * head_col + (1.0 - decay_rate) * head_col_sum / VOCAB
    head_mean = (decay_rate * totals[7] + (1.0 - decay_rate) * totals[11] / D) / VOCAB
    head_update = head_grad * lax.rsqrt(head_row_new[:, None] * head_col_new[None, :] / head_mean)
    moment_new = decay_rate * gains_moment + (1.0 - decay_rate) * (
        gains_grad * gains_grad + eps_square
    )
    gains_update = gains_grad * lax.rsqrt(moment_new)
    attn_new = finish(attn_w, attn_update, totals[2], D * (QKV + D))
    mlp_new = finish(mlp_w, mlp_update, totals[4], D * 3 * FF)
    emb_new = finish(emb, emb_update, totals[6], VOCAB * D)
    head_new = finish(head, head_update, totals[8], VOCAB * D)
    gains_new = finish(gains, gains_update, totals[9], 3 * D)
    return (
        totals[0],
        count,
        emb_grad,
        emb_new,
        emb_row_new,
        emb_col_new,
        head_grad,
        head_new,
        head_row_new,
        head_col_new,
        attn_grad,
        attn_new,
        attn_row_new,
        attn_col_new,
        mlp_grad,
        mlp_new,
        mlp_row_new,
        mlp_col_new,
        gains_grad,
        moment_new,
        gains_new,
    )


def solution(mesh):
    return jax.shard_map(
        on_device,
        mesh=mesh,
        in_specs=(
            P("dp", None),
            P("dp", None),
            P("dp", None),
            P(),
            P("dp", "seq"),
            P("seq", "dp"),
            P(("dp", "seq"), None),
            P(("dp", "seq"), None),
            P(None, ("dp", "seq")),
            P("dp"),
            P("seq"),
            P("seq"),
            P("dp"),
            P(("dp", "seq")),
            P(),
            P(("dp", "seq")),
            P(),
            P(None, ("dp", "seq")),
        ),
        out_specs=(
            P(),
            P(),
            P("dp", "seq"),
            P("dp", "seq"),
            P("dp"),
            P("seq"),
            P("seq", "dp"),
            P("seq", "dp"),
            P("seq"),
            P("dp"),
            P(("dp", "seq"), None),
            P(("dp", "seq"), None),
            P(("dp", "seq")),
            P(),
            P(("dp", "seq"), None),
            P(("dp", "seq"), None),
            P(("dp", "seq")),
            P(),
            P(None, ("dp", "seq")),
            P(None, ("dp", "seq")),
            P(None, ("dp", "seq")),
        ),
        check_vma=False,
    )
```

```python
import functools
import math

import jax
import jax.numpy as jnp
from jax import lax
from jax.experimental import pallas
from jax.experimental.pallas import tpu as pltpu
from jax.sharding import PartitionSpec as P

D = 2048
HEADS = 32
KVH = 4
HD = 64
FF = 5632
VOCAB = 32000
QKV = 2560


eps_norm = 1e-05
eps_square = 1e-30
decay_rate = 0.5
learn_rate = 1.0
zloss_weight = 0.0001
orig_context = 2048.0
yarn_factor = 4.0
highest = lax.Precision.HIGHEST


def yarn_tables(places):
    halves = jnp.arange(HD // 2, dtype=jnp.float32)
    inverse = jnp.power(10000.0, -2.0 * halves / HD)
    ratio = orig_context * inverse / (2.0 * math.pi)
    ramp_part = jnp.clip((ratio - 1.0) / 31.0, 0.0, 1.0)
    frequency = inverse / yarn_factor * (1.0 - ramp_part) + inverse * ramp_part
    angles = places[:, None] * frequency[None, :]
    magnitude = 0.1 * math.log(yarn_factor) + 1.0
    return (jnp.cos(angles) * magnitude, jnp.sin(angles) * magnitude)


def rotate(values, cosine, sine):
    first = values[..., : HD // 2]
    second = values[..., HD // 2 :]
    cosine_row = cosine[:, None, :]
    sine_row = sine[:, None, :]
    return jnp.concatenate(
        [first * cosine_row - second * sine_row, second * cosine_row + first * sine_row], -1
    )


def unrotate(values, cosine, sine):
    first = values[..., : HD // 2]
    second = values[..., HD // 2 :]
    cosine_row = cosine[:, None, :]
    sine_row = sine[:, None, :]
    return jnp.concatenate(
        [first * cosine_row + second * sine_row, second * cosine_row - first * sine_row], -1
    )


def rms_norm(values, gain_row):
    return values * lax.rsqrt(jnp.mean(values * values, -1, keepdims=True) + eps_norm) * gain_row


def norm_back(values, gain_row, upstream):
    factor = lax.rsqrt(jnp.mean(values * values, -1, keepdims=True) + eps_norm)
    normed = values * factor
    gain_grad = jnp.sum(upstream * normed, 0)
    inner = upstream * gain_row
    return (factor * (inner - normed * jnp.mean(inner * normed, -1, keepdims=True)), gain_grad)


def matmul(left, right):
    return jnp.dot(left, right, preferred_element_type=jnp.float32)


def matmul_nt(left, right):
    return lax.dot_general(
        left, right, (((1,), (1,)), ((), ())), preferred_element_type=jnp.float32
    )


def matmul_tn(left, right):
    return lax.dot_general(
        left, right, (((0,), (0,)), ((), ())), preferred_element_type=jnp.float32
    )


def finish(weight, update, weight_square, entries):
    return weight - learn_rate * jnp.maximum(0.001, jnp.sqrt(weight_square / entries)) * update


low = jnp.bfloat16
full = jnp.float32


class Place:
    def __init__(self):
        self.seqs = lax.axis_size("seq")
        self.dps = lax.axis_size("dp")
        self.dp = lax.axis_index("dp")
        self.s = lax.axis_index("seq")
        self.his = self.seqs // 2
        self.y, self.c = self.dp // 2, self.dp % 2
        self.hi, self.lo = self.s // 2, self.s % 2

    def send(self, value, dy=0, dc=0, dlo=0, up=0):
        pairs = []
        for d in range(self.dps):
            for s in range(self.seqs):
                to_d = d ^ (2 * dy + dc)
                to_s = ((s // 2 + up) % self.his) * 2 + ((s % 2) ^ dlo)
                pairs.append((d * self.seqs + s, to_d * self.seqs + to_s))
        return lax.ppermute(value, ("dp", "seq"), pairs)

    def ways(self, names):
        steps = []
        for name in names:
            if name == "hi":
                bit = 1
                while bit < self.his:
                    steps.append(lambda value, bit=bit: self.swap_hi(value, bit))
                    bit *= 2
            else:
                steps.append(lambda value, name=name: self.send(value, **{name: 1}))
        return steps

    def swap_hi(self, value, bit):
        pairs = []
        for d in range(self.dps):
            for s in range(self.seqs):
                pairs.append((d * self.seqs + s, d * self.seqs + (s ^ (2 * bit))))
        return lax.ppermute(value, ("dp", "seq"), pairs)


def after(value, *events):
    return lax.optimization_barrier((value, *events))[0] if events else value


def pick(array, index, axis):
    return lax.dynamic_index_in_dim(array, index, axis, keepdims=False)


def put(array, block, index, axis):
    return lax.dynamic_update_slice_in_dim(array, jnp.expand_dims(block, axis), index, axis)


def line_parts(pl, blocks):
    n = pl.his
    got = []
    for dc in range(2):
        for k in range(n):
            block = pick(blocks, (pl.c ^ dc) * n + (pl.hi + k) % n, 0)
            got.append(pl.send(block, dc=dc, up=k) if dc or k else block)
    return got


def line_place(pl, got):
    n = pl.his
    out = jnp.zeros((2 * n, *got[0].shape), got[0].dtype)
    for at, block in enumerate(got):
        origin = (pl.c ^ (at // n)) * n + (pl.hi + n - at % n) % n
        out = put(out, block, origin, 0)
    return out


def line_gather(pl, rows, work=()):
    first = jnp.stack([rows] + [after(pl.send(rows, up=k), *work) for k in range(1, pl.his)])
    both = jnp.stack([first, pl.send(first, dc=1)])
    return both.reshape(2 * pl.his * rows.shape[0], rows.shape[1])


def hi_sum_start(pl, part):
    parts = [pick(part, pl.hi, 0)]
    for k in range(1, pl.his):
        block = pick(part, (pl.hi + k) % pl.his, 0).astype(low)
        parts.append(pl.send(block, up=k))
    return parts


def hi_sum_end(parts, *work):
    parts = after(parts, *work)
    return sum((part.astype(full) for part in parts[1:]), parts[0].astype(full))


def cross_start(pl, term):
    a, b = term[:, 0], term[:, 1]
    got_a = pl.send(pick(a, 1 - pl.y, 0), dy=1)
    got_b = pl.send(pick(b, 1 - pl.lo, 2), dlo=1)
    return a, b, got_a, got_b


def cross_next(pl, state, *work):
    a, b, got_a, got_b = state
    got_a, got_b = after((got_a, got_b), *work)
    a = pick(a, pl.y, 0).astype(full) + got_a.astype(full)
    b = pick(b, pl.lo, 2).astype(full) + got_b.astype(full)
    send_a = pick(a, 1 - pl.lo, 1).astype(low)
    send_b = pick(b, 1 - pl.y, 0).astype(low)
    return pick(a, pl.lo, 1), pick(b, pl.y, 0), pl.send(send_a, dlo=1), pl.send(send_b, dy=1)


def cross_end(pl, state, *work):
    a, b, got_a, got_b = state
    got_a, got_b = after((got_a, got_b), *work)
    a = (a + got_a.astype(full)).astype(low)
    b = (b + got_b.astype(full)).astype(low)
    return jnp.stack([a, b]).reshape(2 * pl.his, *a.shape[1:])


def split_kernel(line, part, in_ref, out_ref):
    for j in range(3):
        for t in range(line):
            at = (j * line + t) * part
            out_ref[t, :, j * part : (j + 1) * part] = in_ref[:, at : at + part].astype(low)


def split_columns(weight, line):
    rows, columns = weight.shape
    part = columns // (3 * line)
    return pallas.pallas_call(
        lambda *refs: split_kernel(line, part, *refs),
        out_shape=jax.ShapeDtypeStruct((line, rows, 3 * part), low),
        in_specs=[pallas.BlockSpec(memory_space=pltpu.VMEM)],
        out_specs=pallas.BlockSpec(memory_space=pltpu.VMEM),
        compiler_params=pltpu.CompilerParams(vmem_limit_bytes=40 * 2**20),
        name="split_columns",
    )(weight)


def join_kernel(line, part, in_ref, out_ref, rows_ref, columns_ref):
    total = jnp.zeros(rows_ref.shape, full)
    for j in range(3):
        for t in range(line):
            at = (j * line + t) * part
            block = in_ref[t, :, j * part : (j + 1) * part].astype(full)
            out_ref[:, at : at + part] = block
            square = block * block + eps_square
            columns_ref[:, at : at + part] = jnp.sum(square, 0, keepdims=True)
            total = total + jnp.sum(square, 1, keepdims=True)
    rows_ref[...] = total


def join_columns(blocks):
    line, rows, wide = blocks.shape
    part = wide // 3
    grad, row_sum, column_sum = pallas.pallas_call(
        lambda *refs: join_kernel(line, part, *refs),
        out_shape=(
            jax.ShapeDtypeStruct((rows, line * wide), full),
            jax.ShapeDtypeStruct((rows, 1), full),
            jax.ShapeDtypeStruct((1, line * wide), full),
        ),
        in_specs=[pallas.BlockSpec(memory_space=pltpu.VMEM)],
        out_specs=(pallas.BlockSpec(memory_space=pltpu.VMEM),) * 3,
        compiler_params=pltpu.CompilerParams(vmem_limit_bytes=40 * 2**20),
        name="join_columns",
    )(blocks)
    return grad, row_sum[:, 0], column_sum[0]


def halve(pl, part, mine, axis, **way):
    got = pl.send(pick(part, 1 - mine, axis).astype(low), **way)
    return pick(part, mine, axis).astype(full) + got.astype(full)


def hi_sum(pl, part, *work):
    total = pick(part, pl.hi, 0).astype(full)
    for k in range(1, pl.his):
        block = pick(part, (pl.hi + k) % pl.his, 0).astype(low)
        total = total + after(pl.send(block, up=k), *work).astype(full)
    return total


MESH = pallas.DeviceIdType.MESH
ROWS = 16
SMALL = pallas.CostEstimate(flops=1024, bytes_accessed=1024, transcendentals=0)


class Core:
    def __init__(self, his):
        dp, s = lax.axis_index("dp"), lax.axis_index("seq")
        self.his = his
        self.hi, self.lo, self.c = s // 2, s % 2, dp % 2
        self.side = {"c": self.c, "lo": self.lo}
        self.ids = {
            "c": (dp + 1 - 2 * self.c, s),
            "lo": (dp, s + 1 - 2 * self.lo),
            "up": (dp, lax.rem(self.hi + 1, his) * 2 + self.lo),
            "down": (dp, lax.rem(self.hi + his - 1, his) * 2 + self.lo),
        }

    def meet(self, *names):
        barrier = pltpu.get_barrier_semaphore()
        for name in names:
            pallas.semaphore_signal(
                barrier, inc=1, device_id=self.ids[name], device_id_type=MESH
            )
        pallas.semaphore_wait(barrier, len(names))

    def copy(self, source, target, sems, at, name):
        return pltpu.make_async_remote_copy(
            src_ref=source,
            dst_ref=target,
            send_sem=sems[0].at[at],
            recv_sem=sems[1].at[at],
            device_id=self.ids[name],
            device_id_type=MESH,
        )


def by_rows(n, step):
    def one(i, carry):
        step(pallas.ds(pallas.multiple_of(i * ROWS, ROWS), ROWS))
        return carry

    lax.fori_loop(0, n // ROWS, one, 0)


def kernel_scatter(core, name, part, total, held, side_sems, up_sems):
    his, side = core.his, core.side[name]
    side_out, side_in, up_out, up_in = held
    n = part.shape[2]
    over = []
    for j in range(his):
        h = lax.rem(core.hi + 2 * his - 1 - j, his)

        def cast(at, j=j, h=h):
            side_out[j, at, :] = part[h, 1 - side, at, :].astype(low)

        by_rows(n, cast)
        over.append(core.copy(side_out.at[j], side_in.at[j], side_sems, j, name))
        over[j].start()
    climb = []
    for j in range(his):
        h = lax.rem(core.hi + 2 * his - 1 - j, his)
        over[j].wait_recv()
        if j:
            climb[j - 1].wait_recv()

        def add(at, j=j, h=h):
            acc = part[h, side, at, :].astype(full) + side_in[j, at, :].astype(full)
            if j:
                acc = acc + up_in[j - 1, at, :].astype(full)
            if j < his - 1:
                up_out[j, at, :] = acc.astype(low)
            else:
                total[at, :] = acc

        by_rows(n, add)
        if j < his - 1:
            climb.append(core.copy(up_out.at[j], up_in.at[j], up_sems, j, "up"))
            climb[j].start()
    return over + climb


def kernel_gather(core, name, own, out, local_sem, side_sems, up_sems):
    his, side = core.his, core.side[name]
    here = pltpu.make_async_copy(own, out.at[core.hi, side], local_sem)
    here.start()
    over, climb = [], []
    for j in range(his):
        h = lax.rem(core.hi + his - j, his)
        block = out.at[h, side]
        source = own if j == 0 else block
        if j:
            climb[j - 1].wait_recv()
        if j < his - 1:
            climb.append(core.copy(source, block, up_sems, j, "up"))
            climb[j].start()
        over.append(core.copy(source, block, side_sems, j, name))
        over[j].start()
    for copy in over:
        copy.wait_recv()
    here.wait()
    return over + climb


def sent(copies):
    for copy in copies:
        copy.wait_send()


def norm_rows(values, gain):
    return values * lax.rsqrt(jnp.mean(values * values, -1, keepdims=True) + eps_norm) * gain


def norm_rows_back(values, gain, upstream):
    factor = lax.rsqrt(jnp.mean(values * values, -1, keepdims=True) + eps_norm)
    normed = values * factor
    inner = upstream * gain
    back = factor * (inner - normed * jnp.mean(inner * normed, -1, keepdims=True))
    return back, jnp.sum(upstream * normed, 0, keepdims=True)


def norm_gather_body(his, values, gain, out, own, *sems):
    core = Core(his)
    by_rows(
        values.shape[0],
        lambda at: own.__setitem__(
            (at, slice(None)), norm_rows(values[at, :], gain[...]).astype(low)
        ),
    )
    core.meet("c", "up", "down")
    sent(kernel_gather(core, "c", own, out, sems[0], sems[1:3], sems[3:5]))


def turn_keys(source, cosine, sine, target):
    width = KVH * HD
    for at in range(0, width, 2 * HD):
        pair = turned(source[:, at : at + 2 * HD], cosine, sine)
        target[:, at : at + 2 * HD] = pair.astype(low)
    target[:, width:] = source[:, width:].astype(low)


def keys_body(his, projected, cosine, sine, out, own, *sems):
    core = Core(his)
    turn_keys(projected, cosine[...], sine[...], own)
    core.meet("lo", "up", "down")
    sent(kernel_gather(core, "lo", own, out, sems[0], sems[1:3], sems[3:5]))


def keys_back_body(his, part, cosine, sine, out, total, *rest):
    held, sems = rest[:4], rest[4:]
    core = Core(his)
    core.meet("lo", "up", "down")
    copies = kernel_scatter(core, "lo", part, total, held, sems[0:2], sems[2:4])
    turn_keys(total, cosine[...], -sine[...], out)
    sent(copies)


def ending_body(his, part, middle, gain, ending, chosen, own, *rest):
    held, sems = rest[:4], rest[4:]
    core = Core(his)
    core.meet("c", "lo", "up", "down")
    copies = kernel_scatter(core, "c", part, ending, held, sems[0:2], sems[2:4])

    def finish_rows(at):
        values = ending[at, :] + middle[at, :]
        ending[at, :] = values
        own[at, :] = norm_rows(values, gain[...]).astype(low)

    by_rows(middle.shape[0], finish_rows)
    copies += kernel_gather(core, "lo", own, chosen, sems[4], sems[5:7], sems[7:9])
    sent(copies)


def ending_back_body(his, part, ending, gain, grad, gain_grad, branch, own, *rest):
    held, sems = rest[:4], rest[4:]
    core = Core(his)
    core.meet("c", "lo", "up", "down")
    copies = kernel_scatter(core, "lo", part, grad, held, sems[0:2], sems[2:4])
    gain_grad[...] = jnp.zeros(gain_grad.shape, full)

    def back_rows(at):
        back, gained = norm_rows_back(ending[at, :], gain[...], grad[at, :])
        grad[at, :] = back
        own[at, :] = back.astype(low)
        gain_grad[...] += gained

    by_rows(ending.shape[0], back_rows)
    copies += kernel_gather(core, "c", own, branch, sems[4], sems[5:7], sems[7:9])
    sent(copies)


def middle_back_body(his, part, middle, gain, ending_grad, grad, grad_low, gain_grad, *rest):
    held, sems = rest[:4], rest[4:]
    core = Core(his)
    core.meet("c", "up", "down")
    copies = kernel_scatter(core, "c", part, grad, held, sems[0:2], sems[2:4])
    gain_grad[...] = jnp.zeros(gain_grad.shape, full)

    def back_rows(at):
        back, gained = norm_rows_back(middle[at, :], gain[...], grad[at, :])
        back = back + ending_grad[at, :]
        grad[at, :] = back
        grad_low[at, :] = back.astype(low)
        gain_grad[...] += gained

    by_rows(middle.shape[0], back_rows)
    sent(copies)


def move(body, collective_id, outs, args, his, scatter=None, own=None, own_type=low, gathers=False):
    dma = pltpu.SemaphoreType.DMA
    scratch = []
    if own:
        scratch.append(pltpu.VMEM(own, own_type))
    if scatter:
        scratch += [pltpu.VMEM((count, *scatter), low) for count in (his, his, his - 1, his - 1)]
        scratch += [dma((his,)), dma((his,)), dma((his - 1,)), dma((his - 1,))]
    if gathers:
        scratch += [dma, dma((his,)), dma((his,)), dma((his - 1,)), dma((his - 1,))]
    return pallas.pallas_call(
        body,
        out_shape=tuple(jax.ShapeDtypeStruct(shape, dtype) for shape, dtype, _ in outs),
        in_specs=[pallas.BlockSpec(memory_space=pltpu.VMEM)] * len(args),
        out_specs=tuple(pallas.BlockSpec(memory_space=memory) for _, _, memory in outs),
        scratch_shapes=scratch,
        cost_estimate=SMALL,
        compiler_params=pltpu.CompilerParams(
            collective_id=collective_id,
            has_side_effects=True,
            vmem_limit_bytes=48 * 2**20,
        ),
    )(*args)


HALF = HD // 2
STACK = 4


def turn_tables(cosine, sine):
    return jnp.concatenate([cosine] * 4, 1), jnp.concatenate([-sine, sine] * 2, 1)


def turned(values, cosine, sine):
    lane = lax.broadcasted_iota(jnp.int32, values.shape, 1) % HD
    other = jnp.where(
        lane < HALF, pltpu.roll(values, 2 * HD - HALF, 1), pltpu.roll(values, HALF, 1)
    )
    return values * cosine + other * sine


def heads_loop(loops, step):
    def one(t, carry):
        step(t)
        return carry

    lax.fori_loop(0, loops, one, 0)


def split_kv(kv, k_held, v_held):
    width = KVH * HD
    for g in range(KVH):
        k_held[g] = kv[:, g * HD : (g + 1) * HD]
        v_held[g] = kv[:, width + g * HD : width + (g + 1) * HD]


def allowed_keys(places, keys):
    places = jnp.concatenate([places] * STACK, 0)
    return lax.broadcasted_iota(jnp.int32, (places.shape[0], keys), 1) <= places


def dot_nt(left, right):
    return lax.dot_general(
        left, right, (((1,), (1,)), ((), ())), preferred_element_type=jnp.float32
    )


def attend_body(raw, cosine, sine, places, kv, turned_out, out_low, held_out, logs, k_held, v_held):
    picks, keys = raw.shape[0], kv.shape[0]
    split_kv(kv, k_held, v_held)
    for j in range(D // (2 * HD)):
        pair = turned(raw[:, 2 * HD * j : 2 * HD * (j + 1)], cosine[...], sine[...]).astype(low)
        for i in range(2):
            t, at = divmod(2 * j + i, STACK)
            turned_out[t, at * picks : (at + 1) * picks, :] = pair[:, i * HD : (i + 1) * HD]
    allowed = allowed_keys(places[...], keys)

    def step(t):
        g = t // (HEADS // KVH // STACK)
        scores = dot_nt(turned_out[t], k_held[g]) * HD ** (-0.5)
        scores = jnp.where(allowed, scores, -1e30)
        high = jnp.max(scores, 1, keepdims=True)
        weights = jnp.exp(scores - high)
        total = jnp.sum(weights, 1, keepdims=True)
        result = jnp.dot(weights.astype(low), v_held[g], preferred_element_type=full)
        held_out[t] = result / total
        logs[t] = jnp.broadcast_to(high + jnp.log(total), (STACK * picks, 2 * HD))

    heads_loop(HEADS // STACK, step)
    for j in range(D // (2 * HD)):
        pair = []
        for i in range(2):
            t, at = divmod(2 * j + i, STACK)
            pair.append(held_out[t, at * picks : (at + 1) * picks, :])
        pair = jnp.concatenate(pair, 1)
        out_low[:, 2 * HD * j : 2 * HD * (j + 1)] = pair.astype(low)


def attend_rows(raw, tables, places, kv):
    picks, keys = raw.shape[0], kv.shape[0]
    stacks, rows = HEADS // STACK, STACK * picks
    return pallas.pallas_call(
        attend_body,
        out_shape=(
            jax.ShapeDtypeStruct((stacks, rows, HD), low),
            jax.ShapeDtypeStruct((picks, D), low),
            jax.ShapeDtypeStruct((stacks, rows, HD), full),
            jax.ShapeDtypeStruct((stacks, rows, 2 * HD), full),
        ),
        in_specs=[pallas.BlockSpec(memory_space=pltpu.VMEM)] * 5,
        out_specs=(pallas.BlockSpec(memory_space=pltpu.VMEM),) * 4,
        scratch_shapes=[pltpu.VMEM((KVH, keys, HD), low)] * 2,
        compiler_params=pltpu.CompilerParams(vmem_limit_bytes=56 * 2**20),
        cost_estimate=SMALL,
        name="attend",
    )(raw, *tables, places[:, None], kv)


def attend_back_body(
    grad, cosine, sine, places, kv, queries, held_out, logs, raw, kv_grad, k_held, v_held,
    grad_held, query_held, *sums
):
    picks, keys = grad.shape[0], kv.shape[0]
    scale = HD ** (-0.5)
    split_kv(kv, k_held, v_held)
    for j in range(D // (2 * HD)):
        pair = grad[:, 2 * HD * j : 2 * HD * (j + 1)]
        for i in range(2):
            t, at = divmod(2 * j + i, STACK)
            grad_held[t, at * picks : (at + 1) * picks, :] = pair[:, i * HD : (i + 1) * HD]
    allowed = allowed_keys(places[...], keys)
    total = sums[0] if sums else kv_grad
    total[...] = jnp.zeros(total.shape, full)

    def step(t):
        g = t // (HEADS // KVH // STACK)
        query, up = queries[t], grad_held[t]
        delta = jnp.sum(up.astype(full) * held_out[t], 1, keepdims=True)
        scores = dot_nt(query, k_held[g]) * scale
        weights = jnp.where(allowed, jnp.exp(scores - logs[t][:, :1]), 0.0)
        weight_grad = dot_nt(up, v_held[g])
        score_grad = (weights * (weight_grad - delta)).astype(low)
        query_held[t] = jnp.dot(score_grad, k_held[g], preferred_element_type=full) * scale
        total[g] += matmul_tn(query, score_grad) * scale
        total[KVH + g] += matmul_tn(up, weights.astype(low))

    heads_loop(HEADS // STACK, step)
    for j in range(D // (2 * HD)):
        pair = []
        for i in range(2):
            t, at = divmod(2 * j + i, STACK)
            pair.append(query_held[t, at * picks : (at + 1) * picks, :])
        pair = jnp.concatenate(pair, 1)
        raw[:, 2 * HD * j : 2 * HD * (j + 1)] = turned(pair, cosine[...], -sine[...]).astype(low)
    if sums:
        for g in range(0, 2 * KVH, 2):
            both = jnp.concatenate([total[g], total[g + 1]], 0)
            kv_grad[:, g * HD : (g + 2) * HD] = both.T


def attend_rows_back(grad, tables, places, kv, queries, held_out, logs):
    picks, keys = grad.shape[0], kv.shape[0]
    stacks, rows = HEADS // STACK, STACK * picks
    outside = keys > 4096
    by_head = (2 * KVH, HD, keys)
    raw, kv_grad = pallas.pallas_call(
        attend_back_body,
        out_shape=(
            jax.ShapeDtypeStruct((picks, D), low),
            jax.ShapeDtypeStruct(by_head if outside else (keys, 2 * KVH * HD), full),
        ),
        in_specs=[pallas.BlockSpec(memory_space=pltpu.VMEM)] * 8,
        out_specs=(pallas.BlockSpec(memory_space=pltpu.VMEM),) * 2,
        scratch_shapes=[
            pltpu.VMEM((KVH, keys, HD), low),
            pltpu.VMEM((KVH, keys, HD), low),
            pltpu.VMEM((stacks, rows, HD), low),
            pltpu.VMEM((stacks, rows, HD), full),
        ]
        + ([] if outside else [pltpu.VMEM(by_head, full)]),
        compiler_params=pltpu.CompilerParams(vmem_limit_bytes=58 * 2**20),
        cost_estimate=SMALL,
        name="attend_back",
    )(grad, *tables, places[:, None], kv, queries, held_out, logs)
    return raw, kv_grad.reshape(2 * KVH * HD, keys).T if outside else kv_grad


def sum_body(his, rows, packed, out, bufs, got, send_sems, recv_sems):
    core = Core(his)
    dp, s = lax.axis_index("dp"), lax.axis_index("seq")
    ways = [("lo", 0)]
    bit = 1
    while bit < his:
        up = lax.rem(core.hi // bit, 2)
        core.ids[f"hi{bit}"] = (dp, s + 2 * bit * (1 - 2 * up))
        ways.append((f"hi{bit}", 0))
        bit *= 2
    y = dp // 2
    core.ids["y"] = (dp + 2 * (1 - 2 * y), s)
    ways += [("c", 1), ("y", 1)]
    core.meet(*(name for name, _ in ways))
    bufs[0] = packed[...]
    copies = []
    for j, (name, over_dp) in enumerate(ways):
        first = rows[0] if over_dp else 0
        last = rows[0] + rows[1] + (rows[2] if over_dp else 0)
        copy = core.copy(
            bufs.at[j, first:last], got.at[j, first:last], (send_sems, recv_sems), j, name
        )
        copy.start()
        copies.append(copy)
        copy.wait_recv()
        bufs[j + 1] = bufs[j]
        bufs[j + 1, first:last] = bufs[j, first:last] + got[j, first:last]
    out[...] = bufs[len(ways)]
    sent(copies)


def padded(parts):
    return [
        jnp.pad(part, (0, -part.shape[0] % 1024)).reshape(-1, 128) for part in parts
    ]


def sum_statistics(his, over_seq, over_all, over_dp):
    groups = [padded(parts) for parts in (over_seq, over_all, over_dp)]
    rows = tuple(sum(part.shape[0] for part in group) for group in groups)
    steps = 3 + his.bit_length() - 1
    total = sum(rows)
    dma = pltpu.SemaphoreType.DMA
    out = pallas.pallas_call(
        functools.partial(sum_body, his, rows),
        out_shape=jax.ShapeDtypeStruct((total, 128), full),
        in_specs=[pallas.BlockSpec(memory_space=pltpu.VMEM)],
        out_specs=pallas.BlockSpec(memory_space=pltpu.VMEM),
        scratch_shapes=[
            pltpu.VMEM((steps + 1, total, 128), full),
            pltpu.VMEM((steps, total, 128), full),
            dma((steps,)),
            dma((steps,)),
        ],
        compiler_params=pltpu.CompilerParams(
            collective_id=6, has_side_effects=True, vmem_limit_bytes=32 * 2**20
        ),
        name="sum_statistics",
    )(jnp.concatenate([part for group in groups for part in group], 0))
    results, at = [], 0
    for parts, group in zip((over_seq, over_all, over_dp), groups):
        for part, block in zip(parts, group):
            results.append(out[at : at + block.shape[0]].reshape(-1)[: part.shape[0]])
            at += block.shape[0]
    return results


def on_device(
    tok_ids,
    targets,
    positions,
    answer_mask,
    emb,
    head,
    attn_w,
    mlp_w,
    gains,
    emb_row,
    emb_col,
    head_row,
    head_col,
    attn_row,
    attn_col,
    mlp_row,
    mlp_col,
    gains_moment,
):
    pl = Place()
    seqs, his = pl.seqs, pl.his
    tokens = tok_ids.shape[1] // seqs
    picks = targets.shape[1] // seqs
    group = HEADS // KVH
    kv_width = KVH * HD
    block = D // (pl.dps * seqs)
    emb_n, emb_m = emb.shape
    line = 2 * his
    part = FF // line
    wide = 3 * part

    def swap_rows(rows, **way):
        return pl.send(rows.astype(low), **way)

    mlp_got = line_parts(pl, split_columns(mlp_w, line))
    ids = jnp.concatenate([tok_ids.reshape(seqs, tokens), targets.reshape(seqs, picks)], 1)
    ids = ids.reshape(seqs * (tokens + picks))
    ids_all = jnp.stack(
        [
            jnp.stack([ids, pl.send(ids, dc=1)]),
            jnp.stack([pl.send(ids, dy=1), pl.send(ids, dy=1, dc=1)]),
        ]
    )
    local = ids_all - pl.dp * emb_n
    local = jnp.where((local >= 0) & (local < emb_n), local, emb_n)

    def look(dy, dc, *work):
        at = after(local[dy, dc], *work)
        rows = jnp.take(emb, jnp.minimum(at, emb_n - 1), axis=0, mode="clip")
        return jnp.where((at < emb_n)[:, None], rows, 0.0).astype(low)

    far_other = look(1, 1)
    far_got = pl.send(far_other, dc=1)
    far_own = look(1, 0, far_other)
    near_other = look(0, 1, far_own)
    near_got = pl.send(near_other, dc=1)
    far_sum = far_own + after(far_got, near_other)
    across = pl.send(far_sum, dy=1)

    first_block = jnp.concatenate(
        [attn_w[:, :QKV], jnp.pad(gains.T, ((0, 0), (0, 125)))], 1
    ).astype(low)
    qkv_full = lax.all_gather(first_block, ("dp", "seq"), axis=0, tiled=True)
    gain_float = qkv_full[:, QKV : QKV + 3].astype(full).T
    out_full = lax.all_gather(
        attn_w[:, QKV:].astype(low), ("dp", "seq"), axis=0, tiled=True
    )
    near_own = look(0, 0, far_sum)
    near_sum = near_own + after(near_got, near_own)
    head_low = after(head, near_sum).astype(low)
    emb_square_sum = jnp.sum(after(emb, head_low) ** 2)
    looked = near_sum + after(across, emb_square_sum)
    mlp_line = line_place(pl, after(mlp_got, looked)).reshape(2, his, block, wide)
    mlp_x, mlp_y = pl.send(mlp_line, dlo=1), pl.send(mlp_line, dy=1)
    start = lax.all_to_all(looked, "seq", split_axis=0, concat_axis=1, tiled=True).astype(full)

    token_pos = pl.s * tokens + jnp.arange(tokens, dtype=jnp.int32)
    pick_pos = lax.dynamic_slice_in_dim(positions[0], pl.s * picks, picks)
    token_tables = turn_tables(*yarn_tables(token_pos.astype(full)))
    pick_tables = turn_tables(*yarn_tables(pick_pos.astype(full)))
    start, token_tables, pick_tables, mlp_line = lax.optimization_barrier(
        (start, token_tables, pick_tables, mlp_line)
    )
    head_rows = lax.all_gather(after(head_low, start), "dp", axis=1, tiled=True)
    normed = rms_norm(start, gain_float[0]).astype(low)
    normed_tok, normed_pick = normed[:tokens], normed[tokens:]
    start_pick = start[tokens:]
    projected = matmul(normed_tok, qkv_full[:, D:QKV])
    (kv_all,) = move(
        functools.partial(keys_body, his),
        0,
        [((his, 2, tokens, 2 * kv_width), low, pallas.ANY)],
        [projected, *token_tables],
        his,
        own=(tokens, 2 * kv_width),
        gathers=True,
    )
    kv_all = kv_all.reshape(seqs * tokens, 2 * kv_width)
    raw = matmul(normed_pick, qkv_full[:, :D])
    mlp_x, mlp_y = after((mlp_x, mlp_y), kv_all)
    mlp_far = (pl.send(mlp_x[0], dy=1), pl.send(mlp_y[1], dlo=1))
    pick_line = line_gather(pl, after(normed_pick, kv_all))
    queries, attended_low, attended, log_total = attend_rows(
        after(raw, mlp_x, mlp_y), pick_tables, pick_pos, kv_all
    )

    def shares(rows):
        rows = jnp.transpose(rows.reshape(picks, line, D // line), (1, 0, 2))
        return jnp.concatenate(line_parts(pl, rows), 0)

    attended_share = shares(attended_low)
    middle = start_pick + matmul_nt(attended_low, out_full)
    mlp_full = jnp.zeros((2, 2, his, 2, block, wide), low)
    for held, at_y, at_lo in (
        (after(mlp_line, middle), pl.y, pl.lo),
        (mlp_x, pl.y, 1 - pl.lo),
        (mlp_y, 1 - pl.y, pl.lo),
    ):
        mlp_full = lax.dynamic_update_slice(
            mlp_full, held[None, :, :, None], (at_y, 0, 0, at_lo, 0, 0)
        )
    (normed_two,) = move(
        functools.partial(norm_gather_body, his),
        1,
        [((his, 2, picks, D), low, pallas.ANY)],
        [middle, gain_float[1:2]],
        his,
        own=(picks, D),
        gathers=True,
    )
    normed_two = normed_two.reshape(line * picks, D)

    mlp_far = after(mlp_far, normed_two)
    for at_c in range(2):
        mlp_full = lax.dynamic_update_slice(
            mlp_full, mlp_far[at_c][None, None, :, None], (1 - pl.y, at_c, 0, 1 - pl.lo, 0, 0)
        )
    mlp_full = mlp_full.reshape(D, wide)

    gate_up = matmul(normed_two, mlp_full[:, : 2 * part])
    gate = gate_up[:, :part]
    upward = gate_up[:, part:]
    mixed = (jax.nn.silu(gate) * upward).astype(low)
    down = matmul_nt(mixed, mlp_full[:, 2 * part :])
    ending, chosen = move(
        functools.partial(ending_body, his),
        2,
        [((picks, D), full, pltpu.VMEM), ((his, 2, picks, D), low, pallas.ANY)],
        [down.reshape(his, 2, picks, D), middle, gain_float[2:3]],
        his,
        scatter=(picks, D),
        own=(picks, D),
        gathers=True,
    )
    chosen = chosen.reshape(seqs * picks, D)
    logits = matmul_nt(chosen, head_rows)
    vocab_part = head_rows.shape[0]
    target_hit = (
        targets[0][:, None]
        == pl.s * vocab_part + jnp.arange(vocab_part, dtype=jnp.int32)[None, :]
    )
    part_high = jnp.max(logits, 1)
    part_sum = jnp.sum(jnp.exp(logits - part_high[:, None]), 1)
    part_target = jnp.sum(jnp.where(target_hit, logits, 0.0), 1)
    stats = jnp.stack([part_high, part_sum, part_target])
    for step in pl.ways(("dlo", "hi")):
        other = step(stats)
        larger = jnp.maximum(stats[0], other[0])
        summed = stats[1] * jnp.exp(stats[0] - larger) + other[1] * jnp.exp(other[0] - larger)
        stats = jnp.stack([larger, summed, stats[2] + other[2]])
    all_high, all_sum_exp, target_logit = stats
    row_total = all_high + jnp.log(all_sum_exp)
    mask_float = answer_mask.astype(full)
    count = jnp.sum(mask_float)
    own_mask = lax.dynamic_slice_in_dim(mask_float, pl.dp, 1, 0)[0]
    loss_part = jnp.where(
        pl.s == 0,
        jnp.sum(own_mask * (row_total - target_logit + zloss_weight * row_total * row_total)),
        0.0,
    )
    probs = jnp.exp(logits - row_total[:, None])
    logit_grad = (
        (own_mask / count)[:, None]
        * (probs * (1.0 + 2.0 * zloss_weight * row_total)[:, None] - target_hit.astype(full))
    ).astype(low)
    chosen_part = matmul(logit_grad, head_rows)
    ending_grad, final_gain_grad, branch_grad = move(
        functools.partial(ending_back_body, his),
        3,
        [
            ((picks, D), full, pltpu.VMEM),
            ((1, D), full, pltpu.VMEM),
            ((his, 2, picks, D), low, pallas.ANY),
        ],
        [chosen_part.reshape(his, 2, picks, D), ending, gain_float[2:3]],
        his,
        scatter=(picks, D),
        own=(picks, D),
        gathers=True,
    )
    branch_grad = branch_grad.reshape(line * picks, D)
    mixed_grad = matmul(branch_grad, mlp_full[:, 2 * part :])
    sigmoid_gate = jax.nn.sigmoid(gate)
    gate_grad = mixed_grad * upward * sigmoid_gate * (1.0 + gate * (1.0 - sigmoid_gate))
    upward_grad = mixed_grad * gate * sigmoid_gate
    gate_up_grad = jnp.concatenate([gate_grad, upward_grad], 1).astype(low)
    middle_up = matmul_nt(gate_up_grad, mlp_full[:, : 2 * part])
    down_grad = matmul_tn(after(branch_grad, middle_up), mixed)
    mlp_term = jnp.concatenate([matmul_tn(normed_two, gate_up_grad), down_grad], 1)
    mlp_term = mlp_term.astype(low).reshape(2, 2, his, 2, block, wide)
    mlp_state = cross_start(pl, mlp_term)
    head_rows_grad = matmul_tn(after(logit_grad, mlp_term), chosen).astype(low)
    head_grad = lax.psum_scatter(head_rows_grad, "dp", scatter_dimension=1, tiled=True)
    middle_up = after(middle_up, mlp_term, head_rows_grad)
    middle_grad, attn_branch_grad, middle_gain_grad = move(
        functools.partial(middle_back_body, his),
        4,
        [
            ((picks, D), full, pltpu.VMEM),
            ((picks, D), low, pltpu.VMEM),
            ((1, D), full, pltpu.VMEM),
        ],
        [middle_up.reshape(his, 2, picks, D), middle, gain_float[1:2], ending_grad],
        his,
        scatter=(picks, D),
    )
    branch_line = line_gather(pl, attn_branch_grad)
    attended_grad = matmul(attn_branch_grad, out_full).astype(low)
    query_raw, kv_part = attend_rows_back(
        attended_grad, pick_tables, pick_pos, kv_all, queries, attended, log_total
    )
    query_share = shares(query_raw)
    (kv_raw,) = move(
        functools.partial(keys_back_body, his),
        5,
        [((tokens, 2 * kv_width), low, pltpu.VMEM)],
        [kv_part.reshape(his, 2, tokens, 2 * kv_width), *token_tables],
        his,
        scatter=(tokens, 2 * kv_width),
        own=(tokens, 2 * kv_width),
        own_type=full,
    )
    pick_up = matmul_nt(query_raw, qkv_full[:, :D])
    tok_up = matmul_nt(kv_raw, qkv_full[:, D:QKV])
    start_part, start_gain_grad = norm_back(
        start, gain_float[0], jnp.concatenate([tok_up, pick_up], 0)
    )
    start_grad = jnp.concatenate(
        [start_part[:tokens], start_part[tokens:] + middle_grad], 0
    ).astype(low)

    back_rows = lax.all_to_all(start_grad, "seq", split_axis=1, concat_axis=0, tiled=True)
    branch_line, pick_line, query_share = after((branch_line, pick_line, query_share), start_grad)
    query_term = jnp.concatenate(
        [matmul_tn(pick_line, query_share), matmul_tn(branch_line, attended_share)], 1
    )
    query_term = query_term.astype(low).reshape(2, 2, his, 2, block, query_term.shape[-1])
    query_state = cross_start(pl, query_term)
    gains_term = jnp.stack([start_gain_grad, middle_gain_grad[0], final_gain_grad[0]], 1)

    def by_core(rows, core):
        rows = rows.reshape(rows.shape[0], 2, 2, seqs * block)
        return pick(rows, core, 2).reshape(rows.shape[0], D // 2)

    def grid(rows):
        return rows.astype(low).reshape(2, his, 2, block, rows.shape[-1])

    def token_term(core):
        return jnp.concatenate(
            [
                matmul_tn(by_core(after(normed_tok, start_grad), core), kv_raw),
                jnp.pad(by_core(gains_term.T, core).T, ((0, 0), (0, 125))),
            ],
            1,
        )

    token_got = pl.send(token_term(1 - pl.c).astype(low), dc=1)
    token_keep = token_term(pl.c)
    other_squares = [jnp.sum(after(w, token_keep) ** 2) for w in (attn_w, mlp_w, head)]
    mlp_state = cross_next(pl, mlp_state, other_squares)
    back_rows = after(back_rows, mlp_state[:2], query_term)
    back_got = pl.send(back_rows, dy=1)
    token_sum = grid(token_keep + after(token_got, back_rows).astype(full))
    token_got = pl.send(pick(token_sum, 1 - pl.y, 0), dy=1)

    other = ids_all[:, 0] - (pl.dp ^ 1) * emb_n
    places_in = jnp.where(
        local[:, 0] < emb_n,
        local[:, 0],
        jnp.where((other >= 0) & (other < emb_n), other + emb_n, 2 * emb_n),
    )
    chip_grad = (
        jnp.zeros((2 * emb_n + 8, emb_m), full)
        .at[places_in[0]]
        .add(after(back_rows, token_sum).astype(full))
    )
    mlp_term = cross_end(pl, mlp_state, chip_grad)
    mlp_got = line_parts(pl, mlp_term)
    query_state = cross_next(pl, query_state, chip_grad)
    token_sum = pick(token_sum, pl.y, 0).astype(full) + after(token_got, chip_grad).astype(full)
    token_got = pl.send(pick(token_sum, 1 - pl.lo, 1).astype(low), dlo=1)
    back_got = after(back_got, mlp_term, query_state[:2], token_sum)
    chip_grad = chip_grad.at[places_in[1]].add(back_got.astype(full))
    emb_part = chip_grad[emb_n : 2 * emb_n].astype(low)
    emb_got = pl.send(emb_part, dc=1)
    query_term = cross_end(pl, query_state, emb_part)
    query_got = line_parts(pl, query_term)
    token_sum = pick(token_sum, pl.lo, 1) + after(token_got, emb_part).astype(full)
    token_parts = hi_sum_start(pl, token_sum)
    head_grad = after(head_grad, emb_part).astype(full)
    head_square = head_grad * head_grad + eps_square
    head_rows_sum = jnp.sum(head_square, 1)
    head_cols_sum = jnp.sum(head_square, 0)
    emb_grad = chip_grad[:emb_n] + after(emb_got, head_rows_sum).astype(full)
    emb_square = emb_grad * emb_grad + eps_square
    emb_rows = jnp.sum(emb_square, 1)
    mlp_grad, mlp_rows, mlp_cols = join_columns(line_place(pl, after(mlp_got, emb_rows)))
    mlp_row_new = decay_rate * mlp_row + (1.0 - decay_rate) * mlp_rows / (3 * FF)
    token_sum = hi_sum_end(token_parts, mlp_cols)
    query_all = line_place(pl, after(query_got, mlp_cols)).reshape(line, block, 2, D // line)
    query_all = jnp.transpose(query_all, (1, 2, 0, 3)).reshape(block, 2 * D).astype(full)
    attn_grad = jnp.concatenate(
        [query_all[:, :D], token_sum[:, : 2 * kv_width], query_all[:, D:]], 1
    )
    gains_grad = token_sum[:, 2 * kv_width : 2 * kv_width + 3].T
    attn_square = attn_grad * attn_grad + eps_square
    attn_row_new = decay_rate * attn_row + (1.0 - decay_rate) * jnp.mean(attn_square, 1)
    attn_weight_square, mlp_weight_square, head_weight_square = other_squares
    scalars = [
        loss_part,
        jnp.sum(attn_row_new),
        *other_squares,
        jnp.where(pl.s == 0, jnp.sum(emb_row), 0.0),
        emb_square_sum,
        jnp.where(pl.dp == 0, jnp.sum(head_row), 0.0),
        jnp.sum(gains * gains),
        jnp.sum(emb_rows),
        jnp.sum(mlp_row_new),
        jnp.sum(head_rows_sum),
    ]
    slot = jnp.arange(128, dtype=jnp.int32)
    scalars = sum(jnp.where(slot == i, value, 0.0) for i, value in enumerate(scalars))
    (
        emb_row_sum,
        head_col_sum,
        attn_cols_sum,
        mlp_cols_sum,
        totals,
        head_row_sum,
        emb_col_sum,
    ) = sum_statistics(
        his,
        (emb_rows, head_cols_sum),
        (jnp.sum(attn_square, 0), mlp_cols, scalars),
        (head_rows_sum, jnp.sum(emb_square, 0)),
    )
    mlp_row_total, head_row_total = totals[10], totals[11]

    attn_col_new = decay_rate * attn_col + (1.0 - decay_rate) * attn_cols_sum / D
    mlp_col_new = decay_rate * mlp_col + (1.0 - decay_rate) * mlp_cols_sum / D
    attn_update = attn_grad * lax.rsqrt(
        attn_row_new[:, None] * attn_col_new[None, :] / (totals[1] / D)
    )
    mlp_update = mlp_grad * lax.rsqrt(
        mlp_row_new[:, None] * mlp_col_new[None, :] / (mlp_row_total / D)
    )
    emb_row_new = decay_rate * emb_row + (1.0 - decay_rate) * emb_row_sum / D
    emb_col_new = decay_rate * emb_col + (1.0 - decay_rate) * emb_col_sum / VOCAB
    emb_mean = (decay_rate * totals[5] + (1.0 - decay_rate) * totals[9] / D) / VOCAB
    emb_update = emb_grad * lax.rsqrt(emb_row_new[:, None] * emb_col_new[None, :] / emb_mean)
    head_row_new = decay_rate * head_row + (1.0 - decay_rate) * head_row_sum / D
    head_col_new = decay_rate * head_col + (1.0 - decay_rate) * head_col_sum / VOCAB
    head_mean = (decay_rate * totals[7] + (1.0 - decay_rate) * head_row_total / D) / VOCAB
    head_update = head_grad * lax.rsqrt(head_row_new[:, None] * head_col_new[None, :] / head_mean)
    moment_new = decay_rate * gains_moment + (1.0 - decay_rate) * (
        gains_grad * gains_grad + eps_square
    )
    gains_update = gains_grad * lax.rsqrt(moment_new)
    attn_new = finish(attn_w, attn_update, totals[2], D * (QKV + D))
    mlp_new = finish(mlp_w, mlp_update, totals[3], D * 3 * FF)
    emb_new = finish(emb, emb_update, totals[6], VOCAB * D)
    head_new = finish(head, head_update, totals[4], VOCAB * D)
    gains_new = finish(gains, gains_update, totals[8], 3 * D)
    return (
        totals[0],
        count,
        emb_grad,
        emb_new,
        emb_row_new,
        emb_col_new,
        head_grad,
        head_new,
        head_row_new,
        head_col_new,
        attn_grad,
        attn_new,
        attn_row_new,
        attn_col_new,
        mlp_grad,
        mlp_new,
        mlp_row_new,
        mlp_col_new,
        gains_grad,
        moment_new,
        gains_new,
    )


def solution(mesh):
    return jax.shard_map(
        on_device,
        mesh=mesh,
        in_specs=(
            P("dp", None),
            P("dp", None),
            P("dp", None),
            P(),
            P("dp", "seq"),
            P("seq", "dp"),
            P(("dp", "seq"), None),
            P(("dp", "seq"), None),
            P(None, ("dp", "seq")),
            P("dp"),
            P("seq"),
            P("seq"),
            P("dp"),
            P(("dp", "seq")),
            P(),
            P(("dp", "seq")),
            P(),
            P(None, ("dp", "seq")),
        ),
        out_specs=(
            P(),
            P(),
            P("dp", "seq"),
            P("dp", "seq"),
            P("dp"),
            P("seq"),
            P("seq", "dp"),
            P("seq", "dp"),
            P("seq"),
            P("dp"),
            P(("dp", "seq"), None),
            P(("dp", "seq"), None),
            P(("dp", "seq")),
            P(),
            P(("dp", "seq"), None),
            P(("dp", "seq"), None),
            P(("dp", "seq")),
            P(),
            P(None, ("dp", "seq")),
            P(None, ("dp", "seq")),
            P(None, ("dp", "seq")),
        ),
        check_vma=False,
    )
```

```python
import functools
import math

import jax
import jax.numpy as jnp
from jax import lax
from jax.experimental import pallas
from jax.experimental.pallas import tpu as pltpu
from jax.sharding import PartitionSpec as P

D = 2048
HEADS = 32
KVH = 4
HD = 64
FF = 5632
VOCAB = 32000
QKV = 2560


eps_norm = 1e-05
eps_square = 1e-30
decay_rate = 0.5
learn_rate = 1.0
zloss_weight = 0.0001
orig_context = 2048.0
yarn_factor = 4.0
highest = lax.Precision.HIGHEST


def yarn_tables(places):
    halves = jnp.arange(HD // 2, dtype=jnp.float32)
    inverse = jnp.power(10000.0, -2.0 * halves / HD)
    ratio = orig_context * inverse / (2.0 * math.pi)
    ramp_part = jnp.clip((ratio - 1.0) / 31.0, 0.0, 1.0)
    frequency = inverse / yarn_factor * (1.0 - ramp_part) + inverse * ramp_part
    angles = places[:, None] * frequency[None, :]
    magnitude = 0.1 * math.log(yarn_factor) + 1.0
    return (jnp.cos(angles) * magnitude, jnp.sin(angles) * magnitude)


def rotate(values, cosine, sine):
    first = values[..., : HD // 2]
    second = values[..., HD // 2 :]
    cosine_row = cosine[:, None, :]
    sine_row = sine[:, None, :]
    return jnp.concatenate(
        [first * cosine_row - second * sine_row, second * cosine_row + first * sine_row], -1
    )


def unrotate(values, cosine, sine):
    first = values[..., : HD // 2]
    second = values[..., HD // 2 :]
    cosine_row = cosine[:, None, :]
    sine_row = sine[:, None, :]
    return jnp.concatenate(
        [first * cosine_row + second * sine_row, second * cosine_row - first * sine_row], -1
    )


def rms_norm(values, gain_row):
    return values * lax.rsqrt(jnp.mean(values * values, -1, keepdims=True) + eps_norm) * gain_row


def norm_back(values, gain_row, upstream):
    factor = lax.rsqrt(jnp.mean(values * values, -1, keepdims=True) + eps_norm)
    normed = values * factor
    gain_grad = jnp.sum(upstream * normed, 0)
    inner = upstream * gain_row
    return (factor * (inner - normed * jnp.mean(inner * normed, -1, keepdims=True)), gain_grad)


def matmul(left, right):
    return jnp.dot(left, right, preferred_element_type=jnp.float32)


def matmul_nt(left, right):
    return lax.dot_general(
        left, right, (((1,), (1,)), ((), ())), preferred_element_type=jnp.float32
    )


def matmul_tn(left, right):
    return lax.dot_general(
        left, right, (((0,), (0,)), ((), ())), preferred_element_type=jnp.float32
    )


def finish(weight, update, weight_square, entries):
    return weight - learn_rate * jnp.maximum(0.001, jnp.sqrt(weight_square / entries)) * update


low = jnp.bfloat16
full = jnp.float32


class Place:
    def __init__(self):
        self.seqs = lax.axis_size("seq")
        self.dps = lax.axis_size("dp")
        self.dp = lax.axis_index("dp")
        self.s = lax.axis_index("seq")
        self.his = self.seqs // 2
        self.y, self.c = self.dp // 2, self.dp % 2
        self.hi, self.lo = self.s // 2, self.s % 2

    def send(self, value, dy=0, dc=0, dlo=0, up=0):
        pairs = []
        for d in range(self.dps):
            for s in range(self.seqs):
                to_d = d ^ (2 * dy + dc)
                to_s = ((s // 2 + up) % self.his) * 2 + ((s % 2) ^ dlo)
                pairs.append((d * self.seqs + s, to_d * self.seqs + to_s))
        return lax.ppermute(value, ("dp", "seq"), pairs)

    def ways(self, names):
        steps = []
        for name in names:
            if name == "hi":
                bit = 1
                while bit < self.his:
                    steps.append(lambda value, bit=bit: self.swap_hi(value, bit))
                    bit *= 2
            else:
                steps.append(lambda value, name=name: self.send(value, **{name: 1}))
        return steps

    def swap_hi(self, value, bit):
        pairs = []
        for d in range(self.dps):
            for s in range(self.seqs):
                pairs.append((d * self.seqs + s, d * self.seqs + (s ^ (2 * bit))))
        return lax.ppermute(value, ("dp", "seq"), pairs)


def after(value, *events):
    return lax.optimization_barrier((value, *events))[0] if events else value


def pick(array, index, axis):
    return lax.dynamic_index_in_dim(array, index, axis, keepdims=False)


def put(array, block, index, axis):
    return lax.dynamic_update_slice_in_dim(array, jnp.expand_dims(block, axis), index, axis)


def line_pairs(pl, blocks):
    grid = blocks.reshape(2, pl.his, *blocks.shape[1:])
    return pick(grid, pl.c, 0), pl.send(pick(grid, 1 - pl.c, 0), dc=1)


def line_sends(pl, here, came):
    pairs = jnp.stack([here, came], 1)
    got = []
    for k in range(pl.his):
        pair = pick(pairs, (pl.hi + k) % pl.his, 0)
        got.append(pl.send(pair, up=k) if k else pair)
    return got


def place_body(*refs):
    pairs, out, sems = refs[:-2], refs[-2], refs[-1]
    n = len(pairs)
    dp, s = lax.axis_index("dp"), lax.axis_index("seq")
    c, hi = dp % 2, s // 2
    copies = []
    for k, pair in enumerate(pairs):
        for j, side in enumerate((c, 1 - c)):
            copies.append(
                pltpu.make_async_copy(
                    pair.at[j], out.at[side * n + lax.rem(hi + n - k, n)], sems.at[2 * k + j]
                )
            )
            copies[-1].start()
    for copy in copies:
        copy.wait()


def line_place(pl, got):
    count = len(got)
    shape = (2 * count, *got[0].shape[1:])
    return pallas.pallas_call(
        place_body,
        out_shape=jax.ShapeDtypeStruct(shape, got[0].dtype),
        in_specs=[pallas.BlockSpec(memory_space=pallas.ANY)] * count,
        out_specs=pallas.BlockSpec(memory_space=pltpu.VMEM),
        scratch_shapes=[pltpu.SemaphoreType.DMA((2 * count,))],
        cost_estimate=SMALL,
        name="line_place",
    )(*got)


def cross_start(pl, term):
    a, b = term[:, 0], term[:, 1]
    got_a = pl.send(pick(a, 1 - pl.y, 0), dy=1)
    got_b = pl.send(pick(b, 1 - pl.lo, 2), dlo=1)
    return a, b, got_a, got_b


def cross_next(pl, state, *work):
    a, b, got_a, got_b = state
    got_a, got_b = after((got_a, got_b), *work)
    a = pick(a, pl.y, 0).astype(full) + got_a.astype(full)
    b = pick(b, pl.lo, 2).astype(full) + got_b.astype(full)
    send_a = pick(a, 1 - pl.lo, 1).astype(low)
    send_b = pick(b, 1 - pl.y, 0).astype(low)
    keep = pick(a, pl.lo, 1), pick(b, pl.y, 0)
    return keep, (send_a, send_b)


def cross_send(pl, keep, sends):
    return *keep, pl.send(sends[0], dlo=1), pl.send(sends[1], dy=1)


def cross_end(pl, state, *work):
    a, b, got_a, got_b = state
    got_a, got_b = after((got_a, got_b), *work)
    a = (a + got_a.astype(full)).astype(low)
    b = (b + got_b.astype(full)).astype(low)
    return jnp.stack([a, b]).reshape(2 * pl.his, *a.shape[1:])


def split_kernel(line, part, in_ref, out_ref):
    for j in range(3):
        for t in range(line):
            at = (j * line + t) * part
            out_ref[t, :, j * part : (j + 1) * part] = in_ref[:, at : at + part].astype(low)


def split_columns(weight, line):
    rows, columns = weight.shape
    part = columns // (3 * line)
    return pallas.pallas_call(
        lambda *refs: split_kernel(line, part, *refs),
        out_shape=jax.ShapeDtypeStruct((line, rows, 3 * part), low),
        in_specs=[pallas.BlockSpec(memory_space=pltpu.VMEM)],
        out_specs=pallas.BlockSpec(memory_space=pltpu.VMEM),
        compiler_params=pltpu.CompilerParams(vmem_limit_bytes=40 * 2**20),
        name="split_columns",
    )(weight)


def join_kernel(line, part, in_ref, out_ref, rows_ref, columns_ref):
    total = jnp.zeros(rows_ref.shape, full)
    for j in range(3):
        for t in range(line):
            at = (j * line + t) * part
            block = in_ref[t, :, j * part : (j + 1) * part].astype(full)
            out_ref[:, at : at + part] = block
            square = block * block + eps_square
            columns_ref[:, at : at + part] = jnp.sum(square, 0, keepdims=True)
            total = total + jnp.sum(square, 1, keepdims=True)
    rows_ref[...] = total


def join_columns(blocks):
    line, rows, wide = blocks.shape
    part = wide // 3
    grad, row_sum, column_sum = pallas.pallas_call(
        lambda *refs: join_kernel(line, part, *refs),
        out_shape=(
            jax.ShapeDtypeStruct((rows, line * wide), full),
            jax.ShapeDtypeStruct((rows, 1), full),
            jax.ShapeDtypeStruct((1, line * wide), full),
        ),
        in_specs=[pallas.BlockSpec(memory_space=pltpu.VMEM)],
        out_specs=(pallas.BlockSpec(memory_space=pltpu.VMEM),) * 3,
        compiler_params=pltpu.CompilerParams(vmem_limit_bytes=40 * 2**20),
        name="join_columns",
    )(blocks)
    return grad, row_sum[:, 0], column_sum[0]


def halve(pl, part, mine, axis, **way):
    got = pl.send(pick(part, 1 - mine, axis).astype(low), **way)
    return pick(part, mine, axis).astype(full) + got.astype(full)


def hi_sum(pl, part, *work):
    total = pick(part, pl.hi, 0).astype(full)
    for k in range(1, pl.his):
        block = pick(part, (pl.hi + k) % pl.his, 0).astype(low)
        total = total + after(pl.send(block, up=k), *work).astype(full)
    return total


MESH = pallas.DeviceIdType.MESH
ROWS = 16
SMALL = pallas.CostEstimate(flops=1024, bytes_accessed=1024, transcendentals=0)


class Core:
    def __init__(self, his):
        dp, s = lax.axis_index("dp"), lax.axis_index("seq")
        self.his = his
        self.hi, self.lo, self.c = s // 2, s % 2, dp % 2
        self.side = {"c": self.c, "lo": self.lo}
        self.across = [
            (dp, lax.rem(self.hi + k, his) * 2 + self.lo) for k in range(his)
        ]
        self.ids = {
            "c": (dp + 1 - 2 * self.c, s),
            "lo": (dp, s + 1 - 2 * self.lo),
            "up": (dp, lax.rem(self.hi + 1, his) * 2 + self.lo),
            "down": (dp, lax.rem(self.hi + his - 1, his) * 2 + self.lo),
        }

    def meet(self, *names):
        others = [self.ids[name] for name in names if name != "line"]
        if "line" in names:
            others += self.across[1:]
        barrier = pltpu.get_barrier_semaphore()
        for other in others:
            pallas.semaphore_signal(barrier, inc=1, device_id=other, device_id_type=MESH)
        pallas.semaphore_wait(barrier, len(others))

    def copy(self, source, target, sems, at, name):
        return pltpu.make_async_remote_copy(
            src_ref=source,
            dst_ref=target,
            send_sem=sems[0].at[at],
            recv_sem=sems[1].at[at],
            device_id=self.ids[name] if isinstance(name, str) else self.across[name],
            device_id_type=MESH,
        )


def by_rows(n, step):
    def one(i, carry):
        step(pallas.ds(pallas.multiple_of(i * ROWS, ROWS), ROWS))
        return carry

    lax.fori_loop(0, n // ROWS, one, 0)


def kernel_scatter(core, name, part, total, held, side_sems, up_sems, beside=iter(())):
    his, side = core.his, core.side[name]
    side_out, side_in, up_out, up_in = held
    n = part.shape[2]
    over = []
    for j in range(his):
        h = lax.rem(core.hi + 2 * his - 1 - j, his)

        def cast(at, j=j, h=h):
            side_out[j, at, :] = part[h, 1 - side, at, :].astype(low)

        by_rows(n, cast)
        over.append(core.copy(side_out.at[j], side_in.at[j], side_sems, j, name))
        over[j].start()
    climb = []
    for j in range(his):
        h = lax.rem(core.hi + 2 * his - 1 - j, his)
        over[j].wait_recv()
        if j:
            climb[j - 1].wait_recv()

        def add(at, j=j, h=h):
            acc = part[h, side, at, :].astype(full) + side_in[j, at, :].astype(full)
            if j:
                acc = acc + up_in[j - 1, at, :].astype(full)
            if j < his - 1:
                up_out[j, at, :] = acc.astype(low)
            else:
                total[at, :] = acc

        by_rows(n, add)
        if j < his - 1:
            climb.append(core.copy(up_out.at[j], up_in.at[j], up_sems, j, "up"))
            climb[j].start()
        next(beside, None)
    return over + climb


def gather_steps(core, name, own, out, copies, sems, side_first=False):
    his, side = core.his, core.side[name]
    local_sem, side_sems, up_sems = sems[0], sems[1:3], sems[3:5]

    def slot(h):
        return out.at[side, h] if side_first else out.at[h, side]

    here = pltpu.make_async_copy(own, slot(core.hi), local_sem)
    here.start()
    over, climb = [], []
    for j in range(his):
        block = slot(lax.rem(core.hi + his - j, his))
        source = own if j == 0 else block
        if j:
            climb[j - 1].wait_recv()
        if j < his - 1:
            climb.append(core.copy(source, block, up_sems, j, "up"))
            climb[j].start()
        over.append(core.copy(source, block, side_sems, j, name))
        over[j].start()
        yield
    for copy in over:
        copy.wait_recv()
    here.wait()
    copies += over + climb


def kernel_gather(*args, **kwargs):
    for _ in gather_steps(*args, **kwargs):
        pass


def direct_start(core, own, out, sems):
    here = pltpu.make_async_copy(own, out.at[core.c, core.hi], sems[0])
    place = out.at[core.c, core.hi]
    climb = [core.copy(own, place, sems[3:5], k - 1, k) for k in range(1, core.his)]
    over = [core.copy(own, place, sems[1:3], 0, "c")]
    for copy in [here, *climb, *over]:
        copy.start()
    return here, climb, over


def direct_end(core, started, out, sems):
    here, climb, over = started
    order = sorted(range(1, core.his), key=lambda k: min(k, core.his - k))
    for k in order:
        climb[k - 1].wait_recv()
        block = out.at[core.c, lax.rem(core.hi + core.his - k, core.his)]
        over.append(core.copy(block, block, sems[1:3], k, "c"))
        over[-1].start()
    for copy in over:
        copy.wait_recv()
    here.wait()
    sent(climb + over)


def direct_scratch(his):
    dma = pltpu.SemaphoreType.DMA
    return [dma, dma((his,)), dma((his,)), dma((his - 1,)), dma((his - 1,))]


def kernel_swap_start(core, blocks, came, side_sems):
    his = core.his
    over = core.copy(
        blocks.at[pallas.ds((1 - core.c) * his, his)], came, side_sems, 0, "c"
    )
    over.start()
    return over


def kernel_swap_end(core, over, blocks, came, out, local_sems, up_sems):
    his, c, hi = core.his, core.c, core.hi
    mine, theirs = c * his + hi, (1 - c) * his + hi
    here = [pltpu.make_async_copy(blocks.at[mine], out.at[mine], local_sems.at[0])]
    climb = []
    for k in range(1, his):
        to = lax.rem(hi + k, his)
        climb.append(core.copy(blocks.at[c * his + to], out.at[mine], up_sems, 2 * k - 2, k))
    over.wait_recv()
    here.append(pltpu.make_async_copy(came.at[hi], out.at[theirs], local_sems.at[1]))
    for k in range(1, his):
        to = lax.rem(hi + k, his)
        climb.append(core.copy(came.at[to], out.at[theirs], up_sems, 2 * k - 1, k))
    for copy in here + climb:
        copy.start()
    return here, [over] + climb


def swap_done(here, copies):
    for copy in here:
        copy.wait()
    for copy in copies[1:]:
        copy.wait_recv()


def sent(copies):
    for copy in copies:
        copy.wait_send()


def norm_rows(values, gain):
    return values * lax.rsqrt(jnp.mean(values * values, -1, keepdims=True) + eps_norm) * gain


def norm_rows_back(values, gain, upstream):
    factor = lax.rsqrt(jnp.mean(values * values, -1, keepdims=True) + eps_norm)
    normed = values * factor
    inner = upstream * gain
    back = factor * (inner - normed * jnp.mean(inner * normed, -1, keepdims=True))
    return back, jnp.sum(upstream * normed, 0, keepdims=True)


def norm_gather_body(his, values, gain, blocks, out, swapped, came, own, *sems):
    core = Core(his)
    by_rows(
        values.shape[0],
        lambda at: own.__setitem__(
            (at, slice(None)), norm_rows(values[at, :], gain[...]).astype(low)
        ),
    )
    core.meet("c", "line")
    over = kernel_swap_start(core, blocks, came, sems[1:3])
    copies = []
    kernel_gather(core, "c", own, out, copies, sems[5:10])
    here, more = kernel_swap_end(core, over, blocks, came, swapped, sems[0], sems[3:5])
    swap_done(here, more)
    sent(copies + more)


def turn_keys(source, cosine, sine, target):
    width = KVH * HD
    for at in range(0, width, 2 * HD):
        pair = turned(source[:, at : at + 2 * HD], cosine, sine)
        target[:, at : at + 2 * HD] = pair.astype(low)
    target[:, width:] = source[:, width:].astype(low)


def keys_body(his, projected, cosine, sine, out, own, *sems):
    core = Core(his)
    turn_keys(projected, cosine[...], sine[...], own)
    core.meet("lo", "up", "down")
    copies = []
    kernel_gather(core, "lo", own, out, copies, sems)
    sent(copies)


def keys_back_body(
    his, part, cosine, sine, blocks, out, swapped, came, total, *rest
):
    swap_sems, held, sems = rest[:5], rest[5:9], rest[9:13]
    core = Core(his)
    core.meet("c", "lo", "line")
    over = kernel_swap_start(core, blocks, came, swap_sems[1:3])
    copies = []
    copies += kernel_scatter(core, "lo", part, total, held, sems[0:2], sems[2:4])
    here, more = kernel_swap_end(core, over, blocks, came, swapped, swap_sems[0], swap_sems[3:5])
    turn_keys(total, cosine[...], -sine[...], out)
    swap_done(here, more)
    sent(copies + more)


def layer_body(his, blocks, tokens, grad, gains, rows, columns, swapped, came, out_low, in_low, *sems):
    core = Core(his)
    wide = blocks.shape[2] // 2
    side, keys = 2 * his, 2 * KVH * HD
    core.meet("c", "line")
    over = kernel_swap_start(core, blocks, came, sems[1:3])
    climb = []
    for k in range(1, his):
        to = lax.rem(core.hi + k, his)
        out_low[k - 1] = tokens[to].astype(low)
        climb.append(core.copy(out_low.at[k - 1], in_low.at[k - 1], sems[5:7], k - 1, k))
        climb[-1].start()
    here, more = kernel_swap_end(core, over, blocks, came, swapped, sems[0], sems[3:5])
    total = tokens[core.hi]
    for k, copy in enumerate(climb):
        copy.wait_recv()
        total = total + in_low[k].astype(full)
    gains[...] = total[:, keys:]
    row_sum = jnp.zeros(rows.shape, full)
    pieces = [(D, total[:, :keys])]
    swap_done(here, more)
    for t in range(side):
        pieces.append((t * wide, swapped[t, :, :wide].astype(full)))
        pieces.append((QKV + t * wide, swapped[t, :, wide:].astype(full)))
    for at, piece in pieces:
        till = at + piece.shape[1]
        grad[:, at:till] = piece
        square = piece * piece + eps_square
        columns[:, at:till] = jnp.sum(square, 0, keepdims=True)
        row_sum = row_sum + jnp.sum(square, 1, keepdims=True)
    rows[...] = row_sum
    sent(climb + more)


def layer_gradient(his, blocks, tokens):
    line, rows, columns = blocks.shape
    extra = tokens.shape[2] - 2 * KVH * HD
    dma = pltpu.SemaphoreType.DMA
    return pallas.pallas_call(
        functools.partial(layer_body, his),
        out_shape=(
            jax.ShapeDtypeStruct((rows, QKV + D), full),
            jax.ShapeDtypeStruct((rows, extra), full),
            jax.ShapeDtypeStruct((rows, 1), full),
            jax.ShapeDtypeStruct((1, QKV + D), full),
        ),
        in_specs=[pallas.BlockSpec(memory_space=pltpu.VMEM)] * 2,
        out_specs=(pallas.BlockSpec(memory_space=pltpu.VMEM),) * 4,
        scratch_shapes=[
            pltpu.VMEM(blocks.shape, low),
            pltpu.VMEM((his, rows, columns), low),
            pltpu.VMEM((his - 1, *tokens.shape[1:]), low),
            pltpu.VMEM((his - 1, *tokens.shape[1:]), low),
            dma((2,)),
            *[dma((count,)) for count in (1, 1, 2 * his - 2, 2 * his - 2, his - 1, his - 1)],
        ],
        cost_estimate=SMALL,
        compiler_params=pltpu.CompilerParams(
            collective_id=7, has_side_effects=True, vmem_limit_bytes=32 * 2**20
        ),
        name="layer_gradient",
    )(blocks, tokens)


def ending_body(his, part, middle, gain, ending, chosen, own, *rest):
    held, sems = rest[:4], rest[4:]
    core = Core(his)
    core.meet("c", "lo", "up", "down")
    copies = kernel_scatter(core, "c", part, ending, held, sems[0:2], sems[2:4])

    def finish_rows(at):
        values = ending[at, :] + middle[at, :]
        ending[at, :] = values
        own[at, :] = norm_rows(values, gain[...]).astype(low)

    by_rows(middle.shape[0], finish_rows)
    kernel_gather(core, "lo", own, chosen, copies, sems[4:9])
    sent(copies)


def ending_back_body(his, part, ending, gain, grad, gain_grad, branch, own, *rest):
    held, sems = rest[:4], rest[4:]
    core = Core(his)
    core.meet("c", "lo", "up", "down")
    copies = kernel_scatter(core, "lo", part, grad, held, sems[0:2], sems[2:4])
    gain_grad[...] = jnp.zeros(gain_grad.shape, full)

    def back_rows(at):
        back, gained = norm_rows_back(ending[at, :], gain[...], grad[at, :])
        grad[at, :] = back
        own[at, :] = back.astype(low)
        gain_grad[...] += gained

    by_rows(ending.shape[0], back_rows)
    kernel_gather(core, "c", own, branch, copies, sems[4:9])
    sent(copies)


def middle_back_body(his, part, middle, gain, ending_grad, grad, grad_low, gain_grad, *rest):
    held, sems = rest[:4], rest[4:]
    core = Core(his)
    core.meet("c", "up", "down")
    copies = kernel_scatter(core, "c", part, grad, held, sems[0:2], sems[2:4])
    gain_grad[...] = jnp.zeros(gain_grad.shape, full)

    def back_rows(at):
        back, gained = norm_rows_back(middle[at, :], gain[...], grad[at, :])
        back = back + ending_grad[at, :]
        grad[at, :] = back
        grad_low[at, :] = back.astype(low)
        gain_grad[...] += gained

    by_rows(middle.shape[0], back_rows)
    sent(copies)


def move(body, collective_id, outs, args, his, scatter=None, own=None, own_type=low, gathers=0, swap=None):
    dma = pltpu.SemaphoreType.DMA
    scratch = []
    if swap:
        scratch.append(pltpu.VMEM(swap, low))
    if own:
        scratch.append(pltpu.VMEM(own, own_type))
    if swap:
        scratch += [dma((2,))]
        scratch += [dma((count,)) for count in (1, 1, 2 * his - 2, 2 * his - 2)]
    if scatter:
        scratch += [pltpu.VMEM((count, *scatter), low) for count in (his, his, his - 1, his - 1)]
        scratch += [dma((his,)), dma((his,)), dma((his - 1,)), dma((his - 1,))]
    for _ in range(gathers):
        scratch += [dma, dma((his,)), dma((his,)), dma((his - 1,)), dma((his - 1,))]
    return pallas.pallas_call(
        body,
        out_shape=tuple(jax.ShapeDtypeStruct(shape, dtype) for shape, dtype, _ in outs),
        in_specs=[pallas.BlockSpec(memory_space=pltpu.VMEM)] * len(args),
        out_specs=tuple(pallas.BlockSpec(memory_space=memory) for _, _, memory in outs),
        scratch_shapes=scratch,
        cost_estimate=SMALL,
        compiler_params=pltpu.CompilerParams(
            collective_id=collective_id,
            has_side_effects=True,
            vmem_limit_bytes=48 * 2**20,
        ),
    )(*args)


HALF = HD // 2
STACK = 4


def turn_tables(cosine, sine):
    return jnp.concatenate([cosine] * 4, 1), jnp.concatenate([-sine, sine] * 2, 1)


def turned(values, cosine, sine):
    lane = lax.broadcasted_iota(jnp.int32, values.shape, 1) % HD
    other = jnp.where(
        lane < HALF, pltpu.roll(values, 2 * HD - HALF, 1), pltpu.roll(values, HALF, 1)
    )
    return values * cosine + other * sine


def heads_loop(loops, step):
    def one(t, carry):
        step(t)
        return carry

    lax.fori_loop(0, loops, one, 0)


def split_kv(kv, k_held, v_held):
    width = KVH * HD
    for g in range(KVH):
        k_held[g] = kv[:, g * HD : (g + 1) * HD]
        v_held[g] = kv[:, width + g * HD : width + (g + 1) * HD]


def allowed_keys(places, keys):
    places = jnp.concatenate([places] * STACK, 0)
    return lax.broadcasted_iota(jnp.int32, (places.shape[0], keys), 1) <= places


def dot_nt(left, right):
    return lax.dot_general(
        left, right, (((1,), (1,)), ((), ())), preferred_element_type=jnp.float32
    )


def attend_body(
    his, raw, cosine, sine, places, kv, own, turned_out, out_low, held_out, logs, line_out, k_held, v_held, *sems
):
    picks, keys = raw.shape[0], kv.shape[0]
    core = Core(his)
    core.meet("c", "line")
    started = direct_start(core, own, line_out, sems)
    split_kv(kv, k_held, v_held)
    for j in range(D // (2 * HD)):
        pair = turned(raw[:, 2 * HD * j : 2 * HD * (j + 1)], cosine[...], sine[...]).astype(low)
        for i in range(2):
            t, at = divmod(2 * j + i, STACK)
            turned_out[t, at * picks : (at + 1) * picks, :] = pair[:, i * HD : (i + 1) * HD]
    allowed = allowed_keys(places[...], keys)

    def step(t):
        g = t // (HEADS // KVH // STACK)
        scores = dot_nt(turned_out[t], k_held[g]) * HD ** (-0.5)
        scores = jnp.where(allowed, scores, -1e30)
        high = jnp.max(scores, 1, keepdims=True)
        weights = jnp.exp(scores - high)
        total = jnp.sum(weights, 1, keepdims=True)
        result = jnp.dot(weights.astype(low), v_held[g], preferred_element_type=full)
        held_out[t] = result / total
        logs[t] = jnp.broadcast_to(high + jnp.log(total), (STACK * picks, 2 * HD))

    heads_loop(HEADS // STACK, step)
    for j in range(D // (2 * HD)):
        pair = []
        for i in range(2):
            t, at = divmod(2 * j + i, STACK)
            pair.append(held_out[t, at * picks : (at + 1) * picks, :])
        pair = jnp.concatenate(pair, 1)
        out_low[:, 2 * HD * j : 2 * HD * (j + 1)] = pair.astype(low)
    direct_end(core, started, line_out, sems)


def attend_rows(his, raw, tables, places, kv, own):
    picks, keys = raw.shape[0], kv.shape[0]
    stacks, rows = HEADS // STACK, STACK * picks
    return pallas.pallas_call(
        functools.partial(attend_body, his),
        out_shape=(
            jax.ShapeDtypeStruct((stacks, rows, HD), low),
            jax.ShapeDtypeStruct((picks, D), low),
            jax.ShapeDtypeStruct((stacks, rows, HD), full),
            jax.ShapeDtypeStruct((stacks, rows, 2 * HD), full),
            jax.ShapeDtypeStruct((2, his, *own.shape), low),
        ),
        in_specs=[pallas.BlockSpec(memory_space=pltpu.VMEM)] * 6,
        out_specs=(pallas.BlockSpec(memory_space=pltpu.VMEM),) * 4
        + (pallas.BlockSpec(memory_space=pallas.ANY),),
        scratch_shapes=[pltpu.VMEM((KVH, keys, HD), low)] * 2 + direct_scratch(his),
        compiler_params=pltpu.CompilerParams(
            collective_id=9, has_side_effects=True, vmem_limit_bytes=56 * 2**20
        ),
        cost_estimate=SMALL,
        name="attend",
    )(raw, *tables, places[:, None], kv, own)


def attend_back_body(
    his, grad, cosine, sine, places, kv, queries, held_out, logs, own, raw, kv_grad, line_out, k_held, v_held,
    grad_held, query_held, *rest
):
    picks, keys = grad.shape[0], kv.shape[0]
    sems, sums = rest[:5], rest[5:]
    core = Core(his)
    core.meet("c", "line")
    started = direct_start(core, own, line_out, sems)
    scale = HD ** (-0.5)
    split_kv(kv, k_held, v_held)
    for j in range(D // (2 * HD)):
        pair = grad[:, 2 * HD * j : 2 * HD * (j + 1)]
        for i in range(2):
            t, at = divmod(2 * j + i, STACK)
            grad_held[t, at * picks : (at + 1) * picks, :] = pair[:, i * HD : (i + 1) * HD]
    allowed = allowed_keys(places[...], keys)
    total = sums[0] if sums else kv_grad
    total[...] = jnp.zeros(total.shape, full)

    def step(t):
        g = t // (HEADS // KVH // STACK)
        query, up = queries[t], grad_held[t]
        delta = jnp.sum(up.astype(full) * held_out[t], 1, keepdims=True)
        scores = dot_nt(query, k_held[g]) * scale
        weights = jnp.where(allowed, jnp.exp(scores - logs[t][:, :1]), 0.0)
        weight_grad = dot_nt(up, v_held[g])
        score_grad = (weights * (weight_grad - delta)).astype(low)
        query_held[t] = jnp.dot(score_grad, k_held[g], preferred_element_type=full) * scale
        total[g] += matmul_tn(query, score_grad) * scale
        total[KVH + g] += matmul_tn(up, weights.astype(low))

    heads_loop(HEADS // STACK, step)
    for j in range(D // (2 * HD)):
        pair = []
        for i in range(2):
            t, at = divmod(2 * j + i, STACK)
            pair.append(query_held[t, at * picks : (at + 1) * picks, :])
        pair = jnp.concatenate(pair, 1)
        raw[:, 2 * HD * j : 2 * HD * (j + 1)] = turned(pair, cosine[...], -sine[...]).astype(low)
    if sums:
        for g in range(0, 2 * KVH, 2):
            both = jnp.concatenate([total[g], total[g + 1]], 0)
            kv_grad[:, g * HD : (g + 2) * HD] = both.T
    direct_end(core, started, line_out, sems)


def attend_rows_back(his, grad, tables, places, kv, queries, held_out, logs, own):
    picks, keys = grad.shape[0], kv.shape[0]
    stacks, rows = HEADS // STACK, STACK * picks
    outside = keys > 4096
    by_head = (2 * KVH, HD, keys)
    raw, kv_grad, line_out = pallas.pallas_call(
        functools.partial(attend_back_body, his),
        out_shape=(
            jax.ShapeDtypeStruct((picks, D), low),
            jax.ShapeDtypeStruct(by_head if outside else (keys, 2 * KVH * HD), full),
            jax.ShapeDtypeStruct((2, his, *own.shape), low),
        ),
        in_specs=[pallas.BlockSpec(memory_space=pltpu.VMEM)] * 9,
        out_specs=(pallas.BlockSpec(memory_space=pltpu.VMEM),) * 2
        + (pallas.BlockSpec(memory_space=pallas.ANY),),
        scratch_shapes=[
            pltpu.VMEM((KVH, keys, HD), low),
            pltpu.VMEM((KVH, keys, HD), low),
            pltpu.VMEM((stacks, rows, HD), low),
            pltpu.VMEM((stacks, rows, HD), full),
            *direct_scratch(his),
        ]
        + ([] if outside else [pltpu.VMEM(by_head, full)]),
        compiler_params=pltpu.CompilerParams(
            collective_id=10, has_side_effects=True, vmem_limit_bytes=58 * 2**20
        ),
        cost_estimate=SMALL,
        name="attend_back",
    )(grad, *tables, places[:, None], kv, queries, held_out, logs, own)
    kv_grad = kv_grad.reshape(2 * KVH * HD, keys).T if outside else kv_grad
    return raw, kv_grad, line_out


def weights_body(
    his, blocks, whole, came, local_sems, core_sems, core_sems_in, up_sems, up_sems_in, x_sems, x_sems_in, y_sems,
    y_sems_in
):
    core = Core(his)
    dp, s = lax.axis_index("dp"), lax.axis_index("seq")
    y, c, hi, lo = dp // 2, core.c, core.hi, core.lo
    core.ids["y"] = (dp + 2 - 4 * y, s)
    core.meet("c", "y", "lo", "line")
    swap = core.copy(blocks.at[pallas.ds((1 - c) * his, his)], came, (core_sems, core_sems_in), 0, "c")
    swap.start()
    here, climb, over_x, over_y = [], {}, {}, {}

    def cross(source, slot, at):
        over_x[at] = core.copy(source, slot, (x_sems, x_sems_in), at, "lo")
        over_y[at] = core.copy(source, slot, (y_sems, y_sems_in), at, "y")
        over_x[at].start()
        over_y[at].start()

    def leave(source, j, side):
        slot = whole.at[y, side, hi, lo]
        here.append(pltpu.make_async_copy(source(hi), slot, local_sems.at[j]))
        here[-1].start()
        for k in range(1, his):
            climb[2 * k + j] = core.copy(
                source(lax.rem(hi + k, his)), slot, (up_sems, up_sems_in), 2 * k + j - 2, k
            )
            climb[2 * k + j].start()
        cross(source(hi), slot, j)

    leave(lambda h: blocks.at[c * his + h], 0, c)
    swap.wait_recv()
    leave(lambda h: came.at[h], 1, 1 - c)
    for k in sorted(range(1, his), key=lambda k: min(k, his - k)):
        h = lax.rem(hi + his - k, his)
        for j, side in enumerate((c, 1 - c)):
            climb[2 * k + j].wait_recv()
            slot = whole.at[y, side, h, lo]
            cross(slot, slot, 2 * k + j)
    for copy in [*over_x.values(), *over_y.values()]:
        copy.wait_recv()
    for copy in here:
        copy.wait()
    sent([swap, *climb.values(), *over_x.values(), *over_y.values()])


def gather_weights(his, blocks):
    line, block, wide = blocks.shape
    dma = pltpu.SemaphoreType.DMA
    counts = (1, 2 * his - 2, 2 * his, 2 * his)
    return pallas.pallas_call(
        functools.partial(weights_body, his),
        out_shape=jax.ShapeDtypeStruct((2, 2, his, 2, block, wide), low),
        in_specs=[pallas.BlockSpec(memory_space=pltpu.VMEM)],
        out_specs=pallas.BlockSpec(memory_space=pallas.ANY),
        scratch_shapes=[
            pltpu.VMEM((his, block, wide), low),
            dma((2,)),
            *[dma((count,)) for count in counts for _ in range(2)],
        ],
        cost_estimate=SMALL,
        compiler_params=pltpu.CompilerParams(
            collective_id=8, has_side_effects=True, vmem_limit_bytes=32 * 2**20
        ),
        name="gather_weights",
    )(blocks)


def rows_body(
    his, far, near, whole, start, far_a, far_b, got, looked, local_sem, y_sems, y_sems_in, seq_sems, seq_sems_in,
    a_sems, a_sems_in, b_sems, b_sems_in
):
    core = Core(his)
    dp, s = lax.axis_index("dp"), lax.axis_index("seq")
    y, seqs = dp // 2, 2 * his
    core.ids["y"] = (dp + 2 - 4 * y, s)
    for i in range(1, seqs):
        core.ids[f"seq{i}"] = (dp, lax.rem(s + i, seqs))
    core.meet("y", "lo", *(f"seq{i}" for i in range(1, seqs)))
    over, spread, carried = [], [], []
    for i in range(seqs):
        to = lax.rem(s + i, seqs)
        over.append(core.copy(far.at[to], got.at[to], (y_sems, y_sems_in), i, "y"))
        over[i].start()
    for h in range(his):
        carried.append(
            core.copy(whole.at[y, 0, h, 1 - core.lo], far_a.at[h], (a_sems, a_sems_in), h, "y")
        )
        carried.append(
            core.copy(whole.at[1 - y, 1, h, core.lo], far_b.at[h], (b_sems, b_sems_in), h, "lo")
        )
    for copy in carried:
        copy.start()
    here = None
    for i in [*range(1, seqs), 0]:
        to = lax.rem(s + i, seqs)
        over[i].wait_recv()

        def add(at, to=to):
            looked[to, at, :] = near[to, at, :] + got[to, at, :]

        by_rows(near.shape[1], add)
        if i:
            spread.append(
                core.copy(looked.at[to], start.at[s], (seq_sems, seq_sems_in), i - 1, f"seq{i}")
            )
            spread[-1].start()
        else:
            here = pltpu.make_async_copy(looked.at[s], start.at[s], local_sem)
            here.start()
    for copy in spread + carried:
        copy.wait_recv()
    here.wait()
    sent(over + spread + carried)


def gather_rows(his, far, near, whole):
    seqs = 2 * his
    rows, columns = far.shape[0] // seqs, far.shape[1]
    far, near = (part.reshape(seqs, rows, columns) for part in (far, near))
    dma = pltpu.SemaphoreType.DMA
    start, far_a, far_b = pallas.pallas_call(
        functools.partial(rows_body, his),
        out_shape=(
            jax.ShapeDtypeStruct((seqs, rows, columns), low),
            *[jax.ShapeDtypeStruct((his, *whole.shape[4:]), low)] * 2,
        ),
        in_specs=[pallas.BlockSpec(memory_space=pltpu.VMEM)] * 2
        + [pallas.BlockSpec(memory_space=pallas.ANY)],
        out_specs=(pallas.BlockSpec(memory_space=pallas.ANY),) * 3,
        scratch_shapes=[
            pltpu.VMEM((seqs, rows, columns), low),
            pltpu.VMEM((seqs, rows, columns), low),
            dma,
            *[dma((count,)) for count in (seqs, seqs, seqs - 1, seqs - 1, his, his, his, his)],
        ],
        cost_estimate=SMALL,
        compiler_params=pltpu.CompilerParams(
            collective_id=11, has_side_effects=True, vmem_limit_bytes=32 * 2**20
        ),
        name="gather_rows",
    )(far, near, whole)
    start = jnp.transpose(start, (1, 0, 2)).reshape(rows, seqs * columns).astype(full)
    return start, far_a, far_b


def sum_body(his, rows, packed, out, bufs, got, send_sems, recv_sems):
    core = Core(his)
    dp, s = lax.axis_index("dp"), lax.axis_index("seq")
    ways = [("lo", 0)]
    bit = 1
    while bit < his:
        up = lax.rem(core.hi // bit, 2)
        core.ids[f"hi{bit}"] = (dp, s + 2 * bit * (1 - 2 * up))
        ways.append((f"hi{bit}", 0))
        bit *= 2
    y = dp // 2
    core.ids["y"] = (dp + 2 * (1 - 2 * y), s)
    ways += [("c", 1), ("y", 1)]
    core.meet(*(name for name, _ in ways))
    bufs[0] = packed[...]
    copies = []
    for j, (name, over_dp) in enumerate(ways):
        first = rows[0] if over_dp else 0
        last = rows[0] + rows[1] + (rows[2] if over_dp else 0)
        copy = core.copy(
            bufs.at[j, first:last], got.at[j, first:last], (send_sems, recv_sems), j, name
        )
        copy.start()
        copies.append(copy)
        copy.wait_recv()
        bufs[j + 1] = bufs[j]
        bufs[j + 1, first:last] = bufs[j, first:last] + got[j, first:last]
    out[...] = bufs[len(ways)]
    sent(copies)


def padded(parts):
    return [
        jnp.pad(part, (0, -part.shape[0] % 1024)).reshape(-1, 128) for part in parts
    ]


def sum_statistics(his, over_seq, over_all, over_dp):
    groups = [padded(parts) for parts in (over_seq, over_all, over_dp)]
    rows = tuple(sum(part.shape[0] for part in group) for group in groups)
    steps = 3 + his.bit_length() - 1
    total = sum(rows)
    dma = pltpu.SemaphoreType.DMA
    out = pallas.pallas_call(
        functools.partial(sum_body, his, rows),
        out_shape=jax.ShapeDtypeStruct((total, 128), full),
        in_specs=[pallas.BlockSpec(memory_space=pltpu.VMEM)],
        out_specs=pallas.BlockSpec(memory_space=pltpu.VMEM),
        scratch_shapes=[
            pltpu.VMEM((steps + 1, total, 128), full),
            pltpu.VMEM((steps, total, 128), full),
            dma((steps,)),
            dma((steps,)),
        ],
        compiler_params=pltpu.CompilerParams(
            collective_id=6, has_side_effects=True, vmem_limit_bytes=32 * 2**20
        ),
        name="sum_statistics",
    )(jnp.concatenate([part for group in groups for part in group], 0))
    results, at = [], 0
    for parts, group in zip((over_seq, over_all, over_dp), groups):
        for part, block in zip(parts, group):
            results.append(out[at : at + block.shape[0]].reshape(-1)[: part.shape[0]])
            at += block.shape[0]
    return results


def on_device(
    tok_ids,
    targets,
    positions,
    answer_mask,
    emb,
    head,
    attn_w,
    mlp_w,
    gains,
    emb_row,
    emb_col,
    head_row,
    head_col,
    attn_row,
    attn_col,
    mlp_row,
    mlp_col,
    gains_moment,
):
    pl = Place()
    seqs, his = pl.seqs, pl.his
    tokens = tok_ids.shape[1] // seqs
    picks = targets.shape[1] // seqs
    group = HEADS // KVH
    kv_width = KVH * HD
    block = D // (pl.dps * seqs)
    emb_n, emb_m = emb.shape
    line = 2 * his
    part = FF // line
    wide = 3 * part

    def swap_rows(rows, **way):
        return pl.send(rows.astype(low), **way)

    mlp_whole = gather_weights(his, split_columns(mlp_w, line))
    ids = jnp.concatenate([tok_ids.reshape(seqs, tokens), targets.reshape(seqs, picks)], 1)
    ids = ids.reshape(seqs * (tokens + picks))
    def look(wanted, *work):
        at = after(wanted, *work) - pl.dp * emb_n
        rows = jnp.take(emb, jnp.clip(at, 0, emb_n - 1), axis=0, mode="clip")
        return jnp.where(((at >= 0) & (at < emb_n))[:, None], rows, 0.0).astype(low)

    ids_y = pl.send(ids, dy=1)
    ids_c, ids_yc = pl.send(ids, dc=1), pl.send(ids, dy=1, dc=1)
    near_own = look(ids, mlp_whole)
    ids_c, ids_y, ids_yc = after((ids_c, ids_y, ids_yc), near_own)
    far_other = look(ids_yc)
    far_got = pl.send(far_other, dc=1)
    near_other = look(ids_c, far_other)
    near_got = pl.send(near_other, dc=1)
    far_own = look(ids_y, near_other)
    far_sum = far_own + after(far_got, far_own)
    near_sum = near_own + after(near_got, far_own)

    kv_block = jnp.concatenate(
        [attn_w[:, D:QKV], jnp.pad(gains.T, ((0, 0), (0, 125)))], 1
    ).astype(low)
    kv_full = lax.all_gather(kv_block, ("dp", "seq"), axis=0, tiled=True)
    gain_float = kv_full[:, 2 * kv_width : 2 * kv_width + 3].astype(full).T
    kv_full = kv_full[:, : 2 * kv_width]
    rest_low = after(attn_w, mlp_whole).astype(low)
    rest_full = lax.all_gather(
        jnp.concatenate([rest_low[:, :D], rest_low[:, QKV:]], 1), ("dp", "seq"), axis=0, tiled=True
    )
    query_full, out_full = rest_full[:, :D], rest_full[:, D:]
    start, far_a, far_b = gather_rows(his, far_sum, near_sum, mlp_whole)
    head_low = after(head, start).astype(low)
    emb_square_sum = jnp.sum(after(emb, start) ** 2)

    token_pos = pl.s * tokens + jnp.arange(tokens, dtype=jnp.int32)
    pick_pos = lax.dynamic_slice_in_dim(positions[0], pl.s * picks, picks)
    token_tables = turn_tables(*yarn_tables(token_pos.astype(full)))
    pick_tables = turn_tables(*yarn_tables(pick_pos.astype(full)))
    head_rows = lax.all_gather(after(head_low, start), "dp", axis=1, tiled=True)
    normed = rms_norm(start, gain_float[0]).astype(low)
    normed_tok, normed_pick = normed[:tokens], normed[tokens:]
    start_pick = start[tokens:]
    projected = matmul(normed_tok, kv_full)
    (kv_all,) = move(
        functools.partial(keys_body, his),
        0,
        [((his, 2, tokens, 2 * kv_width), low, pallas.ANY)],
        [projected, *token_tables],
        his,
        own=(tokens, 2 * kv_width),
        gathers=1,
    )
    kv_all = kv_all.reshape(seqs * tokens, 2 * kv_width)
    raw = matmul(normed_pick, query_full)
    queries, attended_low, attended, log_total, pick_line = attend_rows(
        his, raw, pick_tables, pick_pos, kv_all, normed_pick
    )
    for c, block_far in enumerate((far_a, far_b)):
        mlp_whole = lax.dynamic_update_slice(
            mlp_whole, block_far[None, None, :, None], (1 - pl.y, c, 0, 1 - pl.lo, 0, 0)
        )
    mlp_full = mlp_whole.reshape(D, wide)

    def shares(rows):
        return jnp.transpose(rows.reshape(picks, line, D // line), (1, 0, 2))

    middle = start_pick + matmul_nt(attended_low, out_full)
    normed_two, attended_share = move(
        functools.partial(norm_gather_body, his),
        1,
        [
            ((his, 2, picks, D), low, pallas.ANY),
            ((line, picks, D // line), low, pltpu.VMEM),
        ],
        [middle, gain_float[1:2], shares(attended_low)],
        his,
        own=(picks, D),
        gathers=1,
        swap=(his, picks, D // line),
    )
    normed_two = normed_two.reshape(line * picks, D)
    gate_up = matmul(normed_two, mlp_full[:, : 2 * part])
    gate = gate_up[:, :part]
    upward = gate_up[:, part:]
    mixed = (jax.nn.silu(gate) * upward).astype(low)
    down = matmul_nt(mixed, mlp_full[:, 2 * part :])
    ending, chosen = move(
        functools.partial(ending_body, his),
        2,
        [((picks, D), full, pltpu.VMEM), ((his, 2, picks, D), low, pallas.ANY)],
        [down.reshape(his, 2, picks, D), middle, gain_float[2:3]],
        his,
        scatter=(picks, D),
        own=(picks, D),
        gathers=1,
    )
    chosen = chosen.reshape(seqs * picks, D)
    logits = matmul_nt(chosen, head_rows)
    vocab_part = head_rows.shape[0]
    target_hit = (
        targets[0][:, None]
        == pl.s * vocab_part + jnp.arange(vocab_part, dtype=jnp.int32)[None, :]
    )
    part_high = jnp.max(logits, 1)
    part_sum = jnp.sum(jnp.exp(logits - part_high[:, None]), 1)
    part_target = jnp.sum(jnp.where(target_hit, logits, 0.0), 1)
    stats = jnp.stack([part_high, part_sum, part_target])
    for step in pl.ways(("dlo", "hi")):
        other = step(stats)
        larger = jnp.maximum(stats[0], other[0])
        summed = stats[1] * jnp.exp(stats[0] - larger) + other[1] * jnp.exp(other[0] - larger)
        stats = jnp.stack([larger, summed, stats[2] + other[2]])
    all_high, all_sum_exp, target_logit = stats
    row_total = all_high + jnp.log(all_sum_exp)
    mask_float = answer_mask.astype(full)
    count = jnp.sum(mask_float)
    own_mask = lax.dynamic_slice_in_dim(mask_float, pl.dp, 1, 0)[0]
    loss_part = jnp.where(
        pl.s == 0,
        jnp.sum(own_mask * (row_total - target_logit + zloss_weight * row_total * row_total)),
        0.0,
    )
    probs = jnp.exp(logits - row_total[:, None])
    logit_grad = (
        (own_mask / count)[:, None]
        * (probs * (1.0 + 2.0 * zloss_weight * row_total)[:, None] - target_hit.astype(full))
    ).astype(low)
    chosen_part = matmul(logit_grad, head_rows)
    ending_grad, final_gain_grad, branch_grad = move(
        functools.partial(ending_back_body, his),
        3,
        [
            ((picks, D), full, pltpu.VMEM),
            ((1, D), full, pltpu.VMEM),
            ((his, 2, picks, D), low, pallas.ANY),
        ],
        [chosen_part.reshape(his, 2, picks, D), ending, gain_float[2:3]],
        his,
        scatter=(picks, D),
        own=(picks, D),
        gathers=1,
    )
    branch_grad = branch_grad.reshape(line * picks, D)
    mixed_grad = matmul(branch_grad, mlp_full[:, 2 * part :])
    sigmoid_gate = jax.nn.sigmoid(gate)
    gate_grad = mixed_grad * upward * sigmoid_gate * (1.0 + gate * (1.0 - sigmoid_gate))
    upward_grad = mixed_grad * gate * sigmoid_gate
    gate_up_grad = jnp.concatenate([gate_grad, upward_grad], 1).astype(low)
    middle_up = matmul_nt(gate_up_grad, mlp_full[:, : 2 * part])
    down_grad = matmul_tn(after(branch_grad, middle_up), mixed)
    mlp_term = jnp.concatenate([matmul_tn(normed_two, gate_up_grad), down_grad], 1)
    mlp_term = mlp_term.astype(low).reshape(2, 2, his, 2, block, wide)
    mlp_state = cross_start(pl, mlp_term)
    head_rows_grad = matmul_tn(after(logit_grad, mlp_term), chosen).astype(low)
    head_grad = lax.psum_scatter(head_rows_grad, "dp", scatter_dimension=1, tiled=True)
    middle_up = after(middle_up, mlp_term, head_rows_grad)
    middle_grad, attn_branch_grad, middle_gain_grad = move(
        functools.partial(middle_back_body, his),
        4,
        [
            ((picks, D), full, pltpu.VMEM),
            ((picks, D), low, pltpu.VMEM),
            ((1, D), full, pltpu.VMEM),
        ],
        [middle_up.reshape(his, 2, picks, D), middle, gain_float[1:2], ending_grad],
        his,
        scatter=(picks, D),
    )
    attended_grad = matmul(attn_branch_grad, out_full).astype(low)
    query_raw, kv_part, branch_line = attend_rows_back(
        his,
        attended_grad,
        pick_tables,
        pick_pos,
        kv_all,
        queries,
        attended,
        log_total,
        attn_branch_grad,
    )
    mlp_keep, mlp_sends = cross_next(pl, mlp_state, kv_part)
    kv_part = after(kv_part, mlp_keep, mlp_sends)
    kv_raw, query_share = move(
        functools.partial(keys_back_body, his),
        5,
        [
            ((tokens, 2 * kv_width), low, pltpu.VMEM),
            ((line, picks, D // line), low, pltpu.VMEM),
        ],
        [
            kv_part.reshape(his, 2, tokens, 2 * kv_width),
            *token_tables,
            shares(query_raw),
        ],
        his,
        swap=(his, picks, D // line),
        scatter=(tokens, 2 * kv_width),
        own=(tokens, 2 * kv_width),
        own_type=full,
    )
    mlp_state = cross_send(pl, mlp_keep, after(mlp_sends, kv_raw))
    pick_up = matmul_nt(query_raw, query_full)
    tok_up = matmul_nt(kv_raw, kv_full)
    start_part, start_gain_grad = norm_back(
        start, gain_float[0], jnp.concatenate([tok_up, pick_up], 0)
    )
    start_grad = jnp.concatenate(
        [start_part[:tokens], start_part[tokens:] + middle_grad], 0
    ).astype(low)

    back_rows = lax.all_to_all(start_grad, "seq", split_axis=1, concat_axis=0, tiled=True)
    branch_line, pick_line = after((branch_line, pick_line), start_grad)
    branch_line, pick_line = (
        part.reshape(line * picks, D) for part in (branch_line, pick_line)
    )
    query_term = jnp.concatenate(
        [
            matmul_tn(pick_line, query_share.reshape(line * picks, D // line)),
            matmul_tn(branch_line, attended_share.reshape(line * picks, D // line)),
        ],
        1,
    )
    query_term = query_term.astype(low).reshape(2, 2, his, 2, block, query_term.shape[-1])
    query_state = cross_start(pl, query_term)
    gains_term = jnp.stack([start_gain_grad, middle_gain_grad[0], final_gain_grad[0]], 1)

    def by_core(rows, core):
        rows = rows.reshape(rows.shape[0], 2, 2, seqs * block)
        return pick(rows, core, 2).reshape(rows.shape[0], D // 2)

    def grid(rows):
        return rows.astype(low).reshape(2, his, 2, block, rows.shape[-1])

    def token_term(core):
        return jnp.concatenate(
            [
                matmul_tn(by_core(after(normed_tok, start_grad), core), kv_raw),
                jnp.pad(by_core(gains_term.T, core).T, ((0, 0), (0, 125))),
            ],
            1,
        )

    token_got = pl.send(token_term(1 - pl.c).astype(low), dc=1)
    token_keep = token_term(pl.c)
    other_squares = [jnp.sum(after(w, token_keep) ** 2) for w in (attn_w, mlp_w, head)]
    early = [
        loss_part,
        jnp.sum(attn_row),
        *other_squares,
        jnp.where(pl.s == 0, jnp.sum(emb_row), 0.0),
        emb_square_sum,
        jnp.where(pl.dp == 0, jnp.sum(head_row), 0.0),
        jnp.sum(gains * gains),
        jnp.sum(mlp_row),
    ]
    slot = jnp.arange(128, dtype=jnp.int32)
    early = sum(jnp.where(slot == i, value, 0.0) for i, value in enumerate(early))
    mlp_term = cross_end(pl, mlp_state, early)
    mlp_here, mlp_came = line_pairs(pl, mlp_term)
    back_rows, early = lax.optimization_barrier((back_rows, early, mlp_term, query_term))[:2]
    back_got = pl.send(back_rows, dy=1)
    token_sum = grid(token_keep + after(token_got, back_rows).astype(full))
    token_got = pl.send(pick(token_sum, 1 - pl.y, 0), dy=1)

    def on_chip(wanted):
        local, other = wanted - pl.dp * emb_n, wanted - (pl.dp ^ 1) * emb_n
        return jnp.where(
            (local >= 0) & (local < emb_n),
            local,
            jnp.where((other >= 0) & (other < emb_n), other + emb_n, 2 * emb_n),
        )

    places_in = on_chip(ids), on_chip(ids_y)
    chip_grad = (
        jnp.zeros((2 * emb_n + 8, emb_m), full)
        .at[places_in[0]]
        .add(after(back_rows, token_sum, mlp_came).astype(full))
    )
    mlp_got = line_sends(pl, mlp_here, after(mlp_came, token_sum))
    near, far = mlp_got[1:2] + mlp_got[-1:], mlp_got[2:-1]
    query_state = cross_send(pl, *cross_next(pl, query_state, chip_grad))
    head_grad = after(head_grad, query_state[:2], near[0]).astype(full)
    head_square = head_grad * head_grad + eps_square
    head_rows_sum = jnp.sum(head_square, 1)
    head_cols_sum = jnp.sum(head_square, 0)
    back_got = after(back_got, near[1:], head_rows_sum, head_cols_sum)
    chip_grad = chip_grad.at[places_in[1]].add(back_got.astype(full))
    token_sum = pick(token_sum, pl.y, 0).astype(full) + after(token_got, chip_grad).astype(full)
    token_got = pl.send(pick(token_sum, 1 - pl.lo, 1).astype(low), dlo=1)
    emb_part = after(chip_grad, far, token_sum)[emb_n : 2 * emb_n].astype(low)
    emb_got = pl.send(emb_part, dc=1)
    query_term = cross_end(pl, query_state, emb_part)
    token_sum = pick(token_sum, pl.lo, 1) + after(token_got, emb_part).astype(full)
    mlp_grad, mlp_rows, mlp_cols = join_columns(line_place(pl, after(mlp_got, query_term)))
    mlp_row_new = decay_rate * mlp_row + (1.0 - decay_rate) * mlp_rows / (3 * FF)
    emb_grad = chip_grad[:emb_n] + after(emb_got, query_term, token_sum).astype(full)
    emb_square = emb_grad * emb_grad + eps_square
    emb_rows, emb_cols = jnp.sum(emb_square, 1), jnp.sum(emb_square, 0)
    attn_grad, gains_grad, attn_rows, attn_cols = layer_gradient(
        his, after(query_term, emb_rows), token_sum
    )
    gains_grad = gains_grad[:, :3].T
    attn_row_new = decay_rate * attn_row + (1.0 - decay_rate) * attn_rows[:, 0] / (QKV + D)
    scalars = early
    for at, value in ((10, emb_cols), (11, head_cols_sum)):
        scalars = scalars + jnp.where(slot == at, jnp.sum(value), 0.0)
    (
        emb_row_sum,
        head_col_sum,
        attn_cols_sum,
        mlp_cols_sum,
        totals,
        head_row_sum,
        emb_col_sum,
    ) = sum_statistics(
        his,
        (emb_rows, head_cols_sum),
        (attn_cols[0], mlp_cols, scalars),
        (head_rows_sum, emb_cols),
    )
    attn_row_total = decay_rate * totals[1] + (1.0 - decay_rate) * jnp.sum(attn_cols_sum) / (QKV + D)
    mlp_row_total = decay_rate * totals[9] + (1.0 - decay_rate) * jnp.sum(mlp_cols_sum) / (3 * FF)
    emb_row_total, head_row_total = totals[10], totals[11]

    attn_col_new = decay_rate * attn_col + (1.0 - decay_rate) * attn_cols_sum / D
    mlp_col_new = decay_rate * mlp_col + (1.0 - decay_rate) * mlp_cols_sum / D
    attn_update = attn_grad * lax.rsqrt(
        attn_row_new[:, None] * attn_col_new[None, :] / (attn_row_total / D)
    )
    mlp_update = mlp_grad * lax.rsqrt(
        mlp_row_new[:, None] * mlp_col_new[None, :] / (mlp_row_total / D)
    )
    emb_row_new = decay_rate * emb_row + (1.0 - decay_rate) * emb_row_sum / D
    emb_col_new = decay_rate * emb_col + (1.0 - decay_rate) * emb_col_sum / VOCAB
    emb_mean = (decay_rate * totals[5] + (1.0 - decay_rate) * emb_row_total / D) / VOCAB
    emb_update = emb_grad * lax.rsqrt(emb_row_new[:, None] * emb_col_new[None, :] / emb_mean)
    head_row_new = decay_rate * head_row + (1.0 - decay_rate) * head_row_sum / D
    head_col_new = decay_rate * head_col + (1.0 - decay_rate) * head_col_sum / VOCAB
    head_mean = (decay_rate * totals[7] + (1.0 - decay_rate) * head_row_total / D) / VOCAB
    head_update = head_grad * lax.rsqrt(head_row_new[:, None] * head_col_new[None, :] / head_mean)
    moment_new = decay_rate * gains_moment + (1.0 - decay_rate) * (
        gains_grad * gains_grad + eps_square
    )
    gains_update = gains_grad * lax.rsqrt(moment_new)
    attn_new = finish(attn_w, attn_update, totals[2], D * (QKV + D))
    mlp_new = finish(mlp_w, mlp_update, totals[3], D * 3 * FF)
    emb_new = finish(emb, emb_update, totals[6], VOCAB * D)
    head_new = finish(head, head_update, totals[4], VOCAB * D)
    gains_new = finish(gains, gains_update, totals[8], 3 * D)
    return (
        totals[0],
        count,
        emb_grad,
        emb_new,
        emb_row_new,
        emb_col_new,
        head_grad,
        head_new,
        head_row_new,
        head_col_new,
        attn_grad,
        attn_new,
        attn_row_new,
        attn_col_new,
        mlp_grad,
        mlp_new,
        mlp_row_new,
        mlp_col_new,
        gains_grad,
        moment_new,
        gains_new,
    )


def solution(mesh):
    return jax.shard_map(
        on_device,
        mesh=mesh,
        in_specs=(
            P("dp", None),
            P("dp", None),
            P("dp", None),
            P(),
            P("dp", "seq"),
            P("seq", "dp"),
            P(("dp", "seq"), None),
            P(("dp", "seq"), None),
            P(None, ("dp", "seq")),
            P("dp"),
            P("seq"),
            P("seq"),
            P("dp"),
            P(("dp", "seq")),
            P(),
            P(("dp", "seq")),
            P(),
            P(None, ("dp", "seq")),
        ),
        out_specs=(
            P(),
            P(),
            P("dp", "seq"),
            P("dp", "seq"),
            P("dp"),
            P("seq"),
            P("seq", "dp"),
            P("seq", "dp"),
            P("seq"),
            P("dp"),
            P(("dp", "seq"), None),
            P(("dp", "seq"), None),
            P(("dp", "seq")),
            P(),
            P(("dp", "seq"), None),
            P(("dp", "seq"), None),
            P(("dp", "seq")),
            P(),
            P(None, ("dp", "seq")),
            P(None, ("dp", "seq")),
            P(None, ("dp", "seq")),
        ),
        check_vma=False,
    )
```

```python
import functools
import math

import jax
import jax.numpy as jnp
from jax import lax
from jax.experimental import pallas
from jax.experimental.pallas import tpu as pltpu
from jax.sharding import PartitionSpec as P

D = 2048
HEADS = 32
KVH = 4
HD = 64
FF = 5632
VOCAB = 32000
QKV = 2560


eps_norm = 1e-05
eps_square = 1e-30
decay_rate = 0.5
learn_rate = 1.0
zloss_weight = 0.0001
orig_context = 2048.0
yarn_factor = 4.0
highest = lax.Precision.HIGHEST


def yarn_tables(places):
    halves = jnp.arange(HD // 2, dtype=jnp.float32)
    inverse = jnp.power(10000.0, -2.0 * halves / HD)
    ratio = orig_context * inverse / (2.0 * math.pi)
    ramp_part = jnp.clip((ratio - 1.0) / 31.0, 0.0, 1.0)
    frequency = inverse / yarn_factor * (1.0 - ramp_part) + inverse * ramp_part
    angles = places[:, None] * frequency[None, :]
    magnitude = 0.1 * math.log(yarn_factor) + 1.0
    return (jnp.cos(angles) * magnitude, jnp.sin(angles) * magnitude)


def rotate(values, cosine, sine):
    first = values[..., : HD // 2]
    second = values[..., HD // 2 :]
    cosine_row = cosine[:, None, :]
    sine_row = sine[:, None, :]
    return jnp.concatenate(
        [first * cosine_row - second * sine_row, second * cosine_row + first * sine_row], -1
    )


def unrotate(values, cosine, sine):
    first = values[..., : HD // 2]
    second = values[..., HD // 2 :]
    cosine_row = cosine[:, None, :]
    sine_row = sine[:, None, :]
    return jnp.concatenate(
        [first * cosine_row + second * sine_row, second * cosine_row - first * sine_row], -1
    )


def rms_norm(values, gain_row):
    return values * lax.rsqrt(jnp.mean(values * values, -1, keepdims=True) + eps_norm) * gain_row


def norm_back(values, gain_row, upstream):
    factor = lax.rsqrt(jnp.mean(values * values, -1, keepdims=True) + eps_norm)
    normed = values * factor
    gain_grad = jnp.sum(upstream * normed, 0)
    inner = upstream * gain_row
    return (factor * (inner - normed * jnp.mean(inner * normed, -1, keepdims=True)), gain_grad)


def matmul(left, right):
    return jnp.dot(left, right, preferred_element_type=jnp.float32)


def matmul_nt(left, right):
    return lax.dot_general(
        left, right, (((1,), (1,)), ((), ())), preferred_element_type=jnp.float32
    )


def matmul_tn(left, right):
    return lax.dot_general(
        left, right, (((0,), (0,)), ((), ())), preferred_element_type=jnp.float32
    )


def finish(weight, update, weight_square, entries):
    return weight - learn_rate * jnp.maximum(0.001, jnp.sqrt(weight_square / entries)) * update


low = jnp.bfloat16
full = jnp.float32


class Place:
    def __init__(self):
        self.seqs = lax.axis_size("seq")
        self.dps = lax.axis_size("dp")
        self.dp = lax.axis_index("dp")
        self.s = lax.axis_index("seq")
        self.his = self.seqs // 2
        self.y, self.c = self.dp // 2, self.dp % 2
        self.hi, self.lo = self.s // 2, self.s % 2

    def send(self, value, dy=0, dc=0, dlo=0, up=0):
        pairs = []
        for d in range(self.dps):
            for s in range(self.seqs):
                to_d = d ^ (2 * dy + dc)
                to_s = ((s // 2 + up) % self.his) * 2 + ((s % 2) ^ dlo)
                pairs.append((d * self.seqs + s, to_d * self.seqs + to_s))
        return lax.ppermute(value, ("dp", "seq"), pairs)

    def ways(self, names):
        steps = []
        for name in names:
            if name == "hi":
                bit = 1
                while bit < self.his:
                    steps.append(lambda value, bit=bit: self.swap_hi(value, bit))
                    bit *= 2
            else:
                steps.append(lambda value, name=name: self.send(value, **{name: 1}))
        return steps

    def swap_hi(self, value, bit):
        pairs = []
        for d in range(self.dps):
            for s in range(self.seqs):
                pairs.append((d * self.seqs + s, d * self.seqs + (s ^ (2 * bit))))
        return lax.ppermute(value, ("dp", "seq"), pairs)


def after(value, *events):
    return lax.optimization_barrier((value, *events))[0] if events else value


def pick(array, index, axis):
    return lax.dynamic_index_in_dim(array, index, axis, keepdims=False)


def put(array, block, index, axis):
    return lax.dynamic_update_slice_in_dim(array, jnp.expand_dims(block, axis), index, axis)


def line_pairs(pl, blocks):
    grid = blocks.reshape(2, pl.his, *blocks.shape[1:])
    return pick(grid, pl.c, 0), pl.send(pick(grid, 1 - pl.c, 0), dc=1)


def line_sends(pl, here, came):
    pairs = jnp.stack([here, came], 1)
    got = []
    for k in range(pl.his):
        pair = pick(pairs, (pl.hi + k) % pl.his, 0)
        got.append(pl.send(pair, up=k) if k else pair)
    return got


def place_body(*refs):
    pairs, out, sems = refs[:-2], refs[-2], refs[-1]
    n = len(pairs)
    dp, s = lax.axis_index("dp"), lax.axis_index("seq")
    c, hi = dp % 2, s // 2
    copies = []
    for k, pair in enumerate(pairs):
        for j, side in enumerate((c, 1 - c)):
            copies.append(
                pltpu.make_async_copy(
                    pair.at[j], out.at[side * n + lax.rem(hi + n - k, n)], sems.at[2 * k + j]
                )
            )
            copies[-1].start()
    for copy in copies:
        copy.wait()


def line_place(pl, got):
    count = len(got)
    shape = (2 * count, *got[0].shape[1:])
    return pallas.pallas_call(
        place_body,
        out_shape=jax.ShapeDtypeStruct(shape, got[0].dtype),
        in_specs=[pallas.BlockSpec(memory_space=pallas.ANY)] * count,
        out_specs=pallas.BlockSpec(memory_space=pltpu.VMEM),
        scratch_shapes=[pltpu.SemaphoreType.DMA((2 * count,))],
        cost_estimate=SMALL,
        name="line_place",
    )(*got)


def assemble_body(line, over_x, over_y, far_a, far_b, out, sems):
    dp, s = lax.axis_index("dp"), lax.axis_index("seq")
    y, lo = dp // 2, s % 2
    his = line.shape[1]
    copies = []
    for c in range(2):
        for h in range(his):
            for block, at_y, at_lo in (
                (line.at[c, h], y, lo),
                (over_x.at[c, h], y, 1 - lo),
                (over_y.at[c, h], 1 - y, lo),
                ((far_b if c else far_a).at[h], 1 - y, 1 - lo),
            ):
                copies.append(
                    pltpu.make_async_copy(
                        block, out.at[at_y, c, h, at_lo], sems.at[len(copies)]
                    )
                )
                copies[-1].start()
    for copy in copies:
        copy.wait()


def assemble(line, over_x, over_y, far_a, far_b):
    two, his, rows, columns = line.shape
    return pallas.pallas_call(
        assemble_body,
        out_shape=jax.ShapeDtypeStruct((2, two, his, 2, rows, columns), line.dtype),
        in_specs=[pallas.BlockSpec(memory_space=pallas.ANY)] * 5,
        out_specs=pallas.BlockSpec(memory_space=pltpu.VMEM),
        scratch_shapes=[pltpu.SemaphoreType.DMA((8 * his,))],
        cost_estimate=SMALL,
        compiler_params=pltpu.CompilerParams(vmem_limit_bytes=32 * 2**20),
        name="assemble",
    )(line, over_x, over_y, far_a, far_b)


def cross_start(pl, term):
    a, b = term[:, 0], term[:, 1]
    got_a = pl.send(pick(a, 1 - pl.y, 0), dy=1)
    got_b = pl.send(pick(b, 1 - pl.lo, 2), dlo=1)
    return a, b, got_a, got_b


def cross_next(pl, state, *work):
    a, b, got_a, got_b = state
    got_a, got_b = after((got_a, got_b), *work)
    a = pick(a, pl.y, 0).astype(full) + got_a.astype(full)
    b = pick(b, pl.lo, 2).astype(full) + got_b.astype(full)
    send_a = pick(a, 1 - pl.lo, 1).astype(low)
    send_b = pick(b, 1 - pl.y, 0).astype(low)
    keep = pick(a, pl.lo, 1), pick(b, pl.y, 0)
    return keep, (send_a, send_b)


def cross_send(pl, keep, sends):
    return *keep, pl.send(sends[0], dlo=1), pl.send(sends[1], dy=1)


def cross_end(pl, state, *work):
    a, b, got_a, got_b = state
    got_a, got_b = after((got_a, got_b), *work)
    a = (a + got_a.astype(full)).astype(low)
    b = (b + got_b.astype(full)).astype(low)
    return jnp.stack([a, b]).reshape(2 * pl.his, *a.shape[1:])


def split_kernel(line, part, in_ref, out_ref):
    for j in range(3):
        for t in range(line):
            at = (j * line + t) * part
            out_ref[t, :, j * part : (j + 1) * part] = in_ref[:, at : at + part].astype(low)


def split_columns(weight, line):
    rows, columns = weight.shape
    part = columns // (3 * line)
    return pallas.pallas_call(
        lambda *refs: split_kernel(line, part, *refs),
        out_shape=jax.ShapeDtypeStruct((line, rows, 3 * part), low),
        in_specs=[pallas.BlockSpec(memory_space=pltpu.VMEM)],
        out_specs=pallas.BlockSpec(memory_space=pltpu.VMEM),
        compiler_params=pltpu.CompilerParams(vmem_limit_bytes=40 * 2**20),
        name="split_columns",
    )(weight)


def join_kernel(line, part, in_ref, out_ref, rows_ref, columns_ref):
    total = jnp.zeros(rows_ref.shape, full)
    for j in range(3):
        for t in range(line):
            at = (j * line + t) * part
            block = in_ref[t, :, j * part : (j + 1) * part].astype(full)
            out_ref[:, at : at + part] = block
            square = block * block + eps_square
            columns_ref[:, at : at + part] = jnp.sum(square, 0, keepdims=True)
            total = total + jnp.sum(square, 1, keepdims=True)
    rows_ref[...] = total


def join_columns(blocks):
    line, rows, wide = blocks.shape
    part = wide // 3
    grad, row_sum, column_sum = pallas.pallas_call(
        lambda *refs: join_kernel(line, part, *refs),
        out_shape=(
            jax.ShapeDtypeStruct((rows, line * wide), full),
            jax.ShapeDtypeStruct((rows, 1), full),
            jax.ShapeDtypeStruct((1, line * wide), full),
        ),
        in_specs=[pallas.BlockSpec(memory_space=pltpu.VMEM)],
        out_specs=(pallas.BlockSpec(memory_space=pltpu.VMEM),) * 3,
        compiler_params=pltpu.CompilerParams(vmem_limit_bytes=40 * 2**20),
        name="join_columns",
    )(blocks)
    return grad, row_sum[:, 0], column_sum[0]


def halve(pl, part, mine, axis, **way):
    got = pl.send(pick(part, 1 - mine, axis).astype(low), **way)
    return pick(part, mine, axis).astype(full) + got.astype(full)


def hi_sum(pl, part, *work):
    total = pick(part, pl.hi, 0).astype(full)
    for k in range(1, pl.his):
        block = pick(part, (pl.hi + k) % pl.his, 0).astype(low)
        total = total + after(pl.send(block, up=k), *work).astype(full)
    return total


MESH = pallas.DeviceIdType.MESH
ROWS = 16
SMALL = pallas.CostEstimate(flops=1024, bytes_accessed=1024, transcendentals=0)


class Core:
    def __init__(self, his):
        dp, s = lax.axis_index("dp"), lax.axis_index("seq")
        self.his = his
        self.hi, self.lo, self.c = s // 2, s % 2, dp % 2
        self.side = {"c": self.c, "lo": self.lo}
        self.across = [
            (dp, lax.rem(self.hi + k, his) * 2 + self.lo) for k in range(his)
        ]
        self.ids = {
            "c": (dp + 1 - 2 * self.c, s),
            "lo": (dp, s + 1 - 2 * self.lo),
            "up": (dp, lax.rem(self.hi + 1, his) * 2 + self.lo),
            "down": (dp, lax.rem(self.hi + his - 1, his) * 2 + self.lo),
        }

    def meet(self, *names):
        others = [self.ids[name] for name in names if name != "line"]
        if "line" in names:
            others += self.across[1:]
        barrier = pltpu.get_barrier_semaphore()
        for other in others:
            pallas.semaphore_signal(barrier, inc=1, device_id=other, device_id_type=MESH)
        pallas.semaphore_wait(barrier, len(others))

    def copy(self, source, target, sems, at, name):
        return pltpu.make_async_remote_copy(
            src_ref=source,
            dst_ref=target,
            send_sem=sems[0].at[at],
            recv_sem=sems[1].at[at],
            device_id=self.ids[name] if isinstance(name, str) else self.across[name],
            device_id_type=MESH,
        )


def by_rows(n, step):
    def one(i, carry):
        step(pallas.ds(pallas.multiple_of(i * ROWS, ROWS), ROWS))
        return carry

    lax.fori_loop(0, n // ROWS, one, 0)


def kernel_scatter(core, name, part, total, held, side_sems, up_sems, beside=iter(())):
    his, side = core.his, core.side[name]
    side_out, side_in, up_out, up_in = held
    n = part.shape[2]
    over = []
    for j in range(his):
        h = lax.rem(core.hi + 2 * his - 1 - j, his)

        def cast(at, j=j, h=h):
            side_out[j, at, :] = part[h, 1 - side, at, :].astype(low)

        by_rows(n, cast)
        over.append(core.copy(side_out.at[j], side_in.at[j], side_sems, j, name))
        over[j].start()
    climb = []
    for j in range(his):
        h = lax.rem(core.hi + 2 * his - 1 - j, his)
        over[j].wait_recv()
        if j:
            climb[j - 1].wait_recv()

        def add(at, j=j, h=h):
            acc = part[h, side, at, :].astype(full) + side_in[j, at, :].astype(full)
            if j:
                acc = acc + up_in[j - 1, at, :].astype(full)
            if j < his - 1:
                up_out[j, at, :] = acc.astype(low)
            else:
                total[at, :] = acc

        by_rows(n, add)
        if j < his - 1:
            climb.append(core.copy(up_out.at[j], up_in.at[j], up_sems, j, "up"))
            climb[j].start()
        next(beside, None)
    return over + climb


def gather_steps(core, name, own, out, copies, sems, side_first=False):
    his, side = core.his, core.side[name]
    local_sem, side_sems, up_sems = sems[0], sems[1:3], sems[3:5]

    def slot(h):
        return out.at[side, h] if side_first else out.at[h, side]

    here = pltpu.make_async_copy(own, slot(core.hi), local_sem)
    here.start()
    over, climb = [], []
    for j in range(his):
        block = slot(lax.rem(core.hi + his - j, his))
        source = own if j == 0 else block
        if j:
            climb[j - 1].wait_recv()
        if j < his - 1:
            climb.append(core.copy(source, block, up_sems, j, "up"))
            climb[j].start()
        over.append(core.copy(source, block, side_sems, j, name))
        over[j].start()
        yield
    for copy in over:
        copy.wait_recv()
    here.wait()
    copies += over + climb


def kernel_gather(*args, **kwargs):
    for _ in gather_steps(*args, **kwargs):
        pass


def direct_start(core, own, out, sems):
    here = pltpu.make_async_copy(own, out.at[core.c, core.hi], sems[0])
    place = out.at[core.c, core.hi]
    climb = [core.copy(own, place, sems[3:5], k - 1, k) for k in range(1, core.his)]
    over = [core.copy(own, place, sems[1:3], 0, "c")]
    for copy in [here, *climb, *over]:
        copy.start()
    return here, climb, over


def direct_end(core, started, out, sems):
    here, climb, over = started
    order = sorted(range(1, core.his), key=lambda k: min(k, core.his - k))
    for k in order:
        climb[k - 1].wait_recv()
        block = out.at[core.c, lax.rem(core.hi + core.his - k, core.his)]
        over.append(core.copy(block, block, sems[1:3], k, "c"))
        over[-1].start()
    for copy in over:
        copy.wait_recv()
    here.wait()
    sent(climb + over)


def direct_scratch(his):
    dma = pltpu.SemaphoreType.DMA
    return [dma, dma((his,)), dma((his,)), dma((his - 1,)), dma((his - 1,))]


def kernel_swap_start(core, blocks, came, side_sems):
    his = core.his
    over = core.copy(
        blocks.at[pallas.ds((1 - core.c) * his, his)], came, side_sems, 0, "c"
    )
    over.start()
    return over


def kernel_swap_end(core, over, blocks, came, out, local_sems, up_sems):
    his, c, hi = core.his, core.c, core.hi
    mine, theirs = c * his + hi, (1 - c) * his + hi
    here = [pltpu.make_async_copy(blocks.at[mine], out.at[mine], local_sems.at[0])]
    climb = []
    for k in range(1, his):
        to = lax.rem(hi + k, his)
        climb.append(core.copy(blocks.at[c * his + to], out.at[mine], up_sems, 2 * k - 2, k))
    over.wait_recv()
    here.append(pltpu.make_async_copy(came.at[hi], out.at[theirs], local_sems.at[1]))
    for k in range(1, his):
        to = lax.rem(hi + k, his)
        climb.append(core.copy(came.at[to], out.at[theirs], up_sems, 2 * k - 1, k))
    for copy in here + climb:
        copy.start()
    return here, [over] + climb


def swap_done(here, copies):
    for copy in here:
        copy.wait()
    for copy in copies[1:]:
        copy.wait_recv()


def sent(copies):
    for copy in copies:
        copy.wait_send()


def norm_rows(values, gain):
    return values * lax.rsqrt(jnp.mean(values * values, -1, keepdims=True) + eps_norm) * gain


def norm_rows_back(values, gain, upstream):
    factor = lax.rsqrt(jnp.mean(values * values, -1, keepdims=True) + eps_norm)
    normed = values * factor
    inner = upstream * gain
    back = factor * (inner - normed * jnp.mean(inner * normed, -1, keepdims=True))
    return back, jnp.sum(upstream * normed, 0, keepdims=True)


def norm_gather_body(his, values, gain, blocks, out, swapped, came, own, *sems):
    core = Core(his)
    by_rows(
        values.shape[0],
        lambda at: own.__setitem__(
            (at, slice(None)), norm_rows(values[at, :], gain[...]).astype(low)
        ),
    )
    core.meet("c", "line")
    over = kernel_swap_start(core, blocks, came, sems[1:3])
    copies = []
    kernel_gather(core, "c", own, out, copies, sems[5:10])
    here, more = kernel_swap_end(core, over, blocks, came, swapped, sems[0], sems[3:5])
    swap_done(here, more)
    sent(copies + more)


def turn_keys(source, cosine, sine, target):
    width = KVH * HD
    for at in range(0, width, 2 * HD):
        pair = turned(source[:, at : at + 2 * HD], cosine, sine)
        target[:, at : at + 2 * HD] = pair.astype(low)
    target[:, width:] = source[:, width:].astype(low)


def keys_body(his, projected, cosine, sine, out, own, *sems):
    core = Core(his)
    turn_keys(projected, cosine[...], sine[...], own)
    core.meet("lo", "up", "down")
    copies = []
    kernel_gather(core, "lo", own, out, copies, sems)
    sent(copies)


def keys_back_body(
    his, part, cosine, sine, blocks, out, swapped, came, total, *rest
):
    swap_sems, held, sems = rest[:5], rest[5:9], rest[9:13]
    core = Core(his)
    core.meet("c", "lo", "line")
    over = kernel_swap_start(core, blocks, came, swap_sems[1:3])
    copies = []
    copies += kernel_scatter(core, "lo", part, total, held, sems[0:2], sems[2:4])
    here, more = kernel_swap_end(core, over, blocks, came, swapped, swap_sems[0], swap_sems[3:5])
    turn_keys(total, cosine[...], -sine[...], out)
    swap_done(here, more)
    sent(copies + more)


def layer_body(his, blocks, tokens, grad, gains, rows, columns, swapped, came, out_low, in_low, *sems):
    core = Core(his)
    wide = blocks.shape[2] // 2
    side, keys = 2 * his, 2 * KVH * HD
    core.meet("c", "line")
    over = kernel_swap_start(core, blocks, came, sems[1:3])
    climb = []
    for k in range(1, his):
        to = lax.rem(core.hi + k, his)
        out_low[k - 1] = tokens[to].astype(low)
        climb.append(core.copy(out_low.at[k - 1], in_low.at[k - 1], sems[5:7], k - 1, k))
        climb[-1].start()
    here, more = kernel_swap_end(core, over, blocks, came, swapped, sems[0], sems[3:5])
    total = tokens[core.hi]
    for k, copy in enumerate(climb):
        copy.wait_recv()
        total = total + in_low[k].astype(full)
    gains[...] = total[:, keys:]
    row_sum = jnp.zeros(rows.shape, full)
    pieces = [(D, total[:, :keys])]
    swap_done(here, more)
    for t in range(side):
        pieces.append((t * wide, swapped[t, :, :wide].astype(full)))
        pieces.append((QKV + t * wide, swapped[t, :, wide:].astype(full)))
    for at, piece in pieces:
        till = at + piece.shape[1]
        grad[:, at:till] = piece
        square = piece * piece + eps_square
        columns[:, at:till] = jnp.sum(square, 0, keepdims=True)
        row_sum = row_sum + jnp.sum(square, 1, keepdims=True)
    rows[...] = row_sum
    sent(climb + more)


def layer_gradient(his, blocks, tokens):
    line, rows, columns = blocks.shape
    extra = tokens.shape[2] - 2 * KVH * HD
    dma = pltpu.SemaphoreType.DMA
    return pallas.pallas_call(
        functools.partial(layer_body, his),
        out_shape=(
            jax.ShapeDtypeStruct((rows, QKV + D), full),
            jax.ShapeDtypeStruct((rows, extra), full),
            jax.ShapeDtypeStruct((rows, 1), full),
            jax.ShapeDtypeStruct((1, QKV + D), full),
        ),
        in_specs=[pallas.BlockSpec(memory_space=pltpu.VMEM)] * 2,
        out_specs=(pallas.BlockSpec(memory_space=pltpu.VMEM),) * 4,
        scratch_shapes=[
            pltpu.VMEM(blocks.shape, low),
            pltpu.VMEM((his, rows, columns), low),
            pltpu.VMEM((his - 1, *tokens.shape[1:]), low),
            pltpu.VMEM((his - 1, *tokens.shape[1:]), low),
            dma((2,)),
            *[dma((count,)) for count in (1, 1, 2 * his - 2, 2 * his - 2, his - 1, his - 1)],
        ],
        cost_estimate=SMALL,
        compiler_params=pltpu.CompilerParams(
            collective_id=7, has_side_effects=True, vmem_limit_bytes=32 * 2**20
        ),
        name="layer_gradient",
    )(blocks, tokens)


def ending_body(his, part, middle, gain, ending, chosen, own, *rest):
    held, sems = rest[:4], rest[4:]
    core = Core(his)
    core.meet("c", "lo", "up", "down")
    copies = kernel_scatter(core, "c", part, ending, held, sems[0:2], sems[2:4])

    def finish_rows(at):
        values = ending[at, :] + middle[at, :]
        ending[at, :] = values
        own[at, :] = norm_rows(values, gain[...]).astype(low)

    by_rows(middle.shape[0], finish_rows)
    kernel_gather(core, "lo", own, chosen, copies, sems[4:9])
    sent(copies)


def ending_back_body(his, part, ending, gain, grad, gain_grad, branch, own, *rest):
    held, sems = rest[:4], rest[4:]
    core = Core(his)
    core.meet("c", "lo", "up", "down")
    copies = kernel_scatter(core, "lo", part, grad, held, sems[0:2], sems[2:4])
    gain_grad[...] = jnp.zeros(gain_grad.shape, full)

    def back_rows(at):
        back, gained = norm_rows_back(ending[at, :], gain[...], grad[at, :])
        grad[at, :] = back
        own[at, :] = back.astype(low)
        gain_grad[...] += gained

    by_rows(ending.shape[0], back_rows)
    kernel_gather(core, "c", own, branch, copies, sems[4:9])
    sent(copies)


def middle_back_body(his, part, middle, gain, ending_grad, grad, grad_low, gain_grad, *rest):
    held, sems = rest[:4], rest[4:]
    core = Core(his)
    core.meet("c", "up", "down")
    copies = kernel_scatter(core, "c", part, grad, held, sems[0:2], sems[2:4])
    gain_grad[...] = jnp.zeros(gain_grad.shape, full)

    def back_rows(at):
        back, gained = norm_rows_back(middle[at, :], gain[...], grad[at, :])
        back = back + ending_grad[at, :]
        grad[at, :] = back
        grad_low[at, :] = back.astype(low)
        gain_grad[...] += gained

    by_rows(middle.shape[0], back_rows)
    sent(copies)


def move(body, collective_id, outs, args, his, scatter=None, own=None, own_type=low, gathers=0, swap=None):
    dma = pltpu.SemaphoreType.DMA
    scratch = []
    if swap:
        scratch.append(pltpu.VMEM(swap, low))
    if own:
        scratch.append(pltpu.VMEM(own, own_type))
    if swap:
        scratch += [dma((2,))]
        scratch += [dma((count,)) for count in (1, 1, 2 * his - 2, 2 * his - 2)]
    if scatter:
        scratch += [pltpu.VMEM((count, *scatter), low) for count in (his, his, his - 1, his - 1)]
        scratch += [dma((his,)), dma((his,)), dma((his - 1,)), dma((his - 1,))]
    for _ in range(gathers):
        scratch += [dma, dma((his,)), dma((his,)), dma((his - 1,)), dma((his - 1,))]
    return pallas.pallas_call(
        body,
        out_shape=tuple(jax.ShapeDtypeStruct(shape, dtype) for shape, dtype, _ in outs),
        in_specs=[pallas.BlockSpec(memory_space=pltpu.VMEM)] * len(args),
        out_specs=tuple(pallas.BlockSpec(memory_space=memory) for _, _, memory in outs),
        scratch_shapes=scratch,
        cost_estimate=SMALL,
        compiler_params=pltpu.CompilerParams(
            collective_id=collective_id,
            has_side_effects=True,
            vmem_limit_bytes=48 * 2**20,
        ),
    )(*args)


HALF = HD // 2
STACK = 4


def turn_tables(cosine, sine):
    return jnp.concatenate([cosine] * 4, 1), jnp.concatenate([-sine, sine] * 2, 1)


def turned(values, cosine, sine):
    lane = lax.broadcasted_iota(jnp.int32, values.shape, 1) % HD
    other = jnp.where(
        lane < HALF, pltpu.roll(values, 2 * HD - HALF, 1), pltpu.roll(values, HALF, 1)
    )
    return values * cosine + other * sine


def heads_loop(loops, step):
    def one(t, carry):
        step(t)
        return carry

    lax.fori_loop(0, loops, one, 0)


def split_kv(kv, k_held, v_held):
    width = KVH * HD
    for g in range(KVH):
        k_held[g] = kv[:, g * HD : (g + 1) * HD]
        v_held[g] = kv[:, width + g * HD : width + (g + 1) * HD]


def allowed_keys(places, keys):
    places = jnp.concatenate([places] * STACK, 0)
    return lax.broadcasted_iota(jnp.int32, (places.shape[0], keys), 1) <= places


def dot_nt(left, right):
    return lax.dot_general(
        left, right, (((1,), (1,)), ((), ())), preferred_element_type=jnp.float32
    )


def attend_body(
    his, raw, cosine, sine, places, kv, own, turned_out, out_low, held_out, logs, line_out, k_held, v_held, *sems
):
    picks, keys = raw.shape[0], kv.shape[0]
    core = Core(his)
    core.meet("c", "line")
    started = direct_start(core, own, line_out, sems)
    split_kv(kv, k_held, v_held)
    for j in range(D // (2 * HD)):
        pair = turned(raw[:, 2 * HD * j : 2 * HD * (j + 1)], cosine[...], sine[...]).astype(low)
        for i in range(2):
            t, at = divmod(2 * j + i, STACK)
            turned_out[t, at * picks : (at + 1) * picks, :] = pair[:, i * HD : (i + 1) * HD]
    allowed = allowed_keys(places[...], keys)

    def step(t):
        g = t // (HEADS // KVH // STACK)
        scores = dot_nt(turned_out[t], k_held[g]) * HD ** (-0.5)
        scores = jnp.where(allowed, scores, -1e30)
        high = jnp.max(scores, 1, keepdims=True)
        weights = jnp.exp(scores - high)
        total = jnp.sum(weights, 1, keepdims=True)
        result = jnp.dot(weights.astype(low), v_held[g], preferred_element_type=full)
        held_out[t] = result / total
        logs[t] = jnp.broadcast_to(high + jnp.log(total), (STACK * picks, 2 * HD))

    heads_loop(HEADS // STACK, step)
    for j in range(D // (2 * HD)):
        pair = []
        for i in range(2):
            t, at = divmod(2 * j + i, STACK)
            pair.append(held_out[t, at * picks : (at + 1) * picks, :])
        pair = jnp.concatenate(pair, 1)
        out_low[:, 2 * HD * j : 2 * HD * (j + 1)] = pair.astype(low)
    direct_end(core, started, line_out, sems)


def attend_rows(his, raw, tables, places, kv, own):
    picks, keys = raw.shape[0], kv.shape[0]
    stacks, rows = HEADS // STACK, STACK * picks
    return pallas.pallas_call(
        functools.partial(attend_body, his),
        out_shape=(
            jax.ShapeDtypeStruct((stacks, rows, HD), low),
            jax.ShapeDtypeStruct((picks, D), low),
            jax.ShapeDtypeStruct((stacks, rows, HD), full),
            jax.ShapeDtypeStruct((stacks, rows, 2 * HD), full),
            jax.ShapeDtypeStruct((2, his, *own.shape), low),
        ),
        in_specs=[pallas.BlockSpec(memory_space=pltpu.VMEM)] * 6,
        out_specs=(pallas.BlockSpec(memory_space=pltpu.VMEM),) * 4
        + (pallas.BlockSpec(memory_space=pallas.ANY),),
        scratch_shapes=[pltpu.VMEM((KVH, keys, HD), low)] * 2 + direct_scratch(his),
        compiler_params=pltpu.CompilerParams(
            collective_id=9, has_side_effects=True, vmem_limit_bytes=56 * 2**20
        ),
        cost_estimate=SMALL,
        name="attend",
    )(raw, *tables, places[:, None], kv, own)


def attend_back_body(
    his, grad, cosine, sine, places, kv, queries, held_out, logs, own, raw, kv_grad, line_out, k_held, v_held,
    grad_held, query_held, *rest
):
    picks, keys = grad.shape[0], kv.shape[0]
    sems, sums = rest[:5], rest[5:]
    core = Core(his)
    core.meet("c", "line")
    started = direct_start(core, own, line_out, sems)
    scale = HD ** (-0.5)
    split_kv(kv, k_held, v_held)
    for j in range(D // (2 * HD)):
        pair = grad[:, 2 * HD * j : 2 * HD * (j + 1)]
        for i in range(2):
            t, at = divmod(2 * j + i, STACK)
            grad_held[t, at * picks : (at + 1) * picks, :] = pair[:, i * HD : (i + 1) * HD]
    allowed = allowed_keys(places[...], keys)
    total = sums[0] if sums else kv_grad
    total[...] = jnp.zeros(total.shape, full)

    def step(t):
        g = t // (HEADS // KVH // STACK)
        query, up = queries[t], grad_held[t]
        delta = jnp.sum(up.astype(full) * held_out[t], 1, keepdims=True)
        scores = dot_nt(query, k_held[g]) * scale
        weights = jnp.where(allowed, jnp.exp(scores - logs[t][:, :1]), 0.0)
        weight_grad = dot_nt(up, v_held[g])
        score_grad = (weights * (weight_grad - delta)).astype(low)
        query_held[t] = jnp.dot(score_grad, k_held[g], preferred_element_type=full) * scale
        total[g] += matmul_tn(query, score_grad) * scale
        total[KVH + g] += matmul_tn(up, weights.astype(low))

    heads_loop(HEADS // STACK, step)
    for j in range(D // (2 * HD)):
        pair = []
        for i in range(2):
            t, at = divmod(2 * j + i, STACK)
            pair.append(query_held[t, at * picks : (at + 1) * picks, :])
        pair = jnp.concatenate(pair, 1)
        raw[:, 2 * HD * j : 2 * HD * (j + 1)] = turned(pair, cosine[...], -sine[...]).astype(low)
    if sums:
        for g in range(0, 2 * KVH, 2):
            both = jnp.concatenate([total[g], total[g + 1]], 0)
            kv_grad[:, g * HD : (g + 2) * HD] = both.T
    direct_end(core, started, line_out, sems)


def attend_rows_back(his, grad, tables, places, kv, queries, held_out, logs, own):
    picks, keys = grad.shape[0], kv.shape[0]
    stacks, rows = HEADS // STACK, STACK * picks
    outside = keys > 4096
    by_head = (2 * KVH, HD, keys)
    raw, kv_grad, line_out = pallas.pallas_call(
        functools.partial(attend_back_body, his),
        out_shape=(
            jax.ShapeDtypeStruct((picks, D), low),
            jax.ShapeDtypeStruct(by_head if outside else (keys, 2 * KVH * HD), full),
            jax.ShapeDtypeStruct((2, his, *own.shape), low),
        ),
        in_specs=[pallas.BlockSpec(memory_space=pltpu.VMEM)] * 9,
        out_specs=(pallas.BlockSpec(memory_space=pltpu.VMEM),) * 2
        + (pallas.BlockSpec(memory_space=pallas.ANY),),
        scratch_shapes=[
            pltpu.VMEM((KVH, keys, HD), low),
            pltpu.VMEM((KVH, keys, HD), low),
            pltpu.VMEM((stacks, rows, HD), low),
            pltpu.VMEM((stacks, rows, HD), full),
            *direct_scratch(his),
        ]
        + ([] if outside else [pltpu.VMEM(by_head, full)]),
        compiler_params=pltpu.CompilerParams(
            collective_id=10, has_side_effects=True, vmem_limit_bytes=58 * 2**20
        ),
        cost_estimate=SMALL,
        name="attend_back",
    )(grad, *tables, places[:, None], kv, queries, held_out, logs, own)
    kv_grad = kv_grad.reshape(2 * KVH * HD, keys).T if outside else kv_grad
    return raw, kv_grad, line_out


def rows_body(his, far, near, start, got, looked, local_sem, y_sems, y_sems_in, seq_sems, seq_sems_in):
    core = Core(his)
    dp, s = lax.axis_index("dp"), lax.axis_index("seq")
    seqs = 2 * his
    core.ids["y"] = (dp + 2 - 4 * (dp // 2), s)
    for i in range(1, seqs):
        core.ids[f"seq{i}"] = (dp, lax.rem(s + i, seqs))
    core.meet("y", *(f"seq{i}" for i in range(1, seqs)))
    over, spread = [], []
    for i in range(seqs):
        to = lax.rem(s + i, seqs)
        over.append(core.copy(far.at[to], got.at[to], (y_sems, y_sems_in), i, "y"))
        over[i].start()
    here = None
    for i in [*range(1, seqs), 0]:
        to = lax.rem(s + i, seqs)
        over[i].wait_recv()

        def add(at, to=to):
            looked[to, at, :] = near[to, at, :] + got[to, at, :]

        by_rows(near.shape[1], add)
        if i:
            spread.append(
                core.copy(looked.at[to], start.at[s], (seq_sems, seq_sems_in), i - 1, f"seq{i}")
            )
            spread[-1].start()
        else:
            here = pltpu.make_async_copy(looked.at[s], start.at[s], local_sem)
            here.start()
    for copy in spread:
        copy.wait_recv()
    here.wait()
    sent(over + spread)


def gather_rows(his, far, near):
    seqs = 2 * his
    rows, columns = far.shape[0] // seqs, far.shape[1]
    far, near = (part.reshape(seqs, rows, columns) for part in (far, near))
    dma = pltpu.SemaphoreType.DMA
    start = pallas.pallas_call(
        functools.partial(rows_body, his),
        out_shape=jax.ShapeDtypeStruct((seqs, rows, columns), low),
        in_specs=[pallas.BlockSpec(memory_space=pltpu.VMEM)] * 2,
        out_specs=pallas.BlockSpec(memory_space=pallas.ANY),
        scratch_shapes=[
            pltpu.VMEM((seqs, rows, columns), low),
            pltpu.VMEM((seqs, rows, columns), low),
            dma,
            *[dma((count,)) for count in (seqs, seqs, seqs - 1, seqs - 1)],
        ],
        cost_estimate=SMALL,
        compiler_params=pltpu.CompilerParams(
            collective_id=11, has_side_effects=True, vmem_limit_bytes=32 * 2**20
        ),
        name="gather_rows",
    )(far, near)
    return jnp.transpose(start, (1, 0, 2)).reshape(rows, seqs * columns).astype(full)


def sum_body(his, rows, packed, out, bufs, got, send_sems, recv_sems):
    core = Core(his)
    dp, s = lax.axis_index("dp"), lax.axis_index("seq")
    ways = [("lo", 0)]
    bit = 1
    while bit < his:
        up = lax.rem(core.hi // bit, 2)
        core.ids[f"hi{bit}"] = (dp, s + 2 * bit * (1 - 2 * up))
        ways.append((f"hi{bit}", 0))
        bit *= 2
    y = dp // 2
    core.ids["y"] = (dp + 2 * (1 - 2 * y), s)
    ways += [("c", 1), ("y", 1)]
    core.meet(*(name for name, _ in ways))
    bufs[0] = packed[...]
    copies = []
    for j, (name, over_dp) in enumerate(ways):
        first = rows[0] if over_dp else 0
        last = rows[0] + rows[1] + (rows[2] if over_dp else 0)
        copy = core.copy(
            bufs.at[j, first:last], got.at[j, first:last], (send_sems, recv_sems), j, name
        )
        copy.start()
        copies.append(copy)
        copy.wait_recv()
        bufs[j + 1] = bufs[j]
        bufs[j + 1, first:last] = bufs[j, first:last] + got[j, first:last]
    out[...] = bufs[len(ways)]
    sent(copies)


def padded(parts):
    return [
        jnp.pad(part, (0, -part.shape[0] % 1024)).reshape(-1, 128) for part in parts
    ]


def sum_statistics(his, over_seq, over_all, over_dp):
    groups = [padded(parts) for parts in (over_seq, over_all, over_dp)]
    rows = tuple(sum(part.shape[0] for part in group) for group in groups)
    steps = 3 + his.bit_length() - 1
    total = sum(rows)
    dma = pltpu.SemaphoreType.DMA
    out = pallas.pallas_call(
        functools.partial(sum_body, his, rows),
        out_shape=jax.ShapeDtypeStruct((total, 128), full),
        in_specs=[pallas.BlockSpec(memory_space=pltpu.VMEM)],
        out_specs=pallas.BlockSpec(memory_space=pltpu.VMEM),
        scratch_shapes=[
            pltpu.VMEM((steps + 1, total, 128), full),
            pltpu.VMEM((steps, total, 128), full),
            dma((steps,)),
            dma((steps,)),
        ],
        compiler_params=pltpu.CompilerParams(
            collective_id=6, has_side_effects=True, vmem_limit_bytes=32 * 2**20
        ),
        name="sum_statistics",
    )(jnp.concatenate([part for group in groups for part in group], 0))
    results, at = [], 0
    for parts, group in zip((over_seq, over_all, over_dp), groups):
        for part, block in zip(parts, group):
            results.append(out[at : at + block.shape[0]].reshape(-1)[: part.shape[0]])
            at += block.shape[0]
    return results


def on_device(
    tok_ids,
    targets,
    positions,
    answer_mask,
    emb,
    head,
    attn_w,
    mlp_w,
    gains,
    emb_row,
    emb_col,
    head_row,
    head_col,
    attn_row,
    attn_col,
    mlp_row,
    mlp_col,
    gains_moment,
):
    pl = Place()
    seqs, his = pl.seqs, pl.his
    tokens = tok_ids.shape[1] // seqs
    picks = targets.shape[1] // seqs
    group = HEADS // KVH
    kv_width = KVH * HD
    block = D // (pl.dps * seqs)
    emb_n, emb_m = emb.shape
    line = 2 * his
    part = FF // line
    wide = 3 * part

    def swap_rows(rows, **way):
        return pl.send(rows.astype(low), **way)

    mlp_here, mlp_came = line_pairs(pl, split_columns(mlp_w, line))
    ids = jnp.concatenate([tok_ids.reshape(seqs, tokens), targets.reshape(seqs, picks)], 1)
    ids = ids.reshape(seqs * (tokens + picks))
    def look(wanted, *work):
        at = after(wanted, *work) - pl.dp * emb_n
        rows = jnp.take(emb, jnp.clip(at, 0, emb_n - 1), axis=0, mode="clip")
        return jnp.where(((at >= 0) & (at < emb_n))[:, None], rows, 0.0).astype(low)

    ids_y = pl.send(ids, dy=1)
    ids_c, ids_yc = pl.send(ids, dc=1), pl.send(ids, dy=1, dc=1)
    near_own = look(ids)
    ids_c, ids_y, ids_yc = after((ids_c, ids_y, ids_yc), near_own)
    mlp_came = after(mlp_came, near_own)
    far_other = look(ids_yc, mlp_came)
    mlp_got = line_sends(pl, mlp_here, mlp_came)
    far_got = pl.send(far_other, dc=1)
    near_other = look(ids_c, far_other)
    near_got = pl.send(near_other, dc=1)
    far_own = look(ids_y, near_other)
    far_sum = far_own + after(far_got, far_own)
    near_sum = near_own + after(near_got, far_own)

    attn_block = jnp.concatenate([attn_w, jnp.pad(gains.T, ((0, 0), (0, 125)))], 1).astype(low)
    attn_full = lax.all_gather(attn_block, ("dp", "seq"), axis=0, tiled=True)
    query_full, out_full = attn_full[:, :D], attn_full[:, QKV : QKV + D]
    kv_full = attn_full[:, D:QKV]
    gain_float = attn_full[:, QKV + D : QKV + D + 3].astype(full).T
    start = gather_rows(his, far_sum, near_sum)
    mlp_line = line_place(pl, after(mlp_got, start)).reshape(2, his, block, wide)
    mlp_x, mlp_y = pl.send(mlp_line, dlo=1), pl.send(mlp_line, dy=1)
    start = after(start, mlp_line)
    head_low = after(head, start).astype(low)
    emb_square_sum = jnp.sum(after(emb, start) ** 2)

    token_pos = pl.s * tokens + jnp.arange(tokens, dtype=jnp.int32)
    pick_pos = lax.dynamic_slice_in_dim(positions[0], pl.s * picks, picks)
    token_tables = turn_tables(*yarn_tables(token_pos.astype(full)))
    pick_tables = turn_tables(*yarn_tables(pick_pos.astype(full)))
    normed = rms_norm(start, gain_float[0]).astype(low)
    normed_tok, normed_pick = normed[:tokens], normed[tokens:]
    start_pick = start[tokens:]
    projected = matmul(normed_tok, kv_full)
    (kv_all,) = move(
        functools.partial(keys_body, his),
        0,
        [((his, 2, tokens, 2 * kv_width), low, pallas.ANY)],
        [projected, *token_tables],
        his,
        own=(tokens, 2 * kv_width),
        gathers=1,
    )
    kv_all = kv_all.reshape(seqs * tokens, 2 * kv_width)
    kv_all, mlp_x, mlp_y = lax.optimization_barrier((kv_all, mlp_x, mlp_y))
    raw = matmul(after(normed_pick, kv_all), query_full)
    mlp_far = (pl.send(mlp_x[0], dy=1), pl.send(mlp_y[1], dlo=1))
    head_rows = lax.all_gather(after(head_low, kv_all), "dp", axis=1, tiled=True)
    queries, attended_low, attended, log_total, pick_line = attend_rows(
        his, raw, pick_tables, pick_pos, kv_all, normed_pick
    )
    def shares(rows):
        return jnp.transpose(rows.reshape(picks, line, D // line), (1, 0, 2))

    middle = start_pick + matmul_nt(attended_low, out_full)
    normed_two, attended_share = move(
        functools.partial(norm_gather_body, his),
        1,
        [
            ((his, 2, picks, D), low, pallas.ANY),
            ((line, picks, D // line), low, pltpu.VMEM),
        ],
        [middle, gain_float[1:2], shares(attended_low)],
        his,
        own=(picks, D),
        gathers=1,
        swap=(his, picks, D // line),
    )
    normed_two = normed_two.reshape(line * picks, D)
    mlp_far = after(mlp_far, normed_two)
    mlp_full = assemble(mlp_line, mlp_x, mlp_y, *mlp_far).reshape(D, wide)
    gate_up = matmul(normed_two, mlp_full[:, : 2 * part])
    gate = gate_up[:, :part]
    upward = gate_up[:, part:]
    mixed = (jax.nn.silu(gate) * upward).astype(low)
    down = matmul_nt(mixed, mlp_full[:, 2 * part :])
    ending, chosen = move(
        functools.partial(ending_body, his),
        2,
        [((picks, D), full, pltpu.VMEM), ((his, 2, picks, D), low, pallas.ANY)],
        [down.reshape(his, 2, picks, D), middle, gain_float[2:3]],
        his,
        scatter=(picks, D),
        own=(picks, D),
        gathers=1,
    )
    chosen = chosen.reshape(seqs * picks, D)
    logits = matmul_nt(chosen, head_rows)
    vocab_part = head_rows.shape[0]
    target_hit = (
        targets[0][:, None]
        == pl.s * vocab_part + jnp.arange(vocab_part, dtype=jnp.int32)[None, :]
    )
    part_high = jnp.max(logits, 1)
    part_sum = jnp.sum(jnp.exp(logits - part_high[:, None]), 1)
    part_target = jnp.sum(jnp.where(target_hit, logits, 0.0), 1)
    stats = jnp.stack([part_high, part_sum, part_target])
    for step in pl.ways(("dlo", "hi")):
        other = step(stats)
        larger = jnp.maximum(stats[0], other[0])
        summed = stats[1] * jnp.exp(stats[0] - larger) + other[1] * jnp.exp(other[0] - larger)
        stats = jnp.stack([larger, summed, stats[2] + other[2]])
    all_high, all_sum_exp, target_logit = stats
    row_total = all_high + jnp.log(all_sum_exp)
    mask_float = answer_mask.astype(full)
    count = jnp.sum(mask_float)
    own_mask = lax.dynamic_slice_in_dim(mask_float, pl.dp, 1, 0)[0]
    loss_part = jnp.where(
        pl.s == 0,
        jnp.sum(own_mask * (row_total - target_logit + zloss_weight * row_total * row_total)),
        0.0,
    )
    probs = jnp.exp(logits - row_total[:, None])
    logit_grad = (
        (own_mask / count)[:, None]
        * (probs * (1.0 + 2.0 * zloss_weight * row_total)[:, None] - target_hit.astype(full))
    ).astype(low)
    chosen_part = matmul(logit_grad, head_rows)
    ending_grad, final_gain_grad, branch_grad = move(
        functools.partial(ending_back_body, his),
        3,
        [
            ((picks, D), full, pltpu.VMEM),
            ((1, D), full, pltpu.VMEM),
            ((his, 2, picks, D), low, pallas.ANY),
        ],
        [chosen_part.reshape(his, 2, picks, D), ending, gain_float[2:3]],
        his,
        scatter=(picks, D),
        own=(picks, D),
        gathers=1,
    )
    branch_grad = branch_grad.reshape(line * picks, D)
    mixed_grad = matmul(branch_grad, mlp_full[:, 2 * part :])
    sigmoid_gate = jax.nn.sigmoid(gate)
    gate_grad = mixed_grad * upward * sigmoid_gate * (1.0 + gate * (1.0 - sigmoid_gate))
    upward_grad = mixed_grad * gate * sigmoid_gate
    gate_up_grad = jnp.concatenate([gate_grad, upward_grad], 1).astype(low)
    middle_up = matmul_nt(gate_up_grad, mlp_full[:, : 2 * part])
    down_grad = matmul_tn(after(branch_grad, middle_up), mixed)
    mlp_term = jnp.concatenate([matmul_tn(normed_two, gate_up_grad), down_grad], 1)
    mlp_term = mlp_term.astype(low).reshape(2, 2, his, 2, block, wide)
    mlp_state = cross_start(pl, mlp_term)
    head_rows_grad = matmul_tn(after(logit_grad, mlp_term), chosen).astype(low)
    head_grad = lax.psum_scatter(head_rows_grad, "dp", scatter_dimension=1, tiled=True)
    middle_up = after(middle_up, mlp_term, head_rows_grad)
    middle_grad, attn_branch_grad, middle_gain_grad = move(
        functools.partial(middle_back_body, his),
        4,
        [
            ((picks, D), full, pltpu.VMEM),
            ((picks, D), low, pltpu.VMEM),
            ((1, D), full, pltpu.VMEM),
        ],
        [middle_up.reshape(his, 2, picks, D), middle, gain_float[1:2], ending_grad],
        his,
        scatter=(picks, D),
    )
    attended_grad = matmul(attn_branch_grad, out_full).astype(low)
    query_raw, kv_part, branch_line = attend_rows_back(
        his,
        attended_grad,
        pick_tables,
        pick_pos,
        kv_all,
        queries,
        attended,
        log_total,
        attn_branch_grad,
    )
    mlp_keep, mlp_sends = cross_next(pl, mlp_state, kv_part)
    kv_part = after(kv_part, mlp_keep, mlp_sends)
    kv_raw, query_share = move(
        functools.partial(keys_back_body, his),
        5,
        [
            ((tokens, 2 * kv_width), low, pltpu.VMEM),
            ((line, picks, D // line), low, pltpu.VMEM),
        ],
        [
            kv_part.reshape(his, 2, tokens, 2 * kv_width),
            *token_tables,
            shares(query_raw),
        ],
        his,
        swap=(his, picks, D // line),
        scatter=(tokens, 2 * kv_width),
        own=(tokens, 2 * kv_width),
        own_type=full,
    )
    mlp_state = cross_send(pl, mlp_keep, after(mlp_sends, kv_raw))
    pick_up = matmul_nt(query_raw, query_full)
    tok_up = matmul_nt(kv_raw, kv_full)
    start_part, start_gain_grad = norm_back(
        start, gain_float[0], jnp.concatenate([tok_up, pick_up], 0)
    )
    start_grad = jnp.concatenate(
        [start_part[:tokens], start_part[tokens:] + middle_grad], 0
    ).astype(low)

    back_rows = lax.all_to_all(start_grad, "seq", split_axis=1, concat_axis=0, tiled=True)
    branch_line, pick_line = after((branch_line, pick_line), start_grad)
    branch_line, pick_line = (
        part.reshape(line * picks, D) for part in (branch_line, pick_line)
    )
    query_term = jnp.concatenate(
        [
            matmul_tn(pick_line, query_share.reshape(line * picks, D // line)),
            matmul_tn(branch_line, attended_share.reshape(line * picks, D // line)),
        ],
        1,
    )
    query_term = query_term.astype(low).reshape(2, 2, his, 2, block, query_term.shape[-1])
    query_state = cross_start(pl, query_term)
    gains_term = jnp.stack([start_gain_grad, middle_gain_grad[0], final_gain_grad[0]], 1)

    def by_core(rows, core):
        rows = rows.reshape(rows.shape[0], 2, 2, seqs * block)
        return pick(rows, core, 2).reshape(rows.shape[0], D // 2)

    def grid(rows):
        return rows.astype(low).reshape(2, his, 2, block, rows.shape[-1])

    def token_term(core):
        return jnp.concatenate(
            [
                matmul_tn(by_core(after(normed_tok, start_grad), core), kv_raw),
                jnp.pad(by_core(gains_term.T, core).T, ((0, 0), (0, 125))),
            ],
            1,
        )

    token_got = pl.send(token_term(1 - pl.c).astype(low), dc=1)
    token_keep = token_term(pl.c)
    other_squares = [jnp.sum(after(w, token_keep) ** 2) for w in (attn_w, mlp_w, head)]
    early = [
        loss_part,
        jnp.sum(attn_row),
        *other_squares,
        jnp.where(pl.s == 0, jnp.sum(emb_row), 0.0),
        emb_square_sum,
        jnp.where(pl.dp == 0, jnp.sum(head_row), 0.0),
        jnp.sum(gains * gains),
        jnp.sum(mlp_row),
    ]
    slot = jnp.arange(128, dtype=jnp.int32)
    early = sum(jnp.where(slot == i, value, 0.0) for i, value in enumerate(early))
    mlp_term = cross_end(pl, mlp_state, early)
    mlp_here, mlp_came = line_pairs(pl, mlp_term)
    back_rows, early = lax.optimization_barrier((back_rows, early, mlp_term, query_term))[:2]
    back_got = pl.send(back_rows, dy=1)
    token_sum = grid(token_keep + after(token_got, back_rows).astype(full))
    token_got = pl.send(pick(token_sum, 1 - pl.y, 0), dy=1)

    def on_chip(wanted):
        local, other = wanted - pl.dp * emb_n, wanted - (pl.dp ^ 1) * emb_n
        return jnp.where(
            (local >= 0) & (local < emb_n),
            local,
            jnp.where((other >= 0) & (other < emb_n), other + emb_n, 2 * emb_n),
        )

    places_in = on_chip(ids), on_chip(ids_y)
    chip_grad = (
        jnp.zeros((2 * emb_n + 8, emb_m), full)
        .at[places_in[0]]
        .add(after(back_rows, token_sum, mlp_came).astype(full))
    )
    mlp_got = line_sends(pl, mlp_here, after(mlp_came, token_sum))
    near, far = mlp_got[1:2] + mlp_got[-1:], mlp_got[2:-1]
    query_state = cross_send(pl, *cross_next(pl, query_state, chip_grad))
    head_grad = after(head_grad, query_state[:2], near[0]).astype(full)
    head_square = head_grad * head_grad + eps_square
    head_rows_sum = jnp.sum(head_square, 1)
    head_cols_sum = jnp.sum(head_square, 0)
    back_got = after(back_got, near[1:], head_rows_sum, head_cols_sum)
    chip_grad = chip_grad.at[places_in[1]].add(back_got.astype(full))
    token_sum = pick(token_sum, pl.y, 0).astype(full) + after(token_got, chip_grad).astype(full)
    token_got = pl.send(pick(token_sum, 1 - pl.lo, 1).astype(low), dlo=1)
    emb_part = after(chip_grad, far, token_sum)[emb_n : 2 * emb_n].astype(low)
    emb_got = pl.send(emb_part, dc=1)
    query_term = cross_end(pl, query_state, emb_part)
    token_sum = pick(token_sum, pl.lo, 1) + after(token_got, emb_part).astype(full)
    mlp_grad, mlp_rows, mlp_cols = join_columns(line_place(pl, after(mlp_got, query_term)))
    mlp_row_new = decay_rate * mlp_row + (1.0 - decay_rate) * mlp_rows / (3 * FF)
    emb_grad = chip_grad[:emb_n] + after(emb_got, query_term, token_sum).astype(full)
    emb_square = emb_grad * emb_grad + eps_square
    emb_rows, emb_cols = jnp.sum(emb_square, 1), jnp.sum(emb_square, 0)
    attn_grad, gains_grad, attn_rows, attn_cols = layer_gradient(
        his, after(query_term, emb_rows), token_sum
    )
    gains_grad = gains_grad[:, :3].T
    attn_row_new = decay_rate * attn_row + (1.0 - decay_rate) * attn_rows[:, 0] / (QKV + D)
    scalars = early
    for at, value in ((10, emb_cols), (11, head_cols_sum)):
        scalars = scalars + jnp.where(slot == at, jnp.sum(value), 0.0)
    (
        emb_row_sum,
        head_col_sum,
        attn_cols_sum,
        mlp_cols_sum,
        totals,
        head_row_sum,
        emb_col_sum,
    ) = sum_statistics(
        his,
        (emb_rows, head_cols_sum),
        (attn_cols[0], mlp_cols, scalars),
        (head_rows_sum, emb_cols),
    )
    attn_row_total = decay_rate * totals[1] + (1.0 - decay_rate) * jnp.sum(attn_cols_sum) / (QKV + D)
    mlp_row_total = decay_rate * totals[9] + (1.0 - decay_rate) * jnp.sum(mlp_cols_sum) / (3 * FF)
    emb_row_total, head_row_total = totals[10], totals[11]

    attn_col_new = decay_rate * attn_col + (1.0 - decay_rate) * attn_cols_sum / D
    mlp_col_new = decay_rate * mlp_col + (1.0 - decay_rate) * mlp_cols_sum / D
    attn_update = attn_grad * lax.rsqrt(
        attn_row_new[:, None] * attn_col_new[None, :] / (attn_row_total / D)
    )
    mlp_update = mlp_grad * lax.rsqrt(
        mlp_row_new[:, None] * mlp_col_new[None, :] / (mlp_row_total / D)
    )
    emb_row_new = decay_rate * emb_row + (1.0 - decay_rate) * emb_row_sum / D
    emb_col_new = decay_rate * emb_col + (1.0 - decay_rate) * emb_col_sum / VOCAB
    emb_mean = (decay_rate * totals[5] + (1.0 - decay_rate) * emb_row_total / D) / VOCAB
    emb_update = emb_grad * lax.rsqrt(emb_row_new[:, None] * emb_col_new[None, :] / emb_mean)
    head_row_new = decay_rate * head_row + (1.0 - decay_rate) * head_row_sum / D
    head_col_new = decay_rate * head_col + (1.0 - decay_rate) * head_col_sum / VOCAB
    head_mean = (decay_rate * totals[7] + (1.0 - decay_rate) * head_row_total / D) / VOCAB
    head_update = head_grad * lax.rsqrt(head_row_new[:, None] * head_col_new[None, :] / head_mean)
    moment_new = decay_rate * gains_moment + (1.0 - decay_rate) * (
        gains_grad * gains_grad + eps_square
    )
    gains_update = gains_grad * lax.rsqrt(moment_new)
    attn_new = finish(attn_w, attn_update, totals[2], D * (QKV + D))
    mlp_new = finish(mlp_w, mlp_update, totals[3], D * 3 * FF)
    emb_new = finish(emb, emb_update, totals[6], VOCAB * D)
    head_new = finish(head, head_update, totals[4], VOCAB * D)
    gains_new = finish(gains, gains_update, totals[8], 3 * D)
    return (
        totals[0],
        count,
        emb_grad,
        emb_new,
        emb_row_new,
        emb_col_new,
        head_grad,
        head_new,
        head_row_new,
        head_col_new,
        attn_grad,
        attn_new,
        attn_row_new,
        attn_col_new,
        mlp_grad,
        mlp_new,
        mlp_row_new,
        mlp_col_new,
        gains_grad,
        moment_new,
        gains_new,
    )


def solution(mesh):
    return jax.shard_map(
        on_device,
        mesh=mesh,
        in_specs=(
            P("dp", None),
            P("dp", None),
            P("dp", None),
            P(),
            P("dp", "seq"),
            P("seq", "dp"),
            P(("dp", "seq"), None),
            P(("dp", "seq"), None),
            P(None, ("dp", "seq")),
            P("dp"),
            P("seq"),
            P("seq"),
            P("dp"),
            P(("dp", "seq")),
            P(),
            P(("dp", "seq")),
            P(),
            P(None, ("dp", "seq")),
        ),
        out_specs=(
            P(),
            P(),
            P("dp", "seq"),
            P("dp", "seq"),
            P("dp"),
            P("seq"),
            P("seq", "dp"),
            P("seq", "dp"),
            P("seq"),
            P("dp"),
            P(("dp", "seq"), None),
            P(("dp", "seq"), None),
            P(("dp", "seq")),
            P(),
            P(("dp", "seq"), None),
            P(("dp", "seq"), None),
            P(("dp", "seq")),
            P(),
            P(None, ("dp", "seq")),
            P(None, ("dp", "seq")),
            P(None, ("dp", "seq")),
        ),
        check_vma=False,
    )
```

```python
import functools
import math

import jax
import jax.numpy as jnp
from jax import lax
from jax.experimental import pallas
from jax.experimental.pallas import tpu as pltpu
from jax.sharding import PartitionSpec as P

D = 2048
HEADS = 32
KVH = 4
HD = 64
FF = 5632
VOCAB = 32000
QKV = 2560


eps_norm = 1e-05
eps_square = 1e-30
decay_rate = 0.5
learn_rate = 1.0
zloss_weight = 0.0001
orig_context = 2048.0
yarn_factor = 4.0
highest = lax.Precision.HIGHEST


def yarn_tables(places):
    halves = jnp.arange(HD // 2, dtype=jnp.float32)
    inverse = jnp.power(10000.0, -2.0 * halves / HD)
    ratio = orig_context * inverse / (2.0 * math.pi)
    ramp_part = jnp.clip((ratio - 1.0) / 31.0, 0.0, 1.0)
    frequency = inverse / yarn_factor * (1.0 - ramp_part) + inverse * ramp_part
    angles = places[:, None] * frequency[None, :]
    magnitude = 0.1 * math.log(yarn_factor) + 1.0
    return (jnp.cos(angles) * magnitude, jnp.sin(angles) * magnitude)


def rotate(values, cosine, sine):
    first = values[..., : HD // 2]
    second = values[..., HD // 2 :]
    cosine_row = cosine[:, None, :]
    sine_row = sine[:, None, :]
    return jnp.concatenate(
        [first * cosine_row - second * sine_row, second * cosine_row + first * sine_row], -1
    )


def unrotate(values, cosine, sine):
    first = values[..., : HD // 2]
    second = values[..., HD // 2 :]
    cosine_row = cosine[:, None, :]
    sine_row = sine[:, None, :]
    return jnp.concatenate(
        [first * cosine_row + second * sine_row, second * cosine_row - first * sine_row], -1
    )


def rms_norm(values, gain_row):
    return values * lax.rsqrt(jnp.mean(values * values, -1, keepdims=True) + eps_norm) * gain_row


def norm_back(values, gain_row, upstream):
    factor = lax.rsqrt(jnp.mean(values * values, -1, keepdims=True) + eps_norm)
    normed = values * factor
    gain_grad = jnp.sum(upstream * normed, 0)
    inner = upstream * gain_row
    return (factor * (inner - normed * jnp.mean(inner * normed, -1, keepdims=True)), gain_grad)


def matmul(left, right):
    return jnp.dot(left, right, preferred_element_type=jnp.float32)


def matmul_nt(left, right):
    return lax.dot_general(
        left, right, (((1,), (1,)), ((), ())), preferred_element_type=jnp.float32
    )


def matmul_tn(left, right):
    return lax.dot_general(
        left, right, (((0,), (0,)), ((), ())), preferred_element_type=jnp.float32
    )


def finish(weight, update, weight_square, entries):
    return weight - learn_rate * jnp.maximum(0.001, jnp.sqrt(weight_square / entries)) * update


low = jnp.bfloat16
full = jnp.float32


class Place:
    def __init__(self):
        self.seqs = lax.axis_size("seq")
        self.dps = lax.axis_size("dp")
        self.dp = lax.axis_index("dp")
        self.s = lax.axis_index("seq")
        self.his = self.seqs // 2
        self.y, self.c = self.dp // 2, self.dp % 2
        self.hi, self.lo = self.s // 2, self.s % 2

    def send(self, value, dy=0, dc=0, dlo=0, up=0):
        pairs = []
        for d in range(self.dps):
            for s in range(self.seqs):
                to_d = d ^ (2 * dy + dc)
                to_s = ((s // 2 + up) % self.his) * 2 + ((s % 2) ^ dlo)
                pairs.append((d * self.seqs + s, to_d * self.seqs + to_s))
        return lax.ppermute(value, ("dp", "seq"), pairs)

    def ways(self, names):
        steps = []
        for name in names:
            if name == "hi":
                bit = 1
                while bit < self.his:
                    steps.append(lambda value, bit=bit: self.swap_hi(value, bit))
                    bit *= 2
            else:
                steps.append(lambda value, name=name: self.send(value, **{name: 1}))
        return steps

    def swap_hi(self, value, bit):
        pairs = []
        for d in range(self.dps):
            for s in range(self.seqs):
                pairs.append((d * self.seqs + s, d * self.seqs + (s ^ (2 * bit))))
        return lax.ppermute(value, ("dp", "seq"), pairs)


def after(value, *events):
    return lax.optimization_barrier((value, *events))[0] if events else value


def pick(array, index, axis):
    return lax.dynamic_index_in_dim(array, index, axis, keepdims=False)


def put(array, block, index, axis):
    return lax.dynamic_update_slice_in_dim(array, jnp.expand_dims(block, axis), index, axis)


def line_pairs(pl, blocks):
    grid = blocks.reshape(2, pl.his, *blocks.shape[1:])
    return pick(grid, pl.c, 0), pl.send(pick(grid, 1 - pl.c, 0), dc=1)


def line_sends(pl, here, came):
    pairs = jnp.stack([here, came], 1)
    got = []
    for k in range(pl.his):
        pair = pick(pairs, (pl.hi + k) % pl.his, 0)
        got.append(pl.send(pair, up=k) if k else pair)
    return got


def place_body(*refs):
    pairs, out, sems = refs[:-2], refs[-2], refs[-1]
    n = len(pairs)
    dp, s = lax.axis_index("dp"), lax.axis_index("seq")
    c, hi = dp % 2, s // 2
    copies = []
    for k, pair in enumerate(pairs):
        for j, side in enumerate((c, 1 - c)):
            copies.append(
                pltpu.make_async_copy(
                    pair.at[j], out.at[side * n + lax.rem(hi + n - k, n)], sems.at[2 * k + j]
                )
            )
            copies[-1].start()
    for copy in copies:
        copy.wait()


def line_place(pl, got):
    count = len(got)
    shape = (2 * count, *got[0].shape[1:])
    return pallas.pallas_call(
        place_body,
        out_shape=jax.ShapeDtypeStruct(shape, got[0].dtype),
        in_specs=[pallas.BlockSpec(memory_space=pallas.ANY)] * count,
        out_specs=pallas.BlockSpec(memory_space=pltpu.VMEM),
        scratch_shapes=[pltpu.SemaphoreType.DMA((2 * count,))],
        cost_estimate=SMALL,
        name="line_place",
    )(*got)


def assemble_body(line, over_x, over_y, far_a, far_b, out, sems):
    dp, s = lax.axis_index("dp"), lax.axis_index("seq")
    y, lo = dp // 2, s % 2
    his = line.shape[1]
    copies = []
    for c in range(2):
        for h in range(his):
            for block, at_y, at_lo in (
                (line.at[c, h], y, lo),
                (over_x.at[c, h], y, 1 - lo),
                (over_y.at[c, h], 1 - y, lo),
                ((far_b if c else far_a).at[h], 1 - y, 1 - lo),
            ):
                copies.append(
                    pltpu.make_async_copy(
                        block, out.at[at_y, c, h, at_lo], sems.at[len(copies)]
                    )
                )
                copies[-1].start()
    for copy in copies:
        copy.wait()


def assemble(line, over_x, over_y, far_a, far_b):
    two, his, rows, columns = line.shape
    return pallas.pallas_call(
        assemble_body,
        out_shape=jax.ShapeDtypeStruct((2, two, his, 2, rows, columns), line.dtype),
        in_specs=[pallas.BlockSpec(memory_space=pallas.ANY)] * 5,
        out_specs=pallas.BlockSpec(memory_space=pltpu.VMEM),
        scratch_shapes=[pltpu.SemaphoreType.DMA((8 * his,))],
        cost_estimate=SMALL,
        compiler_params=pltpu.CompilerParams(vmem_limit_bytes=32 * 2**20),
        name="assemble",
    )(line, over_x, over_y, far_a, far_b)


def cross_start(pl, term):
    a, b = term[:, 0], term[:, 1]
    got_a = pl.send(pick(a, 1 - pl.y, 0), dy=1)
    got_b = pl.send(pick(b, 1 - pl.lo, 2), dlo=1)
    return a, b, got_a, got_b


def cross_next(pl, state, *work):
    a, b, got_a, got_b = state
    got_a, got_b = after((got_a, got_b), *work)
    a = pick(a, pl.y, 0).astype(full) + got_a.astype(full)
    b = pick(b, pl.lo, 2).astype(full) + got_b.astype(full)
    send_a = pick(a, 1 - pl.lo, 1).astype(low)
    send_b = pick(b, 1 - pl.y, 0).astype(low)
    keep = pick(a, pl.lo, 1), pick(b, pl.y, 0)
    return keep, (send_a, send_b)


def cross_send(pl, keep, sends):
    return *keep, pl.send(sends[0], dlo=1), pl.send(sends[1], dy=1)


def cross_end(pl, state, *work):
    a, b, got_a, got_b = state
    got_a, got_b = after((got_a, got_b), *work)
    a = (a + got_a.astype(full)).astype(low)
    b = (b + got_b.astype(full)).astype(low)
    return jnp.stack([a, b]).reshape(2 * pl.his, *a.shape[1:])


def split_kernel(line, part, in_ref, out_ref):
    for j in range(3):
        for t in range(line):
            at = (j * line + t) * part
            out_ref[t, :, j * part : (j + 1) * part] = in_ref[:, at : at + part].astype(low)


def split_columns(weight, line):
    rows, columns = weight.shape
    part = columns // (3 * line)
    return pallas.pallas_call(
        lambda *refs: split_kernel(line, part, *refs),
        out_shape=jax.ShapeDtypeStruct((line, rows, 3 * part), low),
        in_specs=[pallas.BlockSpec(memory_space=pltpu.VMEM)],
        out_specs=pallas.BlockSpec(memory_space=pltpu.VMEM),
        compiler_params=pltpu.CompilerParams(vmem_limit_bytes=40 * 2**20),
        name="split_columns",
    )(weight)


def join_kernel(line, part, in_ref, out_ref, rows_ref, columns_ref):
    total = jnp.zeros(rows_ref.shape, full)
    for j in range(3):
        for t in range(line):
            at = (j * line + t) * part
            block = in_ref[t, :, j * part : (j + 1) * part].astype(full)
            out_ref[:, at : at + part] = block
            square = block * block + eps_square
            columns_ref[:, at : at + part] = jnp.sum(square, 0, keepdims=True)
            total = total + jnp.sum(square, 1, keepdims=True)
    rows_ref[...] = total


def join_columns(blocks):
    line, rows, wide = blocks.shape
    part = wide // 3
    grad, row_sum, column_sum = pallas.pallas_call(
        lambda *refs: join_kernel(line, part, *refs),
        out_shape=(
            jax.ShapeDtypeStruct((rows, line * wide), full),
            jax.ShapeDtypeStruct((rows, 1), full),
            jax.ShapeDtypeStruct((1, line * wide), full),
        ),
        in_specs=[pallas.BlockSpec(memory_space=pltpu.VMEM)],
        out_specs=(pallas.BlockSpec(memory_space=pltpu.VMEM),) * 3,
        compiler_params=pltpu.CompilerParams(vmem_limit_bytes=40 * 2**20),
        name="join_columns",
    )(blocks)
    return grad, row_sum[:, 0], column_sum[0]


def halve(pl, part, mine, axis, **way):
    got = pl.send(pick(part, 1 - mine, axis).astype(low), **way)
    return pick(part, mine, axis).astype(full) + got.astype(full)


def hi_sum(pl, part, *work):
    total = pick(part, pl.hi, 0).astype(full)
    for k in range(1, pl.his):
        block = pick(part, (pl.hi + k) % pl.his, 0).astype(low)
        total = total + after(pl.send(block, up=k), *work).astype(full)
    return total


MESH = pallas.DeviceIdType.MESH
ROWS = 16
SMALL = pallas.CostEstimate(flops=1024, bytes_accessed=1024, transcendentals=0)


class Core:
    def __init__(self, his):
        dp, s = lax.axis_index("dp"), lax.axis_index("seq")
        self.his = his
        self.hi, self.lo, self.c = s // 2, s % 2, dp % 2
        self.side = {"c": self.c, "lo": self.lo}
        self.across = [
            (dp, lax.rem(self.hi + k, his) * 2 + self.lo) for k in range(his)
        ]
        self.ids = {
            "c": (dp + 1 - 2 * self.c, s),
            "lo": (dp, s + 1 - 2 * self.lo),
            "up": (dp, lax.rem(self.hi + 1, his) * 2 + self.lo),
            "down": (dp, lax.rem(self.hi + his - 1, his) * 2 + self.lo),
        }

    def meet(self, *names):
        others = [self.ids[name] for name in names if name != "line"]
        if "line" in names:
            others += self.across[1:]
        barrier = pltpu.get_barrier_semaphore()
        for other in others:
            pallas.semaphore_signal(barrier, inc=1, device_id=other, device_id_type=MESH)
        pallas.semaphore_wait(barrier, len(others))

    def copy(self, source, target, sems, at, name):
        return pltpu.make_async_remote_copy(
            src_ref=source,
            dst_ref=target,
            send_sem=sems[0].at[at],
            recv_sem=sems[1].at[at],
            device_id=self.ids[name] if isinstance(name, str) else self.across[name],
            device_id_type=MESH,
        )


def by_rows(n, step):
    def one(i, carry):
        step(pallas.ds(pallas.multiple_of(i * ROWS, ROWS), ROWS))
        return carry

    lax.fori_loop(0, n // ROWS, one, 0)


def kernel_scatter(core, name, part, total, held, side_sems, up_sems, beside=iter(())):
    his, side = core.his, core.side[name]
    side_out, side_in, up_out, up_in = held
    n = part.shape[2]
    over = []
    for j in range(his):
        h = lax.rem(core.hi + 2 * his - 1 - j, his)

        def cast(at, j=j, h=h):
            side_out[j, at, :] = part[h, 1 - side, at, :].astype(low)

        by_rows(n, cast)
        over.append(core.copy(side_out.at[j], side_in.at[j], side_sems, j, name))
        over[j].start()
    climb = []
    for j in range(his):
        h = lax.rem(core.hi + 2 * his - 1 - j, his)
        over[j].wait_recv()
        if j:
            climb[j - 1].wait_recv()

        def add(at, j=j, h=h):
            acc = part[h, side, at, :].astype(full) + side_in[j, at, :].astype(full)
            if j:
                acc = acc + up_in[j - 1, at, :].astype(full)
            if j < his - 1:
                up_out[j, at, :] = acc.astype(low)
            else:
                total[at, :] = acc

        by_rows(n, add)
        if j < his - 1:
            climb.append(core.copy(up_out.at[j], up_in.at[j], up_sems, j, "up"))
            climb[j].start()
        next(beside, None)
    return over + climb


def gather_steps(core, name, own, out, copies, sems, side_first=False):
    his, side = core.his, core.side[name]
    local_sem, side_sems, up_sems = sems[0], sems[1:3], sems[3:5]

    def slot(h):
        return out.at[side, h] if side_first else out.at[h, side]

    here = pltpu.make_async_copy(own, slot(core.hi), local_sem)
    here.start()
    over, climb = [], []
    for j in range(his):
        block = slot(lax.rem(core.hi + his - j, his))
        source = own if j == 0 else block
        if j:
            climb[j - 1].wait_recv()
        if j < his - 1:
            climb.append(core.copy(source, block, up_sems, j, "up"))
            climb[j].start()
        over.append(core.copy(source, block, side_sems, j, name))
        over[j].start()
        yield
    for copy in over:
        copy.wait_recv()
    here.wait()
    copies += over + climb


def kernel_gather(*args, **kwargs):
    for _ in gather_steps(*args, **kwargs):
        pass


def direct_start(core, own, out, sems):
    here = pltpu.make_async_copy(own, out.at[core.c, core.hi], sems[0])
    place = out.at[core.c, core.hi]
    climb = [core.copy(own, place, sems[3:5], k - 1, k) for k in range(1, core.his)]
    over = [core.copy(own, place, sems[1:3], 0, "c")]
    for copy in [here, *climb, *over]:
        copy.start()
    return here, climb, over


def direct_end(core, started, out, sems):
    here, climb, over = started
    order = sorted(range(1, core.his), key=lambda k: min(k, core.his - k))
    for k in order:
        climb[k - 1].wait_recv()
        block = out.at[core.c, lax.rem(core.hi + core.his - k, core.his)]
        over.append(core.copy(block, block, sems[1:3], k, "c"))
        over[-1].start()
    for copy in over:
        copy.wait_recv()
    here.wait()
    sent(climb + over)


def direct_scratch(his):
    dma = pltpu.SemaphoreType.DMA
    return [dma, dma((his,)), dma((his,)), dma((his - 1,)), dma((his - 1,))]


def kernel_swap_start(core, blocks, came, side_sems):
    his = core.his
    over = core.copy(
        blocks.at[pallas.ds((1 - core.c) * his, his)], came, side_sems, 0, "c"
    )
    over.start()
    return over


def kernel_swap_end(core, over, blocks, came, out, local_sems, up_sems):
    his, c, hi = core.his, core.c, core.hi
    mine, theirs = c * his + hi, (1 - c) * his + hi
    here = [pltpu.make_async_copy(blocks.at[mine], out.at[mine], local_sems.at[0])]
    climb = []
    for k in range(1, his):
        to = lax.rem(hi + k, his)
        climb.append(core.copy(blocks.at[c * his + to], out.at[mine], up_sems, 2 * k - 2, k))
    over.wait_recv()
    here.append(pltpu.make_async_copy(came.at[hi], out.at[theirs], local_sems.at[1]))
    for k in range(1, his):
        to = lax.rem(hi + k, his)
        climb.append(core.copy(came.at[to], out.at[theirs], up_sems, 2 * k - 1, k))
    for copy in here + climb:
        copy.start()
    return here, [over] + climb


def swap_done(here, copies):
    for copy in here:
        copy.wait()
    for copy in copies[1:]:
        copy.wait_recv()


def sent(copies):
    for copy in copies:
        copy.wait_send()


def norm_rows(values, gain):
    return values * lax.rsqrt(jnp.mean(values * values, -1, keepdims=True) + eps_norm) * gain


def norm_rows_back(values, gain, upstream):
    factor = lax.rsqrt(jnp.mean(values * values, -1, keepdims=True) + eps_norm)
    normed = values * factor
    inner = upstream * gain
    back = factor * (inner - normed * jnp.mean(inner * normed, -1, keepdims=True))
    return back, jnp.sum(upstream * normed, 0, keepdims=True)


def norm_gather_body(his, values, gain, blocks, out, swapped, came, own, *sems):
    core = Core(his)
    by_rows(
        values.shape[0],
        lambda at: own.__setitem__(
            (at, slice(None)), norm_rows(values[at, :], gain[...]).astype(low)
        ),
    )
    core.meet("c", "line")
    over = kernel_swap_start(core, blocks, came, sems[1:3])
    copies = []
    kernel_gather(core, "c", own, out, copies, sems[5:10])
    here, more = kernel_swap_end(core, over, blocks, came, swapped, sems[0], sems[3:5])
    swap_done(here, more)
    sent(copies + more)


def turn_keys(source, cosine, sine, target):
    width = KVH * HD
    for at in range(0, width, 2 * HD):
        pair = turned(source[:, at : at + 2 * HD], cosine, sine)
        target[:, at : at + 2 * HD] = pair.astype(low)
    target[:, width:] = source[:, width:].astype(low)


def keys_body(his, projected, cosine, sine, out, own, *sems):
    core = Core(his)
    turn_keys(projected, cosine[...], sine[...], own)
    core.meet("lo", "up", "down")
    copies = []
    kernel_gather(core, "lo", own, out, copies, sems)
    sent(copies)


def keys_back_body(
    his, part, cosine, sine, blocks, out, swapped, came, total, *rest
):
    swap_sems, held, sems = rest[:5], rest[5:9], rest[9:13]
    core = Core(his)
    core.meet("c", "lo", "line")
    over = kernel_swap_start(core, blocks, came, swap_sems[1:3])
    copies = []
    copies += kernel_scatter(core, "lo", part, total, held, sems[0:2], sems[2:4])
    here, more = kernel_swap_end(core, over, blocks, came, swapped, swap_sems[0], swap_sems[3:5])
    turn_keys(total, cosine[...], -sine[...], out)
    swap_done(here, more)
    sent(copies + more)


def layer_body(his, blocks, tokens, grad, gains, rows, columns, swapped, came, out_low, in_low, *sems):
    core = Core(his)
    wide = blocks.shape[2] // 2
    side, keys = 2 * his, 2 * KVH * HD
    core.meet("c", "line")
    over = kernel_swap_start(core, blocks, came, sems[1:3])
    climb = []
    for k in range(1, his):
        to = lax.rem(core.hi + k, his)
        out_low[k - 1] = tokens[to].astype(low)
        climb.append(core.copy(out_low.at[k - 1], in_low.at[k - 1], sems[5:7], k - 1, k))
        climb[-1].start()
    here, more = kernel_swap_end(core, over, blocks, came, swapped, sems[0], sems[3:5])
    total = tokens[core.hi]
    for k, copy in enumerate(climb):
        copy.wait_recv()
        total = total + in_low[k].astype(full)
    gains[...] = total[:, keys:]
    row_sum = jnp.zeros(rows.shape, full)
    pieces = [(D, total[:, :keys])]
    swap_done(here, more)
    for t in range(side):
        pieces.append((t * wide, swapped[t, :, :wide].astype(full)))
        pieces.append((QKV + t * wide, swapped[t, :, wide:].astype(full)))
    for at, piece in pieces:
        till = at + piece.shape[1]
        grad[:, at:till] = piece
        square = piece * piece + eps_square
        columns[:, at:till] = jnp.sum(square, 0, keepdims=True)
        row_sum = row_sum + jnp.sum(square, 1, keepdims=True)
    rows[...] = row_sum
    sent(climb + more)


def layer_gradient(his, blocks, tokens):
    line, rows, columns = blocks.shape
    extra = tokens.shape[2] - 2 * KVH * HD
    dma = pltpu.SemaphoreType.DMA
    return pallas.pallas_call(
        functools.partial(layer_body, his),
        out_shape=(
            jax.ShapeDtypeStruct((rows, QKV + D), full),
            jax.ShapeDtypeStruct((rows, extra), full),
            jax.ShapeDtypeStruct((rows, 1), full),
            jax.ShapeDtypeStruct((1, QKV + D), full),
        ),
        in_specs=[pallas.BlockSpec(memory_space=pltpu.VMEM)] * 2,
        out_specs=(pallas.BlockSpec(memory_space=pltpu.VMEM),) * 4,
        scratch_shapes=[
            pltpu.VMEM(blocks.shape, low),
            pltpu.VMEM((his, rows, columns), low),
            pltpu.VMEM((his - 1, *tokens.shape[1:]), low),
            pltpu.VMEM((his - 1, *tokens.shape[1:]), low),
            dma((2,)),
            *[dma((count,)) for count in (1, 1, 2 * his - 2, 2 * his - 2, his - 1, his - 1)],
        ],
        cost_estimate=SMALL,
        compiler_params=pltpu.CompilerParams(
            collective_id=7, has_side_effects=True, vmem_limit_bytes=32 * 2**20
        ),
        name="layer_gradient",
    )(blocks, tokens)


def ending_body(his, part, middle, gain, ending, chosen, own, *rest):
    held, sems = rest[:4], rest[4:]
    core = Core(his)
    core.meet("c", "lo", "up", "down")
    copies = kernel_scatter(core, "c", part, ending, held, sems[0:2], sems[2:4])

    def finish_rows(at):
        values = ending[at, :] + middle[at, :]
        ending[at, :] = values
        own[at, :] = norm_rows(values, gain[...]).astype(low)

    by_rows(middle.shape[0], finish_rows)
    kernel_gather(core, "lo", own, chosen, copies, sems[4:9])
    sent(copies)


def ending_back_body(his, part, ending, gain, grad, gain_grad, branch, own, *rest):
    held, sems = rest[:4], rest[4:]
    core = Core(his)
    core.meet("c", "lo", "up", "down")
    copies = kernel_scatter(core, "lo", part, grad, held, sems[0:2], sems[2:4])
    gain_grad[...] = jnp.zeros(gain_grad.shape, full)

    def back_rows(at):
        back, gained = norm_rows_back(ending[at, :], gain[...], grad[at, :])
        grad[at, :] = back
        own[at, :] = back.astype(low)
        gain_grad[...] += gained

    by_rows(ending.shape[0], back_rows)
    kernel_gather(core, "c", own, branch, copies, sems[4:9])
    sent(copies)


def middle_back_body(his, part, middle, gain, ending_grad, grad, grad_low, gain_grad, *rest):
    held, sems = rest[:4], rest[4:]
    core = Core(his)
    core.meet("c", "up", "down")
    copies = kernel_scatter(core, "c", part, grad, held, sems[0:2], sems[2:4])
    gain_grad[...] = jnp.zeros(gain_grad.shape, full)

    def back_rows(at):
        back, gained = norm_rows_back(middle[at, :], gain[...], grad[at, :])
        back = back + ending_grad[at, :]
        grad[at, :] = back
        grad_low[at, :] = back.astype(low)
        gain_grad[...] += gained

    by_rows(middle.shape[0], back_rows)
    sent(copies)


def move(body, collective_id, outs, args, his, scatter=None, own=None, own_type=low, gathers=0, swap=None):
    dma = pltpu.SemaphoreType.DMA
    scratch = []
    if swap:
        scratch.append(pltpu.VMEM(swap, low))
    if own:
        scratch.append(pltpu.VMEM(own, own_type))
    if swap:
        scratch += [dma((2,))]
        scratch += [dma((count,)) for count in (1, 1, 2 * his - 2, 2 * his - 2)]
    if scatter:
        scratch += [pltpu.VMEM((count, *scatter), low) for count in (his, his, his - 1, his - 1)]
        scratch += [dma((his,)), dma((his,)), dma((his - 1,)), dma((his - 1,))]
    for _ in range(gathers):
        scratch += [dma, dma((his,)), dma((his,)), dma((his - 1,)), dma((his - 1,))]
    return pallas.pallas_call(
        body,
        out_shape=tuple(jax.ShapeDtypeStruct(shape, dtype) for shape, dtype, _ in outs),
        in_specs=[pallas.BlockSpec(memory_space=pltpu.VMEM)] * len(args),
        out_specs=tuple(pallas.BlockSpec(memory_space=memory) for _, _, memory in outs),
        scratch_shapes=scratch,
        cost_estimate=SMALL,
        compiler_params=pltpu.CompilerParams(
            collective_id=collective_id,
            has_side_effects=True,
            vmem_limit_bytes=48 * 2**20,
        ),
    )(*args)


HALF = HD // 2
STACK = 4


def turn_tables(cosine, sine):
    return jnp.concatenate([cosine] * 4, 1), jnp.concatenate([-sine, sine] * 2, 1)


def turned(values, cosine, sine):
    lane = lax.broadcasted_iota(jnp.int32, values.shape, 1) % HD
    other = jnp.where(
        lane < HALF, pltpu.roll(values, 2 * HD - HALF, 1), pltpu.roll(values, HALF, 1)
    )
    return values * cosine + other * sine


def heads_loop(loops, step):
    def one(t, carry):
        step(t)
        return carry

    lax.fori_loop(0, loops, one, 0)


def split_kv(kv, k_held, v_held):
    width = KVH * HD
    for g in range(KVH):
        k_held[g] = kv[:, g * HD : (g + 1) * HD]
        v_held[g] = kv[:, width + g * HD : width + (g + 1) * HD]


def allowed_keys(places, keys):
    places = jnp.concatenate([places] * STACK, 0)
    return lax.broadcasted_iota(jnp.int32, (places.shape[0], keys), 1) <= places


def dot_nt(left, right):
    return lax.dot_general(
        left, right, (((1,), (1,)), ((), ())), preferred_element_type=jnp.float32
    )


def attend_body(
    his, raw, cosine, sine, places, kv, own, turned_out, out_low, held_out, logs, line_out, k_held, v_held, *sems
):
    picks, keys = raw.shape[0], kv.shape[0]
    core = Core(his)
    core.meet("c", "line")
    started = direct_start(core, own, line_out, sems)
    split_kv(kv, k_held, v_held)
    for j in range(D // (2 * HD)):
        pair = turned(raw[:, 2 * HD * j : 2 * HD * (j + 1)], cosine[...], sine[...]).astype(low)
        for i in range(2):
            t, at = divmod(2 * j + i, STACK)
            turned_out[t, at * picks : (at + 1) * picks, :] = pair[:, i * HD : (i + 1) * HD]
    allowed = allowed_keys(places[...], keys)

    def step(t):
        g = t // (HEADS // KVH // STACK)
        scores = dot_nt(turned_out[t], k_held[g]) * HD ** (-0.5)
        scores = jnp.where(allowed, scores, -1e30)
        high = jnp.max(scores, 1, keepdims=True)
        weights = jnp.exp(scores - high)
        total = jnp.sum(weights, 1, keepdims=True)
        result = jnp.dot(weights.astype(low), v_held[g], preferred_element_type=full)
        held_out[t] = result / total
        logs[t] = jnp.broadcast_to(high + jnp.log(total), (STACK * picks, 2 * HD))

    heads_loop(HEADS // STACK, step)
    for j in range(D // (2 * HD)):
        pair = []
        for i in range(2):
            t, at = divmod(2 * j + i, STACK)
            pair.append(held_out[t, at * picks : (at + 1) * picks, :])
        pair = jnp.concatenate(pair, 1)
        out_low[:, 2 * HD * j : 2 * HD * (j + 1)] = pair.astype(low)
    direct_end(core, started, line_out, sems)


def attend_rows(his, raw, tables, places, kv, own):
    picks, keys = raw.shape[0], kv.shape[0]
    stacks, rows = HEADS // STACK, STACK * picks
    return pallas.pallas_call(
        functools.partial(attend_body, his),
        out_shape=(
            jax.ShapeDtypeStruct((stacks, rows, HD), low),
            jax.ShapeDtypeStruct((picks, D), low),
            jax.ShapeDtypeStruct((stacks, rows, HD), full),
            jax.ShapeDtypeStruct((stacks, rows, 2 * HD), full),
            jax.ShapeDtypeStruct((2, his, *own.shape), low),
        ),
        in_specs=[pallas.BlockSpec(memory_space=pltpu.VMEM)] * 6,
        out_specs=(pallas.BlockSpec(memory_space=pltpu.VMEM),) * 4
        + (pallas.BlockSpec(memory_space=pallas.ANY),),
        scratch_shapes=[pltpu.VMEM((KVH, keys, HD), low)] * 2 + direct_scratch(his),
        compiler_params=pltpu.CompilerParams(
            collective_id=9, has_side_effects=True, vmem_limit_bytes=56 * 2**20
        ),
        cost_estimate=SMALL,
        name="attend",
    )(raw, *tables, places[:, None], kv, own)


def attend_back_body(
    his, grad, cosine, sine, places, kv, queries, held_out, logs, own, raw, kv_grad, line_out, k_held, v_held,
    grad_held, query_held, *rest
):
    picks, keys = grad.shape[0], kv.shape[0]
    sems, sums = rest[:5], rest[5:]
    core = Core(his)
    core.meet("c", "line")
    started = direct_start(core, own, line_out, sems)
    scale = HD ** (-0.5)
    split_kv(kv, k_held, v_held)
    for j in range(D // (2 * HD)):
        pair = grad[:, 2 * HD * j : 2 * HD * (j + 1)]
        for i in range(2):
            t, at = divmod(2 * j + i, STACK)
            grad_held[t, at * picks : (at + 1) * picks, :] = pair[:, i * HD : (i + 1) * HD]
    allowed = allowed_keys(places[...], keys)
    total = sums[0] if sums else kv_grad
    total[...] = jnp.zeros(total.shape, full)

    def step(t):
        g = t // (HEADS // KVH // STACK)
        query, up = queries[t], grad_held[t]
        delta = jnp.sum(up.astype(full) * held_out[t], 1, keepdims=True)
        scores = dot_nt(query, k_held[g]) * scale
        weights = jnp.where(allowed, jnp.exp(scores - logs[t][:, :1]), 0.0)
        weight_grad = dot_nt(up, v_held[g])
        score_grad = (weights * (weight_grad - delta)).astype(low)
        query_held[t] = jnp.dot(score_grad, k_held[g], preferred_element_type=full) * scale
        total[g] += matmul_tn(query, score_grad) * scale
        total[KVH + g] += matmul_tn(up, weights.astype(low))

    heads_loop(HEADS // STACK, step)
    for j in range(D // (2 * HD)):
        pair = []
        for i in range(2):
            t, at = divmod(2 * j + i, STACK)
            pair.append(query_held[t, at * picks : (at + 1) * picks, :])
        pair = jnp.concatenate(pair, 1)
        raw[:, 2 * HD * j : 2 * HD * (j + 1)] = turned(pair, cosine[...], -sine[...]).astype(low)
    if sums:
        for g in range(0, 2 * KVH, 2):
            both = jnp.concatenate([total[g], total[g + 1]], 0)
            kv_grad[:, g * HD : (g + 2) * HD] = both.T
    direct_end(core, started, line_out, sems)


def attend_rows_back(his, grad, tables, places, kv, queries, held_out, logs, own):
    picks, keys = grad.shape[0], kv.shape[0]
    stacks, rows = HEADS // STACK, STACK * picks
    outside = keys > 4096
    by_head = (2 * KVH, HD, keys)
    raw, kv_grad, line_out = pallas.pallas_call(
        functools.partial(attend_back_body, his),
        out_shape=(
            jax.ShapeDtypeStruct((picks, D), low),
            jax.ShapeDtypeStruct(by_head if outside else (keys, 2 * KVH * HD), full),
            jax.ShapeDtypeStruct((2, his, *own.shape), low),
        ),
        in_specs=[pallas.BlockSpec(memory_space=pltpu.VMEM)] * 9,
        out_specs=(pallas.BlockSpec(memory_space=pltpu.VMEM),) * 2
        + (pallas.BlockSpec(memory_space=pallas.ANY),),
        scratch_shapes=[
            pltpu.VMEM((KVH, keys, HD), low),
            pltpu.VMEM((KVH, keys, HD), low),
            pltpu.VMEM((stacks, rows, HD), low),
            pltpu.VMEM((stacks, rows, HD), full),
            *direct_scratch(his),
        ]
        + ([] if outside else [pltpu.VMEM(by_head, full)]),
        compiler_params=pltpu.CompilerParams(
            collective_id=10, has_side_effects=True, vmem_limit_bytes=58 * 2**20
        ),
        cost_estimate=SMALL,
        name="attend_back",
    )(grad, *tables, places[:, None], kv, queries, held_out, logs, own)
    kv_grad = kv_grad.reshape(2 * KVH * HD, keys).T if outside else kv_grad
    return raw, kv_grad, line_out


def rows_body(his, far, near, start, got, looked, local_sem, y_sems, y_sems_in, seq_sems, seq_sems_in):
    core = Core(his)
    dp, s = lax.axis_index("dp"), lax.axis_index("seq")
    seqs = 2 * his
    core.ids["y"] = (dp + 2 - 4 * (dp // 2), s)
    for i in range(1, seqs):
        core.ids[f"seq{i}"] = (dp, lax.rem(s + i, seqs))
    core.meet("y", *(f"seq{i}" for i in range(1, seqs)))
    over, spread = [], []
    for i in range(seqs):
        to = lax.rem(s + i, seqs)
        over.append(core.copy(far.at[to], got.at[to], (y_sems, y_sems_in), i, "y"))
        over[i].start()
    here = None
    for i in [*range(1, seqs), 0]:
        to = lax.rem(s + i, seqs)
        over[i].wait_recv()

        def add(at, to=to):
            looked[to, at, :] = near[to, at, :] + got[to, at, :]

        by_rows(near.shape[1], add)
        if i:
            spread.append(
                core.copy(looked.at[to], start.at[s], (seq_sems, seq_sems_in), i - 1, f"seq{i}")
            )
            spread[-1].start()
        else:
            here = pltpu.make_async_copy(looked.at[s], start.at[s], local_sem)
            here.start()
    for copy in spread:
        copy.wait_recv()
    here.wait()
    sent(over + spread)


def gather_rows(his, far, near):
    seqs = 2 * his
    rows, columns = far.shape[0] // seqs, far.shape[1]
    far, near = (part.reshape(seqs, rows, columns) for part in (far, near))
    dma = pltpu.SemaphoreType.DMA
    start = pallas.pallas_call(
        functools.partial(rows_body, his),
        out_shape=jax.ShapeDtypeStruct((seqs, rows, columns), low),
        in_specs=[pallas.BlockSpec(memory_space=pltpu.VMEM)] * 2,
        out_specs=pallas.BlockSpec(memory_space=pallas.ANY),
        scratch_shapes=[
            pltpu.VMEM((seqs, rows, columns), low),
            pltpu.VMEM((seqs, rows, columns), low),
            dma,
            *[dma((count,)) for count in (seqs, seqs, seqs - 1, seqs - 1)],
        ],
        cost_estimate=SMALL,
        compiler_params=pltpu.CompilerParams(
            collective_id=11, has_side_effects=True, vmem_limit_bytes=32 * 2**20
        ),
        name="gather_rows",
    )(far, near)
    return jnp.transpose(start, (1, 0, 2)).reshape(rows, seqs * columns).astype(full)


def sum_body(his, rows, packed, out, bufs, got, send_sems, recv_sems):
    core = Core(his)
    dp, s = lax.axis_index("dp"), lax.axis_index("seq")
    ways = [("lo", 0)]
    bit = 1
    while bit < his:
        up = lax.rem(core.hi // bit, 2)
        core.ids[f"hi{bit}"] = (dp, s + 2 * bit * (1 - 2 * up))
        ways.append((f"hi{bit}", 0))
        bit *= 2
    y = dp // 2
    core.ids["y"] = (dp + 2 * (1 - 2 * y), s)
    ways += [("c", 1), ("y", 1)]
    core.meet(*(name for name, _ in ways))
    bufs[0] = packed[...]
    copies = []
    for j, (name, over_dp) in enumerate(ways):
        first = rows[0] if over_dp else 0
        last = rows[0] + rows[1] + (rows[2] if over_dp else 0)
        copy = core.copy(
            bufs.at[j, first:last], got.at[j, first:last], (send_sems, recv_sems), j, name
        )
        copy.start()
        copies.append(copy)
        copy.wait_recv()
        bufs[j + 1] = bufs[j]
        bufs[j + 1, first:last] = bufs[j, first:last] + got[j, first:last]
    out[...] = bufs[len(ways)]
    sent(copies)


def padded(parts):
    return [
        jnp.pad(part, (0, -part.shape[0] % 1024)).reshape(-1, 128) for part in parts
    ]


def sum_statistics(his, over_seq, over_all, over_dp):
    groups = [padded(parts) for parts in (over_seq, over_all, over_dp)]
    rows = tuple(sum(part.shape[0] for part in group) for group in groups)
    steps = 3 + his.bit_length() - 1
    total = sum(rows)
    dma = pltpu.SemaphoreType.DMA
    out = pallas.pallas_call(
        functools.partial(sum_body, his, rows),
        out_shape=jax.ShapeDtypeStruct((total, 128), full),
        in_specs=[pallas.BlockSpec(memory_space=pltpu.VMEM)],
        out_specs=pallas.BlockSpec(memory_space=pltpu.VMEM),
        scratch_shapes=[
            pltpu.VMEM((steps + 1, total, 128), full),
            pltpu.VMEM((steps, total, 128), full),
            dma((steps,)),
            dma((steps,)),
        ],
        compiler_params=pltpu.CompilerParams(
            collective_id=6, has_side_effects=True, vmem_limit_bytes=32 * 2**20
        ),
        name="sum_statistics",
    )(jnp.concatenate([part for group in groups for part in group], 0))
    results, at = [], 0
    for parts, group in zip((over_seq, over_all, over_dp), groups):
        for part, block in zip(parts, group):
            results.append(out[at : at + block.shape[0]].reshape(-1)[: part.shape[0]])
            at += block.shape[0]
    return results


def on_device(
    tok_ids,
    targets,
    positions,
    answer_mask,
    emb,
    head,
    attn_w,
    mlp_w,
    gains,
    emb_row,
    emb_col,
    head_row,
    head_col,
    attn_row,
    attn_col,
    mlp_row,
    mlp_col,
    gains_moment,
):
    pl = Place()
    seqs, his = pl.seqs, pl.his
    tokens = tok_ids.shape[1] // seqs
    picks = targets.shape[1] // seqs
    group = HEADS // KVH
    kv_width = KVH * HD
    block = D // (pl.dps * seqs)
    emb_n, emb_m = emb.shape
    line = 2 * his
    part = FF // line
    wide = 3 * part

    def swap_rows(rows, **way):
        return pl.send(rows.astype(low), **way)

    mlp_here, mlp_came = line_pairs(pl, split_columns(mlp_w, line))
    ids = jnp.concatenate([tok_ids.reshape(seqs, tokens), targets.reshape(seqs, picks)], 1)
    ids = ids.reshape(seqs * (tokens + picks))
    def look(wanted, *work):
        at = after(wanted, *work) - pl.dp * emb_n
        rows = jnp.take(emb, jnp.clip(at, 0, emb_n - 1), axis=0, mode="clip")
        return jnp.where(((at >= 0) & (at < emb_n))[:, None], rows, 0.0).astype(low)

    ids_y = pl.send(ids, dy=1)
    ids_c, ids_yc = pl.send(ids, dc=1), pl.send(ids, dy=1, dc=1)
    near_own = look(ids)
    ids_c, ids_y, ids_yc = after((ids_c, ids_y, ids_yc), near_own)
    mlp_came = after(mlp_came, near_own)
    far_other = look(ids_yc, mlp_came)
    mlp_got = line_sends(pl, mlp_here, mlp_came)
    far_got = pl.send(far_other, dc=1)
    near_other = look(ids_c, far_other)
    near_got = pl.send(near_other, dc=1)
    far_own = look(ids_y, near_other)
    far_sum = far_own + after(far_got, far_own)
    near_sum = near_own + after(near_got, far_own)

    attn_block = jnp.concatenate([attn_w, jnp.pad(gains.T, ((0, 0), (0, 125)))], 1).astype(low)
    attn_full = lax.all_gather(attn_block, ("dp", "seq"), axis=0, tiled=True)
    query_full, out_full = attn_full[:, :D], attn_full[:, QKV : QKV + D]
    kv_full = attn_full[:, D:QKV]
    gain_float = attn_full[:, QKV + D : QKV + D + 3].astype(full).T
    start = gather_rows(his, far_sum, near_sum)
    mlp_line = line_place(pl, after(mlp_got, start)).reshape(2, his, block, wide)
    mlp_x, mlp_y = pl.send(mlp_line, dlo=1), pl.send(mlp_line, dy=1)
    emb_square_sum, *other_squares = (
        jnp.sum(after(w, mlp_line) ** 2) for w in (emb, attn_w, mlp_w, head)
    )
    start = after(start, mlp_line, emb_square_sum, other_squares)
    head_low = after(head, start).astype(low)

    token_pos = pl.s * tokens + jnp.arange(tokens, dtype=jnp.int32)
    pick_pos = lax.dynamic_slice_in_dim(positions[0], pl.s * picks, picks)
    token_tables = turn_tables(*yarn_tables(token_pos.astype(full)))
    pick_tables = turn_tables(*yarn_tables(pick_pos.astype(full)))
    normed = rms_norm(start, gain_float[0]).astype(low)
    normed_tok, normed_pick = normed[:tokens], normed[tokens:]
    start_pick = start[tokens:]
    projected = matmul(normed_tok, kv_full)
    (kv_all,) = move(
        functools.partial(keys_body, his),
        0,
        [((his, 2, tokens, 2 * kv_width), low, pallas.ANY)],
        [projected, *token_tables],
        his,
        own=(tokens, 2 * kv_width),
        gathers=1,
    )
    kv_all = kv_all.reshape(seqs * tokens, 2 * kv_width)
    kv_all, mlp_x, mlp_y = lax.optimization_barrier((kv_all, mlp_x, mlp_y))
    raw = matmul(after(normed_pick, kv_all), query_full)
    mlp_far = (pl.send(mlp_x[0], dy=1), pl.send(mlp_y[1], dlo=1))
    head_rows = lax.all_gather(after(head_low, kv_all), "dp", axis=1, tiled=True)
    queries, attended_low, attended, log_total, pick_line = attend_rows(
        his, raw, pick_tables, pick_pos, kv_all, normed_pick
    )
    def shares(rows):
        return jnp.transpose(rows.reshape(picks, line, D // line), (1, 0, 2))

    middle = start_pick + matmul_nt(attended_low, out_full)
    normed_two, attended_share = move(
        functools.partial(norm_gather_body, his),
        1,
        [
            ((his, 2, picks, D), low, pallas.ANY),
            ((line, picks, D // line), low, pltpu.VMEM),
        ],
        [middle, gain_float[1:2], shares(attended_low)],
        his,
        own=(picks, D),
        gathers=1,
        swap=(his, picks, D // line),
    )
    normed_two = normed_two.reshape(line * picks, D)
    mlp_far = after(mlp_far, normed_two)
    mlp_full = assemble(mlp_line, mlp_x, mlp_y, *mlp_far).reshape(D, wide)
    gate_up = matmul(normed_two, mlp_full[:, : 2 * part])
    gate = gate_up[:, :part]
    upward = gate_up[:, part:]
    mixed = (jax.nn.silu(gate) * upward).astype(low)
    down = matmul_nt(mixed, mlp_full[:, 2 * part :])
    ending, chosen = move(
        functools.partial(ending_body, his),
        2,
        [((picks, D), full, pltpu.VMEM), ((his, 2, picks, D), low, pallas.ANY)],
        [down.reshape(his, 2, picks, D), middle, gain_float[2:3]],
        his,
        scatter=(picks, D),
        own=(picks, D),
        gathers=1,
    )
    chosen = chosen.reshape(seqs * picks, D)
    logits = matmul_nt(chosen, head_rows)
    vocab_part = head_rows.shape[0]
    target_hit = (
        targets[0][:, None]
        == pl.s * vocab_part + jnp.arange(vocab_part, dtype=jnp.int32)[None, :]
    )
    part_high = jnp.max(logits, 1)
    part_sum = jnp.sum(jnp.exp(logits - part_high[:, None]), 1)
    part_target = jnp.sum(jnp.where(target_hit, logits, 0.0), 1)
    stats = jnp.stack([part_high, part_sum, part_target])
    for step in pl.ways(("dlo", "hi")):
        other = step(stats)
        larger = jnp.maximum(stats[0], other[0])
        summed = stats[1] * jnp.exp(stats[0] - larger) + other[1] * jnp.exp(other[0] - larger)
        stats = jnp.stack([larger, summed, stats[2] + other[2]])
    all_high, all_sum_exp, target_logit = stats
    row_total = all_high + jnp.log(all_sum_exp)
    mask_float = answer_mask.astype(full)
    count = jnp.sum(mask_float)
    own_mask = lax.dynamic_slice_in_dim(mask_float, pl.dp, 1, 0)[0]
    loss_part = jnp.where(
        pl.s == 0,
        jnp.sum(own_mask * (row_total - target_logit + zloss_weight * row_total * row_total)),
        0.0,
    )
    probs = jnp.exp(logits - row_total[:, None])
    logit_grad = (
        (own_mask / count)[:, None]
        * (probs * (1.0 + 2.0 * zloss_weight * row_total)[:, None] - target_hit.astype(full))
    ).astype(low)
    chosen_part = matmul(logit_grad, head_rows)
    ending_grad, final_gain_grad, branch_grad = move(
        functools.partial(ending_back_body, his),
        3,
        [
            ((picks, D), full, pltpu.VMEM),
            ((1, D), full, pltpu.VMEM),
            ((his, 2, picks, D), low, pallas.ANY),
        ],
        [chosen_part.reshape(his, 2, picks, D), ending, gain_float[2:3]],
        his,
        scatter=(picks, D),
        own=(picks, D),
        gathers=1,
    )
    branch_grad = branch_grad.reshape(line * picks, D)
    mixed_grad = matmul(branch_grad, mlp_full[:, 2 * part :])
    sigmoid_gate = jax.nn.sigmoid(gate)
    gate_grad = mixed_grad * upward * sigmoid_gate * (1.0 + gate * (1.0 - sigmoid_gate))
    upward_grad = mixed_grad * gate * sigmoid_gate
    gate_up_grad = jnp.concatenate([gate_grad, upward_grad], 1).astype(low)
    middle_up = matmul_nt(gate_up_grad, mlp_full[:, : 2 * part])
    down_grad = matmul_tn(after(branch_grad, middle_up), mixed)
    mlp_term = jnp.concatenate([matmul_tn(normed_two, gate_up_grad), down_grad], 1)
    mlp_term = mlp_term.astype(low).reshape(2, 2, his, 2, block, wide)
    mlp_state = cross_start(pl, mlp_term)
    head_rows_grad = matmul_tn(after(logit_grad, mlp_term), chosen).astype(low)
    head_grad = lax.psum_scatter(head_rows_grad, "dp", scatter_dimension=1, tiled=True)
    middle_up = after(middle_up, mlp_term, head_rows_grad)
    middle_grad, attn_branch_grad, middle_gain_grad = move(
        functools.partial(middle_back_body, his),
        4,
        [
            ((picks, D), full, pltpu.VMEM),
            ((picks, D), low, pltpu.VMEM),
            ((1, D), full, pltpu.VMEM),
        ],
        [middle_up.reshape(his, 2, picks, D), middle, gain_float[1:2], ending_grad],
        his,
        scatter=(picks, D),
    )
    attended_grad = matmul(attn_branch_grad, out_full).astype(low)
    query_raw, kv_part, branch_line = attend_rows_back(
        his,
        attended_grad,
        pick_tables,
        pick_pos,
        kv_all,
        queries,
        attended,
        log_total,
        attn_branch_grad,
    )
    mlp_keep, mlp_sends = cross_next(pl, mlp_state, kv_part)
    kv_part = after(kv_part, mlp_keep, mlp_sends)
    kv_raw, query_share = move(
        functools.partial(keys_back_body, his),
        5,
        [
            ((tokens, 2 * kv_width), low, pltpu.VMEM),
            ((line, picks, D // line), low, pltpu.VMEM),
        ],
        [
            kv_part.reshape(his, 2, tokens, 2 * kv_width),
            *token_tables,
            shares(query_raw),
        ],
        his,
        swap=(his, picks, D // line),
        scatter=(tokens, 2 * kv_width),
        own=(tokens, 2 * kv_width),
        own_type=full,
    )
    mlp_state = cross_send(pl, mlp_keep, after(mlp_sends, kv_raw))
    pick_up = matmul_nt(query_raw, query_full)
    tok_up = matmul_nt(kv_raw, kv_full)
    start_part, start_gain_grad = norm_back(
        start, gain_float[0], jnp.concatenate([tok_up, pick_up], 0)
    )
    start_grad = jnp.concatenate(
        [start_part[:tokens], start_part[tokens:] + middle_grad], 0
    ).astype(low)

    back_rows = lax.all_to_all(start_grad, "seq", split_axis=1, concat_axis=0, tiled=True)
    branch_line, pick_line = after((branch_line, pick_line), start_grad)
    branch_line, pick_line = (
        part.reshape(line * picks, D) for part in (branch_line, pick_line)
    )
    query_term = jnp.concatenate(
        [
            matmul_tn(pick_line, query_share.reshape(line * picks, D // line)),
            matmul_tn(branch_line, attended_share.reshape(line * picks, D // line)),
        ],
        1,
    )
    query_term = query_term.astype(low).reshape(2, 2, his, 2, block, query_term.shape[-1])
    query_state = cross_start(pl, query_term)
    gains_term = jnp.stack([start_gain_grad, middle_gain_grad[0], final_gain_grad[0]], 1)

    def by_core(rows, core):
        rows = rows.reshape(rows.shape[0], 2, 2, seqs * block)
        return pick(rows, core, 2).reshape(rows.shape[0], D // 2)

    def grid(rows):
        return rows.astype(low).reshape(2, his, 2, block, rows.shape[-1])

    def token_term(core):
        return jnp.concatenate(
            [
                matmul_tn(by_core(after(normed_tok, start_grad), core), kv_raw),
                jnp.pad(by_core(gains_term.T, core).T, ((0, 0), (0, 125))),
            ],
            1,
        )

    token_got = pl.send(token_term(1 - pl.c).astype(low), dc=1)
    token_keep = token_term(pl.c)
    early = [
        loss_part,
        jnp.sum(attn_row),
        *other_squares,
        jnp.where(pl.s == 0, jnp.sum(emb_row), 0.0),
        emb_square_sum,
        jnp.where(pl.dp == 0, jnp.sum(head_row), 0.0),
        jnp.sum(gains * gains),
        jnp.sum(mlp_row),
    ]
    slot = jnp.arange(128, dtype=jnp.int32)
    early = sum(jnp.where(slot == i, value, 0.0) for i, value in enumerate(early))
    back_rows, early = lax.optimization_barrier((back_rows, early))
    back_got = pl.send(back_rows, dy=1)
    mlp_term = cross_end(pl, mlp_state, back_rows)
    mlp_here, mlp_came = line_pairs(pl, mlp_term)
    token_sum = grid(token_keep + after(token_got, back_rows).astype(full))
    token_got = pl.send(pick(token_sum, 1 - pl.y, 0), dy=1)

    def on_chip(wanted):
        local, other = wanted - pl.dp * emb_n, wanted - (pl.dp ^ 1) * emb_n
        return jnp.where(
            (local >= 0) & (local < emb_n),
            local,
            jnp.where((other >= 0) & (other < emb_n), other + emb_n, 2 * emb_n),
        )

    places_in = on_chip(ids), on_chip(ids_y)
    chip_grad = (
        jnp.zeros((2 * emb_n + 8, emb_m), full)
        .at[places_in[0]]
        .add(after(back_rows, token_sum, mlp_came, query_term).astype(full))
    )
    mlp_got = line_sends(pl, mlp_here, after(mlp_came, token_sum))
    near, far = mlp_got[1:2] + mlp_got[-1:], mlp_got[2:-1]
    query_state = cross_send(pl, *cross_next(pl, query_state, chip_grad))
    head_grad = after(head_grad, query_state[:2]).astype(full)
    head_square = head_grad * head_grad + eps_square
    head_rows_sum = jnp.sum(head_square, 1)
    head_cols_sum = jnp.sum(head_square, 0)
    back_got = after(back_got, near[0], head_rows_sum, head_cols_sum)
    chip_grad = chip_grad.at[places_in[1]].add(back_got.astype(full))
    token_sum = pick(token_sum, pl.y, 0).astype(full) + after(token_got, chip_grad).astype(full)
    token_got = pl.send(pick(token_sum, 1 - pl.lo, 1).astype(low), dlo=1)
    emb_part = after(chip_grad, near[1:], far, token_sum)[emb_n : 2 * emb_n].astype(low)
    emb_got = pl.send(emb_part, dc=1)
    query_term = cross_end(pl, query_state, emb_part)
    token_sum = pick(token_sum, pl.lo, 1) + after(token_got, emb_part).astype(full)
    mlp_grad, mlp_rows, mlp_cols = join_columns(line_place(pl, after(mlp_got, query_term)))
    mlp_row_new = decay_rate * mlp_row + (1.0 - decay_rate) * mlp_rows / (3 * FF)
    emb_grad = chip_grad[:emb_n] + after(emb_got, query_term, token_sum).astype(full)
    emb_square = emb_grad * emb_grad + eps_square
    emb_rows, emb_cols = jnp.sum(emb_square, 1), jnp.sum(emb_square, 0)
    attn_grad, gains_grad, attn_rows, attn_cols = layer_gradient(
        his, after(query_term, emb_rows), token_sum
    )
    gains_grad = gains_grad[:, :3].T
    attn_row_new = decay_rate * attn_row + (1.0 - decay_rate) * attn_rows[:, 0] / (QKV + D)
    scalars = early
    for at, value in ((10, emb_cols), (11, head_cols_sum)):
        scalars = scalars + jnp.where(slot == at, jnp.sum(value), 0.0)
    (
        emb_row_sum,
        head_col_sum,
        attn_cols_sum,
        mlp_cols_sum,
        totals,
        head_row_sum,
        emb_col_sum,
    ) = sum_statistics(
        his,
        (emb_rows, head_cols_sum),
        (attn_cols[0], mlp_cols, scalars),
        (head_rows_sum, emb_cols),
    )
    attn_row_total = decay_rate * totals[1] + (1.0 - decay_rate) * jnp.sum(attn_cols_sum) / (QKV + D)
    mlp_row_total = decay_rate * totals[9] + (1.0 - decay_rate) * jnp.sum(mlp_cols_sum) / (3 * FF)
    emb_row_total, head_row_total = totals[10], totals[11]

    attn_col_new = decay_rate * attn_col + (1.0 - decay_rate) * attn_cols_sum / D
    mlp_col_new = decay_rate * mlp_col + (1.0 - decay_rate) * mlp_cols_sum / D
    attn_update = attn_grad * lax.rsqrt(
        attn_row_new[:, None] * attn_col_new[None, :] / (attn_row_total / D)
    )
    mlp_update = mlp_grad * lax.rsqrt(
        mlp_row_new[:, None] * mlp_col_new[None, :] / (mlp_row_total / D)
    )
    emb_row_new = decay_rate * emb_row + (1.0 - decay_rate) * emb_row_sum / D
    emb_col_new = decay_rate * emb_col + (1.0 - decay_rate) * emb_col_sum / VOCAB
    emb_mean = (decay_rate * totals[5] + (1.0 - decay_rate) * emb_row_total / D) / VOCAB
    emb_update = emb_grad * lax.rsqrt(emb_row_new[:, None] * emb_col_new[None, :] / emb_mean)
    head_row_new = decay_rate * head_row + (1.0 - decay_rate) * head_row_sum / D
    head_col_new = decay_rate * head_col + (1.0 - decay_rate) * head_col_sum / VOCAB
    head_mean = (decay_rate * totals[7] + (1.0 - decay_rate) * head_row_total / D) / VOCAB
    head_update = head_grad * lax.rsqrt(head_row_new[:, None] * head_col_new[None, :] / head_mean)
    moment_new = decay_rate * gains_moment + (1.0 - decay_rate) * (
        gains_grad * gains_grad + eps_square
    )
    gains_update = gains_grad * lax.rsqrt(moment_new)
    attn_new = finish(attn_w, attn_update, totals[2], D * (QKV + D))
    mlp_new = finish(mlp_w, mlp_update, totals[3], D * 3 * FF)
    emb_new = finish(emb, emb_update, totals[6], VOCAB * D)
    head_new = finish(head, head_update, totals[4], VOCAB * D)
    gains_new = finish(gains, gains_update, totals[8], 3 * D)
    return (
        totals[0],
        count,
        emb_grad,
        emb_new,
        emb_row_new,
        emb_col_new,
        head_grad,
        head_new,
        head_row_new,
        head_col_new,
        attn_grad,
        attn_new,
        attn_row_new,
        attn_col_new,
        mlp_grad,
        mlp_new,
        mlp_row_new,
        mlp_col_new,
        gains_grad,
        moment_new,
        gains_new,
    )


def solution(mesh):
    return jax.shard_map(
        on_device,
        mesh=mesh,
        in_specs=(
            P("dp", None),
            P("dp", None),
            P("dp", None),
            P(),
            P("dp", "seq"),
            P("seq", "dp"),
            P(("dp", "seq"), None),
            P(("dp", "seq"), None),
            P(None, ("dp", "seq")),
            P("dp"),
            P("seq"),
            P("seq"),
            P("dp"),
            P(("dp", "seq")),
            P(),
            P(("dp", "seq")),
            P(),
            P(None, ("dp", "seq")),
        ),
        out_specs=(
            P(),
            P(),
            P("dp", "seq"),
            P("dp", "seq"),
            P("dp"),
            P("seq"),
            P("seq", "dp"),
            P("seq", "dp"),
            P("seq"),
            P("dp"),
            P(("dp", "seq"), None),
            P(("dp", "seq"), None),
            P(("dp", "seq")),
            P(),
            P(("dp", "seq"), None),
            P(("dp", "seq"), None),
            P(("dp", "seq")),
            P(),
            P(None, ("dp", "seq")),
            P(None, ("dp", "seq")),
            P(None, ("dp", "seq")),
        ),
        check_vma=False,
    )
```
